32 devices in a mesh: gx: 8 (over y, x, core), sa: 4 (over z).
Axes of the slice: x: 2, y: 2, z: 4, core: 2. Of those that a mesh axis runs over, the one named last changes fastest.
Arguments:
- field_in: bfloat16 [4, 8, 256, 1024], P('sa', 'gx'), may hold values from -6 to 6
- cotangent: bfloat16 [4, 8, 256, 1024], P('sa', 'gx'), may hold values from -6 to 6
- mode_weights: bfloat16 [32, 512, 64, 128], P(None, 'gx'), may hold values from -1 to 1
- point_weights: bfloat16 [64, 64], replicated, may hold values from -0.75 to 0.75
Outputs:
- field_out: bfloat16 [4, 8, 256, 1024], P('sa', 'gx')
- field_grad: bfloat16 [4, 8, 256, 1024], P('sa', 'gx')
- weight_grad: float32 [32, 512, 64, 128], P('sa', 'gx')
The draws below stay inside these ranges and needn't reach their ends.
All inputs are finite; a program needn't handle non-finite values.
Results may differ from the reference program's by a relative error of at most 0.018.
Values may be sent and summed in bfloat16 or wider, within the bound.
A program may use at most 128 MiB of HBM per device.

```python
import math
import jax
import jax.numpy as jnp
from jax import lax

C = 64
KX = 32
KY = 32
KZ = 16
NY = 256
NZ = 16
NX = 8
SAMPLES = 4
MODES = 512


def steps_of(rng, shape, cuts, smallest, high):
    level, own = 1.0, jax.random.fold_in(rng, 6)
    for position, blocks in cuts:
        steps = jnp.exp(jax.random.uniform(jax.random.fold_in(own, position), (blocks,), jnp.float32, smallest / len(cuts), high / len(cuts)))
        level = level * jnp.repeat(steps, shape[position] // blocks).reshape([-1 if axis == position else 1 for axis in range(len(shape))])
    return level


def noise(own_key, shape, deviation, limit, split=(), kind=jnp.bfloat16):
    factor_of = steps_of(own_key, shape, split, -0.22, 0.18) if split else 1.0
    drawn = jax.random.normal(own_key, shape, jnp.float32) * deviation * factor_of
    return jnp.minimum(jnp.maximum(drawn, -limit), limit).astype(kind)


def setup_inputs(seed: int = 0) -> dict:
    keys = jax.random.split(jax.random.key(seed), 5)
    return {
        "field_in": noise(keys[0], (SAMPLES, NX, NY, NZ * C), 1.0, 6.0, ((0, 4), (1, 8))),
        "cotangent": noise(keys[1], (SAMPLES, NX, NY, NZ * C), 1.0, 6.0, ((0, 4), (1, 8))),
        "mode_weights": noise(keys[2], (KX, MODES, C, 2 * C), ((NX * NY * NZ // (KX * KY * KZ)) ** 0.5 * C ** -0.5), 1.0, ((1, 8),)),
        "point_weights": noise(keys[3], (C, C), C ** -0.5, 0.75),
    }


HIGHEST_PREC = lax.Precision.HIGHEST
GELU_COEF = 0.044715

def angles(freq_count, grid_count):
    frequency = jnp.arange(freq_count, dtype=jnp.int32) - freq_count // 2
    places = jnp.arange(grid_count, dtype=jnp.int32)
    turn_index = jnp.mod(frequency[:, None] * places[None, :], grid_count)
    return turn_index.astype(jnp.float32) * (2.0 * math.pi / grid_count)

def gelu_parts(pre_act):
    root_const = math.sqrt(2.0 / math.pi)
    inner_arg = root_const * (pre_act + GELU_COEF * pre_act * pre_act * pre_act)
    tangent = jnp.tanh(inner_arg)
    activated = 0.5 * pre_act * (1.0 + tangent)
    gelu_slope = 0.5 * (1.0 + tangent) + 0.5 * pre_act * (1.0 - tangent * tangent) * root_const * (1.0 + 3.0 * GELU_COEF * pre_act * pre_act)
    return (activated, gelu_slope)

def along_z_forward(data_in, table_z):
    return jnp.einsum('pyzc,kz->pykc', data_in, table_z, precision=HIGHEST_PREC)

def along_z_inverse(data_in, table_z):
    return jnp.einsum('pykc,kz->pyzc', data_in, table_z, precision=HIGHEST_PREC)

def forward_yz(local_field):
    planes = local_field.shape[0]
    theta_y = angles(KY, NY)
    table_y = jnp.concatenate([jnp.cos(theta_y), -jnp.sin(theta_y)], 0).astype(jnp.bfloat16)
    first_pass = jnp.einsum('fy,pyq->pfq', table_y.astype(jnp.float32), local_field.astype(jnp.float32), precision=HIGHEST_PREC)
    first_pass = first_pass.reshape(planes, 2, KY, NZ, C)
    theta_z = angles(KZ, NZ)
    cos_z = jnp.cos(theta_z)
    sin_z = jnp.sin(theta_z)
    real_in = first_pass[:, 0]
    imag_in = first_pass[:, 1]
    real_out = along_z_forward(real_in, cos_z) + along_z_forward(imag_in, sin_z)
    imag_out = along_z_forward(imag_in, cos_z) - along_z_forward(real_in, sin_z)
    mode_data = jnp.concatenate([real_out, imag_out], -1)
    return mode_data.reshape(planes, KY * KZ, 2 * C).astype(jnp.bfloat16)

def forward_x(mode_data, norm_scale):
    x_length, mode_block, pair_width = mode_data.shape
    channels = pair_width // 2
    theta_x = angles(KX, x_length)
    flat_data = mode_data.reshape(x_length, mode_block * pair_width)
    cos_part = jnp.dot(jnp.cos(theta_x).astype(jnp.bfloat16), flat_data, preferred_element_type=jnp.float32).reshape(KX, mode_block, pair_width)
    sin_part = jnp.dot(jnp.sin(theta_x).astype(jnp.bfloat16), flat_data, preferred_element_type=jnp.float32).reshape(KX, mode_block, pair_width)
    real_out = cos_part[..., :channels] + sin_part[..., channels:]
    imag_out = cos_part[..., channels:] - sin_part[..., :channels]
    return (jnp.concatenate([real_out, imag_out], -1) * norm_scale).astype(jnp.bfloat16)

def inverse_x(mixed_modes, x_length):
    kx_count, mode_block, pair_width = mixed_modes.shape
    channels = pair_width // 2
    theta_x = angles(kx_count, x_length).T
    flat_data = mixed_modes.reshape(kx_count, mode_block * pair_width)
    cos_part = jnp.dot(jnp.cos(theta_x).astype(jnp.bfloat16), flat_data, preferred_element_type=jnp.float32).reshape(x_length, mode_block, pair_width)
    sin_part = jnp.dot(jnp.sin(theta_x).astype(jnp.bfloat16), flat_data, preferred_element_type=jnp.float32).reshape(x_length, mode_block, pair_width)
    real_out = cos_part[..., :channels] - sin_part[..., channels:]
    imag_out = cos_part[..., channels:] + sin_part[..., :channels]
    return jnp.concatenate([real_out, imag_out], -1).astype(jnp.bfloat16)

def inverse_yz(planes_data, y_count, z_count, norm_scale):
    planes, mode_total, pair_width = planes_data.shape
    channels = pair_width // 2
    wide_data = planes_data.astype(jnp.float32).reshape(planes, KY, KZ, pair_width)
    real_in = wide_data[..., :channels]
    imag_in = wide_data[..., channels:]
    theta_z = angles(KZ, z_count)
    cos_z = jnp.cos(theta_z)
    sin_z = jnp.sin(theta_z)
    real_mid = along_z_inverse(real_in, cos_z) - along_z_inverse(imag_in, sin_z)
    imag_mid = along_z_inverse(imag_in, cos_z) + along_z_inverse(real_in, sin_z)
    stacked = jnp.concatenate([real_mid, imag_mid], 1).reshape(planes, 2 * KY, z_count * channels)
    theta_y = angles(KY, y_count)
    table_y = jnp.concatenate([jnp.cos(theta_y), -jnp.sin(theta_y)], 0)
    return jnp.einsum('pfq,fy->pyq', stacked, table_y, precision=HIGHEST_PREC) * norm_scale

def mix_forward(coeffs, weights_wide):
    channels = weights_wide.shape[2]
    wide_coeffs = coeffs.astype(jnp.float32)
    real_part = jnp.einsum('kmc,kmcp->kmp', wide_coeffs[..., :channels], weights_wide, precision=HIGHEST_PREC)
    imag_part = jnp.einsum('kmc,kmcp->kmp', wide_coeffs[..., channels:], weights_wide, precision=HIGHEST_PREC)
    out_real = real_part[..., :channels] - imag_part[..., channels:]
    out_imag = real_part[..., channels:] + imag_part[..., :channels]
    return jnp.concatenate([out_real, out_imag], -1).astype(jnp.bfloat16)

def mix_backward(coeffs, weights_wide):
    channels = weights_wide.shape[2]
    wide_coeffs = coeffs.astype(jnp.float32)
    swapped = jnp.concatenate([wide_coeffs[..., channels:], -wide_coeffs[..., :channels]], -1)
    first_half = jnp.einsum('kmp,kmcp->kmc', wide_coeffs, weights_wide, precision=HIGHEST_PREC)
    second_half = jnp.einsum('kmp,kmcp->kmc', swapped, weights_wide, precision=HIGHEST_PREC)
    return jnp.concatenate([first_half, second_half], -1).astype(jnp.bfloat16)

def pointwise(local_field, weights_small):
    channels = weights_small.shape[0]
    cells = local_field.reshape(-1, channels)
    return jnp.dot(cells, weights_small, preferred_element_type=jnp.float32).reshape(local_field.shape)

def sample_sum(left_side, right_side):
    channels = left_side.shape[-1] // 2
    left_wide = left_side.astype(jnp.float32)
    right_wide = right_side.astype(jnp.float32)
    left_real = left_wide[..., :channels]
    left_imag = left_wide[..., channels:]
    right_real = right_wide[..., :channels]
    right_imag = right_wide[..., channels:]

    def outer_sum(left_op, right_op):
        return jnp.einsum('skmc,skmo->kmco', left_op, right_op, precision=HIGHEST_PREC)
    real_sum = outer_sum(left_real, right_real) + outer_sum(left_imag, right_imag)
    imag_sum = outer_sum(left_real, right_imag) - outer_sum(left_imag, right_real)
    return jnp.concatenate([real_sum, imag_sum], -1)

def reference(field_in, cotangent, mode_weights, point_weights):
    weights_wide = mode_weights.astype(jnp.float32)
    norm_scale = 1.0 / math.sqrt(NX * NY * NZ)

    def one_sample(pair_in):
        local_field, local_cot = pair_in
        coeffs_in = forward_x(forward_yz(local_field), norm_scale)
        spec_out = inverse_yz(inverse_x(mix_forward(coeffs_in, weights_wide), NX), NY, NZ, norm_scale)
        pre_act = spec_out + pointwise(local_field, point_weights)
        activated, gelu_slope = gelu_parts(pre_act)
        out_grad = (local_cot.astype(jnp.float32) * gelu_slope).astype(jnp.bfloat16)
        coeffs_grad = forward_x(forward_yz(out_grad), norm_scale)
        spec_grad = inverse_yz(inverse_x(mix_backward(coeffs_grad, weights_wide), NX), NY, NZ, norm_scale)
        field_grad = (spec_grad + pointwise(out_grad, point_weights.T)).astype(jnp.bfloat16)
        return (activated.astype(jnp.bfloat16), field_grad, coeffs_in, coeffs_grad)
    field_out, field_grad, coeffs_all, grads_all = lax.map(one_sample, (field_in, cotangent))

    def grad_row(row_pair):
        left_row, right_row = row_pair
        return sample_sum(left_row[:, None], right_row[:, None])[0]
    weight_grad = lax.map(grad_row, (coeffs_all.transpose(1, 0, 2, 3), grads_all.transpose(1, 0, 2, 3)))
    return (field_out, field_grad, weight_grad)
```

```python
import functools
import math

import jax
import jax.numpy as jnp
import numpy as np
from jax import lax
from jax.experimental import pallas as pl
from jax.experimental.pallas import tpu as pltpu
from jax.sharding import PartitionSpec as P

KY = 32
KZ = 16


HIGHEST_PREC = lax.Precision.HIGHEST
GELU_COEF = 0.044715


def partner(block, axis, distance):
    count = lax.axis_size(axis)
    route = []
    for low in range(count):
        high = low | 1 << distance
        if high != low and high < count:
            route += [(low, high), (high, low)]
    return lax.ppermute(block, axis, route)


def angles(freq_count, grid_count):
    frequency = jnp.arange(freq_count, dtype=jnp.int32) - freq_count // 2
    places = jnp.arange(grid_count, dtype=jnp.int32)
    turn_index = jnp.mod(frequency[:, None] * places[None, :], grid_count)
    return turn_index.astype(jnp.float32) * (2.0 * math.pi / grid_count)


def gelu_parts(pre_act):
    root_const = math.sqrt(2.0 / math.pi)
    inner_arg = root_const * (pre_act + GELU_COEF * pre_act * pre_act * pre_act)
    tangent = jnp.tanh(inner_arg)
    activated = 0.5 * pre_act * (1.0 + tangent)
    gelu_slope = 0.5 * (1.0 + tangent) + 0.5 * pre_act * (1.0 - tangent * tangent) * root_const * (
        1.0 + 3.0 * GELU_COEF * pre_act * pre_act
    )
    return (activated, gelu_slope)


def along_z_forward(data_in, table_z):
    return jnp.einsum("pyzc,kz->pykc", data_in, table_z, precision=HIGHEST_PREC)


def along_z_inverse(data_in, table_z):
    return jnp.einsum("pykc,kz->pyzc", data_in, table_z, precision=HIGHEST_PREC)


def forward_yz(local_field, channels):
    planes, y_count, last_width = local_field.shape
    z_count = last_width // channels
    theta_y = angles(KY, y_count)
    table_y = jnp.concatenate([jnp.cos(theta_y), -jnp.sin(theta_y)], 0).astype(jnp.bfloat16)
    first_pass = jnp.einsum("fy,pyq->pfq", table_y, local_field, preferred_element_type=jnp.float32)
    first_pass = first_pass.reshape(planes, 2, KY, z_count, channels)
    theta_z = angles(KZ, z_count)
    cos_z = jnp.cos(theta_z)
    sin_z = jnp.sin(theta_z)
    real_in = first_pass[:, 0]
    imag_in = first_pass[:, 1]
    real_out = along_z_forward(real_in, cos_z) + along_z_forward(imag_in, sin_z)
    imag_out = along_z_forward(imag_in, cos_z) - along_z_forward(real_in, sin_z)
    mode_data = jnp.concatenate([real_out, imag_out], -1)
    return mode_data.reshape(planes, KY * KZ, 2 * channels).astype(jnp.bfloat16)


def forward_x(mode_data, kx_count, norm_scale):
    x_length, mode_block, pair_width = mode_data.shape
    channels = pair_width // 2
    theta_x = angles(kx_count, x_length)
    flat_data = mode_data.reshape(x_length, mode_block * pair_width)
    cos_part = jnp.dot(
        jnp.cos(theta_x).astype(jnp.bfloat16), flat_data, preferred_element_type=jnp.float32
    ).reshape(kx_count, mode_block, pair_width)
    sin_part = jnp.dot(
        jnp.sin(theta_x).astype(jnp.bfloat16), flat_data, preferred_element_type=jnp.float32
    ).reshape(kx_count, mode_block, pair_width)
    real_out = cos_part[..., :channels] + sin_part[..., channels:]
    imag_out = cos_part[..., channels:] - sin_part[..., :channels]
    return (jnp.concatenate([real_out, imag_out], -1) * norm_scale).astype(jnp.bfloat16)


def inverse_x(mixed_modes, x_length):
    kx_count, mode_block, pair_width = mixed_modes.shape
    channels = pair_width // 2
    theta_x = angles(kx_count, x_length).T
    flat_data = mixed_modes.reshape(kx_count, mode_block * pair_width)
    cos_part = jnp.dot(
        jnp.cos(theta_x).astype(jnp.bfloat16), flat_data, preferred_element_type=jnp.float32
    ).reshape(x_length, mode_block, pair_width)
    sin_part = jnp.dot(
        jnp.sin(theta_x).astype(jnp.bfloat16), flat_data, preferred_element_type=jnp.float32
    ).reshape(x_length, mode_block, pair_width)
    real_out = cos_part[..., :channels] - sin_part[..., channels:]
    imag_out = cos_part[..., channels:] + sin_part[..., :channels]
    return jnp.concatenate([real_out, imag_out], -1).astype(jnp.bfloat16)


def inverse_yz(planes_data, y_count, z_count, norm_scale):
    planes, mode_total, pair_width = planes_data.shape
    channels = pair_width // 2
    wide_data = planes_data.astype(jnp.float32).reshape(planes, KY, KZ, pair_width)
    real_in = wide_data[..., :channels]
    imag_in = wide_data[..., channels:]
    theta_z = angles(KZ, z_count)
    cos_z = jnp.cos(theta_z)
    sin_z = jnp.sin(theta_z)
    real_mid = along_z_inverse(real_in, cos_z) - along_z_inverse(imag_in, sin_z)
    imag_mid = along_z_inverse(imag_in, cos_z) + along_z_inverse(real_in, sin_z)
    stacked = jnp.concatenate([real_mid, imag_mid], 1).reshape(planes, 2 * KY, z_count * channels)
    theta_y = angles(KY, y_count)
    table_y = jnp.concatenate([jnp.cos(theta_y), -jnp.sin(theta_y)], 0)
    return jnp.einsum("pfq,fy->pyq", stacked, table_y, precision=HIGHEST_PREC) * norm_scale


def mix_forward(coeffs, weights_local):
    channels = weights_local.shape[2]
    real_part = jnp.einsum(
        "kmc,kmcp->kmp", coeffs[..., :channels], weights_local, preferred_element_type=jnp.float32
    )
    imag_part = jnp.einsum(
        "kmc,kmcp->kmp", coeffs[..., channels:], weights_local, preferred_element_type=jnp.float32
    )
    out_real = real_part[..., :channels] - imag_part[..., channels:]
    out_imag = real_part[..., channels:] + imag_part[..., :channels]
    return jnp.concatenate([out_real, out_imag], -1).astype(jnp.bfloat16)


def mix_backward(coeffs, weights_local):
    channels = weights_local.shape[2]
    swapped = jnp.concatenate([coeffs[..., channels:], -coeffs[..., :channels]], -1)
    first_half = jnp.einsum(
        "kmp,kmcp->kmc", coeffs, weights_local, preferred_element_type=jnp.float32
    )
    second_half = jnp.einsum(
        "kmp,kmcp->kmc", swapped, weights_local, preferred_element_type=jnp.float32
    )
    return jnp.concatenate([first_half, second_half], -1).astype(jnp.bfloat16)


def pointwise(local_field, weights_small):
    planes, y_count, last_width = local_field.shape
    channels = weights_small.shape[0]
    paired = jnp.kron(jnp.eye(2, dtype=weights_small.dtype), weights_small)
    cell_pairs = local_field.reshape(planes * y_count * last_width // (2 * channels), 2 * channels)
    return jnp.dot(cell_pairs, paired, preferred_element_type=jnp.float32).reshape(
        planes, y_count, last_width
    )


def sample_sum(left_side, right_side):
    channels = left_side.shape[-1] // 2
    left_real = left_side[..., :channels]
    left_imag = left_side[..., channels:]
    right_real = right_side[..., :channels]
    right_imag = right_side[..., channels:]

    def outer_sum(left_op, right_op):
        return jnp.einsum("skmc,skmo->kmco", left_op, right_op, preferred_element_type=jnp.float32)

    real_sum = outer_sum(left_real, right_real) + outer_sum(left_imag, right_imag)
    imag_sum = outer_sum(left_real, right_imag) - outer_sum(left_imag, right_real)
    return jnp.concatenate([real_sum, imag_sum], -1)


def partner_rounds(slot_buffer):
    slot_count = slot_buffer.shape[0]
    my_index = lax.axis_index("gx")
    for bit_pos in range(slot_count.bit_length() - 1):
        shaped = slot_buffer.reshape(
            (slot_count >> bit_pos + 1, 2, 1 << bit_pos) + slot_buffer.shape[1:]
        )
        lower_half = shaped[:, 0]
        upper_half = shaped[:, 1]
        own_bit = jnp.bitwise_and(jnp.right_shift(my_index, bit_pos), 1) == 1
        outgoing = jnp.where(own_bit, lower_half, upper_half)
        incoming = partner(outgoing, "gx", bit_pos)
        new_lower = jnp.where(own_bit, incoming, lower_half)
        new_upper = jnp.where(own_bit, upper_half, incoming)
        slot_buffer = jnp.stack([new_lower, new_upper], 1).reshape(slot_buffer.shape)
    return slot_buffer


def toward_modes(mode_data):
    planes, mode_total, pair_width = mode_data.shape
    group_size = lax.axis_size("gx")
    slot_buffer = mode_data.reshape(
        planes, group_size, mode_total // group_size, pair_width
    ).transpose(1, 0, 2, 3)
    return partner_rounds(slot_buffer).reshape(
        planes * group_size, mode_total // group_size, pair_width
    )


def toward_planes(back_planes):
    x_length, mode_block, pair_width = back_planes.shape
    group_size = lax.axis_size("gx")
    slot_buffer = back_planes.reshape(group_size, x_length // group_size, mode_block, pair_width)
    arrived = partner_rounds(slot_buffer)
    return arrived.transpose(1, 0, 2, 3).reshape(
        x_length // group_size, group_size * mode_block, pair_width
    )


MESH = pl.DeviceIdType.MESH
NT = (((1,), (1,)), ((), ()))


def angles_host(freq_count, grid_count):
    frequency = np.arange(freq_count) - freq_count // 2
    turn_index = np.mod(frequency[:, None] * np.arange(grid_count)[None, :], grid_count)
    return turn_index.astype(np.float32) * np.float32(2.0 * math.pi / grid_count)


def host_tables(y_count, z_count, channels):
    theta_y = angles_host(KY, y_count)
    table_y = np.concatenate([np.cos(theta_y), -np.sin(theta_y)], 0)
    theta_z = angles_host(KZ, z_count)
    eye = np.eye(16, dtype=np.float32)
    fwd_z = np.concatenate([np.kron(eye, np.cos(theta_z)), np.kron(eye, np.sin(theta_z))], 0)
    inv_z = np.concatenate([np.kron(eye, np.cos(theta_z).T), np.kron(eye, np.sin(theta_z).T)], 0)
    spread = np.tile(np.eye(channels, dtype=np.float32), (256 // channels, 1))
    return [jnp.asarray(t, jnp.bfloat16) for t in (table_y, table_y.T, fwd_z, inv_z, spread)]


def x_tables(kx_count, x_length):
    theta_x = angles_host(kx_count, x_length)[:x_length]
    rounded = [np.asarray(f(theta_x), jnp.bfloat16).astype(np.float32) for f in (np.cos, np.sin)]
    return [np.where(np.abs(t) < 1e-5, 0.0, t) for t in rounded]


def dot32(left, right):
    return jnp.dot(left, right, preferred_element_type=jnp.float32)


def lanes_low(shape):
    return lax.broadcasted_iota(jnp.int32, shape, 1) < 64


def swap(block):
    return pltpu.roll(block, 64, 1)


def turned(block):
    swapped = swap(block)
    return jnp.where(lanes_low(block.shape), swapped, -swapped)


def x_pass(read, write, cos_t, sin_t, mode_block):
    length = cos_t.shape[0]
    half = length // 2

    def step(index, carry):
        rows = pl.ds(pl.multiple_of(index * 16, 16), 16)
        data = [read(j, rows) for j in range(length)]
        folded = [
            [data[j] + data[j + half] for j in range(half)],
            [data[j] - data[j + half] for j in range(half)],
        ]
        spun = [[turned(block) for block in group] for group in folded]
        for k in range(length):
            total = None
            for j in range(half):
                for coef, block in ((cos_t[k, j], folded[k % 2][j]), (sin_t[k, j], spun[k % 2][j])):
                    coef = float(coef)
                    if coef == 0.0:
                        continue
                    term = block if coef == 1.0 else -block if coef == -1.0 else block * coef
                    total = term if total is None else total + term
            write(k, rows, total)
        return carry

    lax.fori_loop(0, mode_block // 16, step, 0)


def forward_planes(source, table_y, fwd_z, mid, send):
    first_pass = dot32(table_y[...], source[...])
    low = lanes_low((KY, 128))
    for pair in range(first_pass.shape[1] // 128):
        real_in = first_pass[:KY, pair * 128 : pair * 128 + 128]
        imag_in = first_pass[KY:, pair * 128 : pair * 128 + 128]
        mid[:, 2 * pair, :] = jnp.where(low, real_in, swap(imag_in))
        mid[:, 2 * pair + 1, :] = jnp.where(low, swap(real_in), imag_in)
    group_size, mode_block, pair_width = send.shape
    per_half = 256 // mode_block
    for half in range(2):
        block = mid[16 * half : 16 * half + 16].reshape(256, pair_width).astype(jnp.bfloat16)
        both = dot32(fwd_z[...], block)
        data = both[:256] + turned(both[256:])
        send[half * per_half : (half + 1) * per_half] = data.reshape(
            per_half, mode_block, pair_width
        ).astype(jnp.bfloat16)


def inverse_planes(arrived, inv_z, mid, stacked, norm_scale):
    group_size, mode_block, pair_width = arrived.shape
    per_half = 256 // mode_block
    for half in range(2):
        block = arrived[half * per_half : (half + 1) * per_half].reshape(256, pair_width)
        both = dot32(inv_z[...], block)
        mid[16 * half : 16 * half + 16] = (
            (both[:256] - turned(both[256:])) * norm_scale
        ).reshape(16, 16, pair_width)
    low = lanes_low((KY, 128))
    for pair in range(stacked.shape[1] // 128):
        even = mid[:, 2 * pair, :]
        odd = mid[:, 2 * pair + 1, :]
        columns = slice(pair * 128, pair * 128 + 128)
        stacked[:KY, columns] = jnp.where(low, even, swap(odd)).astype(jnp.bfloat16)
        stacked[KY:, columns] = jnp.where(low, swap(even), odd).astype(jnp.bfloat16)


def fused_kernel(
    cos_x, sin_x, norm_scale, group_size, sample_count, alias_count,
    field_hbm, cot_hbm, weights_hbm, point_ref, table_y, table_y_t, fwd_z, inv_z, spread,
    field_out, field_grad, shared_in, shared_grad,
    field, cot, weights, send, arrive, coef_in, coef_grad, mixed, mid, stacked, accum,
    out_block, grad_block, tail_block, point_wide, point_wide_t,
    load_sem, weight_sem, send_sem, recv_sem, sa_send, sa_recv, own_sem,
):
    me = lax.axis_index("gx")
    mine = lax.axis_index("sa")
    x_length = group_size
    mode_block = send.shape[2]
    groups = mode_block // 16

    load_field = pltpu.make_async_copy(field_hbm.at[0, 0], field, load_sem.at[0])
    load_cot = pltpu.make_async_copy(cot_hbm.at[0, 0], cot, load_sem.at[1])
    load_field.start()
    load_cot.start()

    def weight_copy(kx):
        return pltpu.make_async_copy(weights_hbm.at[kx], weights.at[kx], weight_sem.at[kx])

    for residue in range(x_length):
        for alias in range(alias_count):
            weight_copy(residue + x_length * alias).start()

    barrier = pltpu.get_barrier_semaphore()
    for hop in range(1, group_size):
        pl.semaphore_signal(
            barrier, inc=1, device_id={"gx": lax.rem(me + hop, group_size)}, device_id_type=MESH
        )
    for hop in range(1, sample_count):
        pl.semaphore_signal(
            barrier, inc=1, device_id={"sa": lax.rem(mine + hop, sample_count)}, device_id_type=MESH
        )

    def plane_copy(turn, hop):
        target = lax.rem(me + hop, group_size)
        return pltpu.make_async_remote_copy(
            src_ref=send.at[turn, target],
            dst_ref=arrive.at[turn, me],
            send_sem=send_sem.at[turn, hop],
            recv_sem=recv_sem.at[turn, hop],
            device_id={"gx": target},
            device_id_type=MESH,
        )

    def exchange_start(turn):
        for hop in range(1, group_size):
            plane_copy(turn, hop).start()
        arrive[turn, me] = send[turn, me]

    def exchange_wait(turn):
        for hop in range(1, group_size):
            plane_copy(turn, hop).wait_recv()

    def sample_copy(which, hop):
        source, target = ((coef_in, shared_in), (coef_grad, shared_grad))[which]
        return pltpu.make_async_remote_copy(
            src_ref=source,
            dst_ref=target.at[mine],
            send_sem=sa_send.at[which, hop],
            recv_sem=sa_recv.at[which, hop],
            device_id={"sa": lax.rem(mine + hop, sample_count)},
            device_id_type=MESH,
        )

    def own_copy(which):
        source, target = ((coef_in, shared_in), (coef_grad, shared_grad))[which]
        return pltpu.make_async_copy(source, target.at[mine], own_sem.at[which])

    def samples_start(which):
        for hop in range(1, sample_count):
            sample_copy(which, hop).start()
        own_copy(which).start()

    def forward_modes(turn, coef):
        def read(j, rows):
            return arrive[turn, j, rows, :].astype(jnp.float32)

        def write(k, rows, value):
            coef[k, rows, :] = (value * norm_scale).astype(jnp.bfloat16)

        x_pass(read, write, cos_x, sin_x, mode_block)

    def inverse_modes(turn):
        def read(j, rows):
            return mixed[j, rows, :]

        def write(k, rows, value):
            send[turn, k, rows, :] = value.astype(jnp.bfloat16)

        x_pass(read, write, cos_x.T, -sin_x.T, mode_block)

    def fold_weights(residue, carry):
        for alias in range(alias_count):
            weight_copy(residue + x_length * alias).wait()

        def step(index, inner):
            rows = pl.ds(pl.multiple_of(index * 128, 128), 128)
            total = weights[residue, rows, :].astype(jnp.float32)
            for alias in range(1, alias_count):
                total = total + weights[residue + x_length * alias, rows, :].astype(jnp.float32)
            weights[residue, rows, :] = total.astype(jnp.bfloat16)
            return inner

        lax.fori_loop(0, weights.shape[1] // 128, step, 0, unroll=4)
        return carry

    own_lanes = (
        lax.broadcasted_iota(jnp.int32, (16, 1024), 1) // 64
        == lax.broadcasted_iota(jnp.int32, (16, 1024), 0)
    )
    low16 = lanes_low((16, 128))

    def diagonal(block):
        wide = jnp.concatenate([block] * 8, axis=1)
        return jnp.where(own_lanes, wide, 0.0).astype(jnp.bfloat16)

    def gathered(block):
        kept = jnp.where(own_lanes, block, 0.0)
        total = kept[:, :128]
        for part in range(1, 8):
            total = total + kept[:, part * 128 : part * 128 + 128]
        return total + swap(total)

    def mix_in(residue, carry):
        def step(index, inner):
            rows = pl.ds(pl.multiple_of(index * 16, 16), 16)
            coef = coef_in[residue, rows, :].astype(jnp.float32)
            other = swap(coef)
            left = jnp.concatenate(
                [diagonal(jnp.where(low16, coef, other)), diagonal(jnp.where(low16, other, coef))], 0
            )
            right = weights[residue, pl.ds(pl.multiple_of(index * 1024, 1024), 1024), :]
            product = dot32(left, right)
            mixed[residue, rows, :] = product[:16] - turned(product[16:])
            return inner

        lax.fori_loop(0, groups, step, 0, unroll=2)
        return carry

    def mix_back(residue, carry):
        def step(index, inner):
            rows = pl.ds(pl.multiple_of(index * 16, 16), 16)
            coef = coef_grad[residue, rows, :].astype(jnp.float32)
            left = jnp.concatenate([coef, turned(coef)], 0).astype(jnp.bfloat16)
            right = weights[residue, pl.ds(pl.multiple_of(index * 1024, 1024), 1024), :]
            product = lax.dot_general(left, right, NT, preferred_element_type=jnp.float32)
            mixed[residue, rows, :] = jnp.where(low16, gathered(product[:16]), gathered(product[16:]))
            return inner

        lax.fori_loop(0, groups, step, 0, unroll=2)
        return carry

    def pointwise_into(source, wide):
        for part in range(accum.shape[1] // 256):
            columns = slice(part * 256, part * 256 + 256)
            accum[:, columns] = dot32(source[:, columns], wide[...])

    def add_spectrum():
        for part in range(accum.shape[1] // 256):
            columns = slice(part * 256, part * 256 + 256)
            accum[:, columns] += dot32(table_y_t[...], stacked[:, columns])

    load_field.wait()
    forward_planes(field, table_y, fwd_z, mid, send.at[0])
    pl.semaphore_wait(barrier, group_size + sample_count - 2)
    exchange_start(0)

    same_block = (
        lax.broadcasted_iota(jnp.int32, (256, 256), 0) // 64
        == lax.broadcasted_iota(jnp.int32, (256, 256), 1) // 64
    )

    def widened(block):
        wide = lax.dot_general(block.astype(jnp.bfloat16), spread[...], NT, preferred_element_type=jnp.float32)
        return jnp.where(same_block, wide, 0.0).astype(jnp.bfloat16)

    point_wide[...] = widened(dot32(spread[...], point_ref[...]))
    point_wide_t[...] = widened(
        lax.dot_general(spread[...], point_ref[...], NT, preferred_element_type=jnp.float32)
    )
    pointwise_into(field, point_wide)

    early = x_length // 4
    lax.fori_loop(0, early, fold_weights, 0)
    exchange_wait(0)
    forward_modes(0, coef_in)
    samples_start(0)
    lax.fori_loop(0, early, mix_in, 0)
    lax.fori_loop(early, x_length, lambda r, c: mix_in(r, fold_weights(r, c)), 0)
    inverse_modes(1)
    exchange_start(1)
    load_cot.wait()
    exchange_wait(1)
    inverse_planes(arrive.at[1], inv_z, mid, stacked, norm_scale)
    add_spectrum()

    def activate(index, carry):
        rows = pl.ds(pl.multiple_of(index * 16, 16), 16)
        activated, gelu_slope = gelu_parts(accum[rows, :])
        out_block[rows, :] = activated.astype(jnp.bfloat16)
        grad_block[rows, :] = (cot[rows, :].astype(jnp.float32) * gelu_slope).astype(jnp.bfloat16)
        return carry

    lax.fori_loop(0, accum.shape[0] // 16, activate, 0)
    store_out = pltpu.make_async_copy(out_block, field_out.at[0, 0], load_sem.at[2])
    store_out.start()

    forward_planes(grad_block, table_y, fwd_z, mid, send.at[2])
    exchange_start(2)
    pointwise_into(grad_block, point_wide_t)
    exchange_wait(2)
    forward_modes(2, coef_grad)
    samples_start(1)
    lax.fori_loop(0, x_length, mix_back, 0)
    inverse_modes(3)
    exchange_start(3)
    exchange_wait(3)
    inverse_planes(arrive.at[3], inv_z, mid, stacked, norm_scale)
    add_spectrum()
    tail_block[...] = accum[...].astype(jnp.bfloat16)
    store_grad = pltpu.make_async_copy(tail_block, field_grad.at[0, 0], load_sem.at[3])
    store_grad.start()

    for turn in range(4):
        for hop in range(1, group_size):
            plane_copy(turn, hop).wait_send()
    for which in range(2):
        own_copy(which).wait()
        for hop in range(1, sample_count):
            sample_copy(which, hop).wait()
    store_out.wait()
    store_grad.wait()


def weight_kernel(left_ref, right_ref, out_ref):
    sample_count = left_ref.shape[0]
    depth = 2 * sample_count * 16
    own_lane = lax.broadcasted_iota(jnp.int32, (64, depth), 1) % 16
    for group in range(left_ref.shape[2] // 16):
        rows = slice(group * 16, group * 16 + 16)
        left = jnp.concatenate([left_ref[s, 0, rows, :] for s in range(sample_count)], 0)
        right = jnp.concatenate([right_ref[s, 0, rows, :] for s in range(sample_count)], 0)
        flipped = left.astype(jnp.float32).T
        flipped = jnp.concatenate([flipped[:64], flipped[64:]], axis=1)
        wide = right.astype(jnp.float32)
        stack = jnp.concatenate([wide, turned(wide)], 0).astype(jnp.bfloat16)
        for mode in range(16):
            kept = jnp.where(own_lane == mode, flipped, 0.0).astype(jnp.bfloat16)
            out_ref[0, group * 16 + mode] = dot32(kept, stack)


def fused_device(field_in, cotangent, mode_weights, point_weights):
    y_count, last_width = field_in.shape[2:]
    channels = point_weights.shape[0]
    z_count = last_width // channels
    kx_count, mode_block = mode_weights.shape[:2]
    group_size = lax.axis_size("gx")
    sample_count = lax.axis_size("sa")
    x_length = group_size
    pair_width = 2 * channels
    norm_scale = 1.0 / math.sqrt(x_length * y_count * z_count)
    cos_x, sin_x = x_tables(kx_count, x_length)
    bf16, f32 = jnp.bfloat16, jnp.float32
    plane = (y_count, last_width)
    coef_shape = (x_length, mode_block, pair_width)
    anywhere = pl.BlockSpec(memory_space=pl.ANY)
    vmem = pl.BlockSpec(memory_space=pltpu.VMEM)
    field_out, field_grad, shared_in, shared_grad = pl.pallas_call(
        functools.partial(
            fused_kernel, cos_x, sin_x, norm_scale, group_size, sample_count, kx_count // x_length
        ),
        out_shape=[
            jax.ShapeDtypeStruct((1, 1) + plane, bf16),
            jax.ShapeDtypeStruct((1, 1) + plane, bf16),
            jax.ShapeDtypeStruct((sample_count,) + coef_shape, bf16),
            jax.ShapeDtypeStruct((sample_count,) + coef_shape, bf16),
        ],
        in_specs=[anywhere] * 3 + [vmem] * 6,
        out_specs=[anywhere] * 4,
        scratch_shapes=[
            pltpu.VMEM(plane, bf16),
            pltpu.VMEM(plane, bf16),
            pltpu.VMEM((kx_count, mode_block * channels, pair_width), bf16),
            pltpu.VMEM((4,) + coef_shape, bf16),
            pltpu.VMEM((4,) + coef_shape, bf16),
            pltpu.VMEM(coef_shape, bf16),
            pltpu.VMEM(coef_shape, bf16),
            pltpu.VMEM(coef_shape, f32),
            pltpu.VMEM((KY, z_count, pair_width), f32),
            pltpu.VMEM((2 * KY, last_width), bf16),
            pltpu.VMEM(plane, f32),
            pltpu.VMEM(plane, bf16),
            pltpu.VMEM(plane, bf16),
            pltpu.VMEM(plane, bf16),
            pltpu.VMEM((256, 256), bf16),
            pltpu.VMEM((256, 256), bf16),
            pltpu.SemaphoreType.DMA((4,)),
            pltpu.SemaphoreType.DMA((kx_count,)),
            pltpu.SemaphoreType.DMA((4, group_size)),
            pltpu.SemaphoreType.DMA((4, group_size)),
            pltpu.SemaphoreType.DMA((2, sample_count)),
            pltpu.SemaphoreType.DMA((2, sample_count)),
            pltpu.SemaphoreType.DMA((2,)),
        ],
        compiler_params=pltpu.CompilerParams(
            collective_id=0, has_side_effects=True, vmem_limit_bytes=56 * 1024 * 1024
        ),
        name="fourier_layer",
    )(
        field_in, cotangent,
        mode_weights.reshape(kx_count, mode_block * channels, pair_width),
        point_weights, *host_tables(y_count, z_count, channels),
    )
    coef_spec = pl.BlockSpec((sample_count, 1, mode_block, pair_width), lambda r: (0, r, 0, 0))
    weight_grad = pl.pallas_call(
        weight_kernel,
        out_shape=jax.ShapeDtypeStruct((x_length, mode_block, channels, pair_width), f32),
        grid=(x_length,),
        in_specs=[coef_spec, coef_spec],
        out_specs=pl.BlockSpec((1, mode_block, channels, pair_width), lambda r: (r, 0, 0, 0)),
        compiler_params=pltpu.CompilerParams(vmem_limit_bytes=32 * 1024 * 1024),
        name="weight_gradient",
    )(shared_in, shared_grad)
    return field_out, field_grad, weight_grad


def folds(field_in, mode_weights, point_weights):
    group_size, sample_count = lax.axis_size("gx"), lax.axis_size("sa")
    kx_count, mode_block, channels = mode_weights.shape[:3]
    planes, y_count, last_width = field_in.shape[1:]
    return (
        planes == 1
        and field_in.shape[0] == 1
        and channels == 64
        and last_width == 16 * channels
        and y_count % 16 == 0
        and mode_block % 16 == 0
        and 256 % mode_block == 0
        and group_size % 4 == 0
        and kx_count % group_size == 0
        and kx_count == sample_count * group_size
    )


def on_device(field_in, cotangent, mode_weights, point_weights):
    if folds(field_in, mode_weights, point_weights):
        return fused_device(field_in, cotangent, mode_weights, point_weights)
    local_field = field_in[0]
    planes, y_count, last_width = local_field.shape
    channels = point_weights.shape[0]
    z_count = last_width // channels
    kx_count = mode_weights.shape[0]
    x_length = planes * lax.axis_size("gx")
    norm_scale = 1.0 / math.sqrt(x_length * y_count * z_count)
    coeffs_in = forward_x(toward_modes(forward_yz(local_field, channels)), kx_count, norm_scale)
    mixed_modes = mix_forward(coeffs_in, mode_weights)
    spec_out = inverse_yz(
        toward_planes(inverse_x(mixed_modes, x_length)), y_count, z_count, norm_scale
    )
    pre_act = spec_out + pointwise(local_field, point_weights)
    activated, gelu_slope = gelu_parts(pre_act)
    out_grad = (cotangent[0].astype(jnp.float32) * gelu_slope).astype(jnp.bfloat16)
    coeffs_grad = forward_x(toward_modes(forward_yz(out_grad, channels)), kx_count, norm_scale)
    back_modes = mix_backward(coeffs_grad, mode_weights)
    spec_grad = inverse_yz(
        toward_planes(inverse_x(back_modes, x_length)), y_count, z_count, norm_scale
    )
    field_grad = (spec_grad + pointwise(out_grad, point_weights.T)).astype(jnp.bfloat16)
    shared_in, shared_grad = (
        lax.all_to_all(coeffs_in[None], "sa", split_axis=1, concat_axis=0, tiled=True),
        lax.all_to_all(coeffs_grad[None], "sa", split_axis=1, concat_axis=0, tiled=True),
    )
    weight_grad = sample_sum(shared_in, shared_grad)
    return (activated.astype(jnp.bfloat16)[None], field_grad[None], weight_grad)


def solution(mesh):
    in_specs = (
        P("sa", "gx", None, None),
        P("sa", "gx", None, None),
        P(None, "gx", None, None),
        P(),
    )
    out_specs = (P("sa", "gx", None, None), P("sa", "gx", None, None), P("sa", "gx", None, None))
    return jax.shard_map(
        on_device, mesh=mesh, in_specs=in_specs, out_specs=out_specs, check_vma=False
    )
```

```python
import functools
import math

import jax
import jax.numpy as jnp
import numpy as np
from jax import lax
from jax.experimental import pallas as pl
from jax.experimental.pallas import tpu as pltpu
from jax.sharding import PartitionSpec as P

KY = 32
KZ = 16


HIGHEST_PREC = lax.Precision.HIGHEST
GELU_COEF = 0.044715


def partner(block, axis, distance):
    count = lax.axis_size(axis)
    route = []
    for low in range(count):
        high = low | 1 << distance
        if high != low and high < count:
            route += [(low, high), (high, low)]
    return lax.ppermute(block, axis, route)


def angles(freq_count, grid_count):
    frequency = jnp.arange(freq_count, dtype=jnp.int32) - freq_count // 2
    places = jnp.arange(grid_count, dtype=jnp.int32)
    turn_index = jnp.mod(frequency[:, None] * places[None, :], grid_count)
    return turn_index.astype(jnp.float32) * (2.0 * math.pi / grid_count)


def gelu_parts(pre_act):
    root_const = math.sqrt(2.0 / math.pi)
    inner_arg = root_const * (pre_act + GELU_COEF * pre_act * pre_act * pre_act)
    tangent = jnp.tanh(inner_arg)
    activated = 0.5 * pre_act * (1.0 + tangent)
    gelu_slope = 0.5 * (1.0 + tangent) + 0.5 * pre_act * (1.0 - tangent * tangent) * root_const * (
        1.0 + 3.0 * GELU_COEF * pre_act * pre_act
    )
    return (activated, gelu_slope)


def along_z_forward(data_in, table_z):
    return jnp.einsum("pyzc,kz->pykc", data_in, table_z, precision=HIGHEST_PREC)


def along_z_inverse(data_in, table_z):
    return jnp.einsum("pykc,kz->pyzc", data_in, table_z, precision=HIGHEST_PREC)


def forward_yz(local_field, channels):
    planes, y_count, last_width = local_field.shape
    z_count = last_width // channels
    theta_y = angles(KY, y_count)
    table_y = jnp.concatenate([jnp.cos(theta_y), -jnp.sin(theta_y)], 0).astype(jnp.bfloat16)
    first_pass = jnp.einsum("fy,pyq->pfq", table_y, local_field, preferred_element_type=jnp.float32)
    first_pass = first_pass.reshape(planes, 2, KY, z_count, channels)
    theta_z = angles(KZ, z_count)
    cos_z = jnp.cos(theta_z)
    sin_z = jnp.sin(theta_z)
    real_in = first_pass[:, 0]
    imag_in = first_pass[:, 1]
    real_out = along_z_forward(real_in, cos_z) + along_z_forward(imag_in, sin_z)
    imag_out = along_z_forward(imag_in, cos_z) - along_z_forward(real_in, sin_z)
    mode_data = jnp.concatenate([real_out, imag_out], -1)
    return mode_data.reshape(planes, KY * KZ, 2 * channels).astype(jnp.bfloat16)


def forward_x(mode_data, kx_count, norm_scale):
    x_length, mode_block, pair_width = mode_data.shape
    channels = pair_width // 2
    theta_x = angles(kx_count, x_length)
    flat_data = mode_data.reshape(x_length, mode_block * pair_width)
    cos_part = jnp.dot(
        jnp.cos(theta_x).astype(jnp.bfloat16), flat_data, preferred_element_type=jnp.float32
    ).reshape(kx_count, mode_block, pair_width)
    sin_part = jnp.dot(
        jnp.sin(theta_x).astype(jnp.bfloat16), flat_data, preferred_element_type=jnp.float32
    ).reshape(kx_count, mode_block, pair_width)
    real_out = cos_part[..., :channels] + sin_part[..., channels:]
    imag_out = cos_part[..., channels:] - sin_part[..., :channels]
    return (jnp.concatenate([real_out, imag_out], -1) * norm_scale).astype(jnp.bfloat16)


def inverse_x(mixed_modes, x_length):
    kx_count, mode_block, pair_width = mixed_modes.shape
    channels = pair_width // 2
    theta_x = angles(kx_count, x_length).T
    flat_data = mixed_modes.reshape(kx_count, mode_block * pair_width)
    cos_part = jnp.dot(
        jnp.cos(theta_x).astype(jnp.bfloat16), flat_data, preferred_element_type=jnp.float32
    ).reshape(x_length, mode_block, pair_width)
    sin_part = jnp.dot(
        jnp.sin(theta_x).astype(jnp.bfloat16), flat_data, preferred_element_type=jnp.float32
    ).reshape(x_length, mode_block, pair_width)
    real_out = cos_part[..., :channels] - sin_part[..., channels:]
    imag_out = cos_part[..., channels:] + sin_part[..., :channels]
    return jnp.concatenate([real_out, imag_out], -1).astype(jnp.bfloat16)


def inverse_yz(planes_data, y_count, z_count, norm_scale):
    planes, mode_total, pair_width = planes_data.shape
    channels = pair_width // 2
    wide_data = planes_data.astype(jnp.float32).reshape(planes, KY, KZ, pair_width)
    real_in = wide_data[..., :channels]
    imag_in = wide_data[..., channels:]
    theta_z = angles(KZ, z_count)
    cos_z = jnp.cos(theta_z)
    sin_z = jnp.sin(theta_z)
    real_mid = along_z_inverse(real_in, cos_z) - along_z_inverse(imag_in, sin_z)
    imag_mid = along_z_inverse(imag_in, cos_z) + along_z_inverse(real_in, sin_z)
    stacked = jnp.concatenate([real_mid, imag_mid], 1).reshape(planes, 2 * KY, z_count * channels)
    theta_y = angles(KY, y_count)
    table_y = jnp.concatenate([jnp.cos(theta_y), -jnp.sin(theta_y)], 0)
    return jnp.einsum("pfq,fy->pyq", stacked, table_y, precision=HIGHEST_PREC) * norm_scale


def mix_forward(coeffs, weights_local):
    channels = weights_local.shape[2]
    real_part = jnp.einsum(
        "kmc,kmcp->kmp", coeffs[..., :channels], weights_local, preferred_element_type=jnp.float32
    )
    imag_part = jnp.einsum(
        "kmc,kmcp->kmp", coeffs[..., channels:], weights_local, preferred_element_type=jnp.float32
    )
    out_real = real_part[..., :channels] - imag_part[..., channels:]
    out_imag = real_part[..., channels:] + imag_part[..., :channels]
    return jnp.concatenate([out_real, out_imag], -1).astype(jnp.bfloat16)


def mix_backward(coeffs, weights_local):
    channels = weights_local.shape[2]
    swapped = jnp.concatenate([coeffs[..., channels:], -coeffs[..., :channels]], -1)
    first_half = jnp.einsum(
        "kmp,kmcp->kmc", coeffs, weights_local, preferred_element_type=jnp.float32
    )
    second_half = jnp.einsum(
        "kmp,kmcp->kmc", swapped, weights_local, preferred_element_type=jnp.float32
    )
    return jnp.concatenate([first_half, second_half], -1).astype(jnp.bfloat16)


def pointwise(local_field, weights_small):
    planes, y_count, last_width = local_field.shape
    channels = weights_small.shape[0]
    paired = jnp.kron(jnp.eye(2, dtype=weights_small.dtype), weights_small)
    cell_pairs = local_field.reshape(planes * y_count * last_width // (2 * channels), 2 * channels)
    return jnp.dot(cell_pairs, paired, preferred_element_type=jnp.float32).reshape(
        planes, y_count, last_width
    )


def sample_sum(left_side, right_side):
    channels = left_side.shape[-1] // 2
    left_real = left_side[..., :channels]
    left_imag = left_side[..., channels:]
    right_real = right_side[..., :channels]
    right_imag = right_side[..., channels:]

    def outer_sum(left_op, right_op):
        return jnp.einsum("skmc,skmo->kmco", left_op, right_op, preferred_element_type=jnp.float32)

    real_sum = outer_sum(left_real, right_real) + outer_sum(left_imag, right_imag)
    imag_sum = outer_sum(left_real, right_imag) - outer_sum(left_imag, right_real)
    return jnp.concatenate([real_sum, imag_sum], -1)


def partner_rounds(slot_buffer):
    slot_count = slot_buffer.shape[0]
    my_index = lax.axis_index("gx")
    for bit_pos in range(slot_count.bit_length() - 1):
        shaped = slot_buffer.reshape(
            (slot_count >> bit_pos + 1, 2, 1 << bit_pos) + slot_buffer.shape[1:]
        )
        lower_half = shaped[:, 0]
        upper_half = shaped[:, 1]
        own_bit = jnp.bitwise_and(jnp.right_shift(my_index, bit_pos), 1) == 1
        outgoing = jnp.where(own_bit, lower_half, upper_half)
        incoming = partner(outgoing, "gx", bit_pos)
        new_lower = jnp.where(own_bit, incoming, lower_half)
        new_upper = jnp.where(own_bit, upper_half, incoming)
        slot_buffer = jnp.stack([new_lower, new_upper], 1).reshape(slot_buffer.shape)
    return slot_buffer


def toward_modes(mode_data):
    planes, mode_total, pair_width = mode_data.shape
    group_size = lax.axis_size("gx")
    slot_buffer = mode_data.reshape(
        planes, group_size, mode_total // group_size, pair_width
    ).transpose(1, 0, 2, 3)
    return partner_rounds(slot_buffer).reshape(
        planes * group_size, mode_total // group_size, pair_width
    )


def toward_planes(back_planes):
    x_length, mode_block, pair_width = back_planes.shape
    group_size = lax.axis_size("gx")
    slot_buffer = back_planes.reshape(group_size, x_length // group_size, mode_block, pair_width)
    arrived = partner_rounds(slot_buffer)
    return arrived.transpose(1, 0, 2, 3).reshape(
        x_length // group_size, group_size * mode_block, pair_width
    )


MESH = pl.DeviceIdType.MESH
NT = (((1,), (1,)), ((), ()))
ROOT_CONST = math.sqrt(2.0 / math.pi)


def angles_host(freq_count, grid_count):
    frequency = np.arange(freq_count) - freq_count // 2
    turn_index = np.mod(frequency[:, None] * np.arange(grid_count)[None, :], grid_count)
    return turn_index.astype(np.float32) * np.float32(2.0 * math.pi / grid_count)


def host_tables(y_count, z_count, channels):
    theta_y = angles_host(KY, y_count)
    table_y = np.concatenate([np.cos(theta_y), -np.sin(theta_y)], 0)
    theta_z = angles_host(KZ, z_count)
    eye = np.eye(16, dtype=np.float32)
    fwd_z = np.concatenate([np.kron(eye, np.cos(theta_z)), np.kron(eye, np.sin(theta_z))], 0)
    inv_z = np.concatenate([np.kron(eye, np.cos(theta_z).T), np.kron(eye, np.sin(theta_z).T)], 0)
    spread = np.tile(np.eye(channels, dtype=np.float32), (256 // channels, 1))
    return [jnp.asarray(t, jnp.bfloat16) for t in (table_y, table_y.T, fwd_z, inv_z, spread)]


def x_tables(kx_count, x_length):
    theta_x = angles_host(kx_count, x_length)[:x_length]
    rounded = [np.asarray(f(theta_x), jnp.bfloat16).astype(np.float32) for f in (np.cos, np.sin)]
    return [np.where(np.abs(t) < 1e-5, 0.0, t) for t in rounded]


def dot32(left, right):
    return jnp.dot(left, right, preferred_element_type=jnp.float32)


def lanes_low(shape):
    return lax.broadcasted_iota(jnp.int32, shape, 1) < 64


def swap(block):
    return pltpu.roll(block, 64, 1)


def turned(block):
    swapped = swap(block)
    return jnp.where(lanes_low(block.shape), swapped, -swapped)


def x_pass(read, write, cos_t, sin_t, mode_block):
    length = cos_t.shape[0]
    half = length // 2

    def step(index, carry):
        rows = pl.ds(pl.multiple_of(index * 16, 16), 16)
        data = [read(j, rows) for j in range(length)]
        folded = [
            [data[j] + data[j + half] for j in range(half)],
            [data[j] - data[j + half] for j in range(half)],
        ]
        spun = [[turned(block) for block in group] for group in folded]
        for k in range(length):
            total = None
            for j in range(half):
                for coef, block in ((cos_t[k, j], folded[k % 2][j]), (sin_t[k, j], spun[k % 2][j])):
                    coef = float(coef)
                    if coef == 0.0:
                        continue
                    term = block if coef == 1.0 else -block if coef == -1.0 else block * coef
                    total = term if total is None else total + term
            write(k, rows, total)
        return carry

    lax.fori_loop(0, mode_block // 16, step, 0)


def forward_planes(source, table_y, fwd_z, mid, send):
    first_pass = dot32(table_y[...], source[...])
    low = lanes_low((KY, 128))
    for pair in range(first_pass.shape[1] // 128):
        real_in = first_pass[:KY, pair * 128 : pair * 128 + 128]
        imag_in = first_pass[KY:, pair * 128 : pair * 128 + 128]
        mid[:, 2 * pair, :] = jnp.where(low, real_in, swap(imag_in))
        mid[:, 2 * pair + 1, :] = jnp.where(low, swap(real_in), imag_in)
    group_size, mode_block, pair_width = send.shape
    per_half = 256 // mode_block
    for half in range(2):
        block = mid[16 * half : 16 * half + 16].reshape(256, pair_width).astype(jnp.bfloat16)
        both = dot32(fwd_z[...], block)
        data = both[:256] + turned(both[256:])
        send[half * per_half : (half + 1) * per_half] = data.reshape(
            per_half, mode_block, pair_width
        ).astype(jnp.bfloat16)


def inverse_planes(arrived, inv_z, mid, stacked, norm_scale):
    group_size, mode_block, pair_width = arrived.shape
    per_half = 256 // mode_block
    for half in range(2):
        block = arrived[half * per_half : (half + 1) * per_half].reshape(256, pair_width)
        both = dot32(inv_z[...], block)
        mid[16 * half : 16 * half + 16] = (
            (both[:256] - turned(both[256:])) * norm_scale
        ).reshape(16, 16, pair_width)
    low = lanes_low((KY, 128))
    for pair in range(stacked.shape[1] // 128):
        even = mid[:, 2 * pair, :]
        odd = mid[:, 2 * pair + 1, :]
        columns = slice(pair * 128, pair * 128 + 128)
        stacked[:KY, columns] = jnp.where(low, even, swap(odd)).astype(jnp.bfloat16)
        stacked[KY:, columns] = jnp.where(low, swap(even), odd).astype(jnp.bfloat16)


def fused_kernel(
    cos_x, sin_x, norm_scale, group_size, sample_count, alias_count,
    field_hbm, cot_hbm, weights_hbm, point_ref, table_y, table_y_t, fwd_z, inv_z, spread,
    field_out, field_grad, shared_in, shared_grad,
    field, cot, weights, folded, send, arrive, coef_in, coef_grad, mixed, mid, stacked, accum,
    out_block, grad_block, tail_block, point_wide, point_wide_t,
    load_sem, weight_sem, send_sem, recv_sem, sa_send, sa_recv, own_sem,
):
    me = lax.axis_index("gx")
    mine = lax.axis_index("sa")
    x_length = group_size
    mode_block = send.shape[2]
    groups = mode_block // 16

    load_field = pltpu.make_async_copy(field_hbm.at[0, 0], field, load_sem.at[0])
    load_cot = pltpu.make_async_copy(cot_hbm.at[0, 0], cot, load_sem.at[1])
    load_field.start()
    load_cot.start()

    def weight_copy(kx):
        return pltpu.make_async_copy(weights_hbm.at[kx], weights.at[kx], weight_sem.at[kx])

    for residue in range(x_length):
        for alias in range(alias_count):
            weight_copy(residue + x_length * alias).start()

    barrier = pltpu.get_barrier_semaphore()
    for hop in range(1, group_size):
        pl.semaphore_signal(
            barrier, inc=1, device_id={"gx": lax.rem(me + hop, group_size)}, device_id_type=MESH
        )
    for hop in range(1, sample_count):
        pl.semaphore_signal(
            barrier, inc=1, device_id={"sa": lax.rem(mine + hop, sample_count)}, device_id_type=MESH
        )

    def plane_copy(turn, hop):
        target = lax.rem(me + hop, group_size)
        return pltpu.make_async_remote_copy(
            src_ref=send.at[turn, target],
            dst_ref=arrive.at[turn, me],
            send_sem=send_sem.at[turn, hop],
            recv_sem=recv_sem.at[turn, hop],
            device_id={"gx": target},
            device_id_type=MESH,
        )

    def exchange_start(turn):
        for hop in range(1, group_size):
            plane_copy(turn, hop).start()
        arrive[turn, me] = send[turn, me]

    def exchange_wait(turn):
        for hop in range(1, group_size):
            plane_copy(turn, hop).wait_recv()

    def sample_copy(which, hop):
        source, target = ((coef_in, shared_in), (coef_grad, shared_grad))[which]
        return pltpu.make_async_remote_copy(
            src_ref=source,
            dst_ref=target.at[mine],
            send_sem=sa_send.at[which, hop],
            recv_sem=sa_recv.at[which, hop],
            device_id={"sa": lax.rem(mine + hop, sample_count)},
            device_id_type=MESH,
        )

    def own_copy(which):
        source, target = ((coef_in, shared_in), (coef_grad, shared_grad))[which]
        return pltpu.make_async_copy(source, target.at[mine], own_sem.at[which])

    def samples_start(which):
        for hop in range(1, sample_count):
            sample_copy(which, hop).start()
        own_copy(which).start()

    def forward_modes(turn, coef):
        def read(j, rows):
            return arrive[turn, j, rows, :].astype(jnp.float32)

        def write(k, rows, value):
            coef[k, rows, :] = (value * norm_scale).astype(jnp.bfloat16)

        x_pass(read, write, cos_x, sin_x, mode_block)

    def inverse_modes(turn):
        def read(j, rows):
            return mixed[j, rows, :]

        def write(k, rows, value):
            send[turn, k, rows, :] = value.astype(jnp.bfloat16)

        x_pass(read, write, cos_x.T, -sin_x.T, mode_block)

    def wait_weights(residue):
        for alias in range(alias_count):
            weight_copy(residue + x_length * alias).wait()

    def fold_rows(residue, start, count):
        for part in range(count // 128):
            rows = pl.ds(pl.multiple_of(start + part * 128, 128), 128)
            total = weights[residue, rows, :].astype(jnp.float32)
            for alias in range(1, alias_count):
                total = total + weights[residue + x_length * alias, rows, :].astype(jnp.float32)
            folded[residue, rows, :] = total.astype(jnp.bfloat16)

    def fold_weights(residue, carry):
        wait_weights(residue)

        def step(index, inner):
            fold_rows(residue, index * 1024, 1024)
            return inner

        lax.fori_loop(0, groups, step, 0)
        return carry

    own_lanes = (
        lax.broadcasted_iota(jnp.int32, (16, 1024), 1) // 64
        == lax.broadcasted_iota(jnp.int32, (16, 1024), 0)
    )
    low16 = lanes_low((16, 128))

    def diagonal(block):
        wide = jnp.concatenate([block] * 8, axis=1)
        return jnp.where(own_lanes, wide, 0.0).astype(jnp.bfloat16)

    def gathered(block):
        kept = jnp.where(own_lanes, block, 0.0)
        total = kept[:, :128]
        for part in range(1, 8):
            total = total + kept[:, part * 128 : part * 128 + 128]
        return total + swap(total)

    def mix_in_group(residue, group):
        rows = slice(group * 16, group * 16 + 16)
        coef = coef_in[residue, rows, :].astype(jnp.float32)
        other = swap(coef)
        left = jnp.concatenate(
            [diagonal(jnp.where(low16, coef, other)), diagonal(jnp.where(low16, other, coef))], 0
        )
        product = dot32(left, folded[residue, group * 1024 : group * 1024 + 1024, :])
        mixed[residue, rows, :] = product[:16] - turned(product[16:])

    def mix_in(residue, carry):
        for group in range(groups):
            mix_in_group(residue, group)
        return carry

    def mix_and_fold(residue, carry):
        wait_weights(residue)
        for group in range(groups):
            mix_in_group(residue - 1, group)
            fold_rows(residue, group * 1024, 1024)
        return carry

    def mix_back(residue, carry):
        for group in range(groups):
            rows = slice(group * 16, group * 16 + 16)
            coef = coef_grad[residue, rows, :].astype(jnp.float32)
            left = jnp.concatenate([coef, turned(coef)], 0).astype(jnp.bfloat16)
            right = folded[residue, group * 1024 : group * 1024 + 1024, :]
            product = lax.dot_general(left, right, NT, preferred_element_type=jnp.float32)
            mixed[residue, rows, :] = jnp.where(
                low16, gathered(product[:16]), gathered(product[16:])
            )
        return carry

    def pointwise_into(source, wide):
        for part in range(accum.shape[1] // 256):
            columns = slice(part * 256, part * 256 + 256)
            accum[:, columns] = dot32(source[:, columns], wide[...])

    def add_spectrum():
        for part in range(accum.shape[1] // 256):
            columns = slice(part * 256, part * 256 + 256)
            accum[:, columns] += dot32(table_y_t[...], stacked[:, columns])

    load_field.wait()
    forward_planes(field, table_y, fwd_z, mid, send.at[0])
    pl.semaphore_wait(barrier, group_size + sample_count - 2)
    exchange_start(0)

    same_block = (
        lax.broadcasted_iota(jnp.int32, (256, 256), 0) // 64
        == lax.broadcasted_iota(jnp.int32, (256, 256), 1) // 64
    )

    def widened(block):
        wide = lax.dot_general(block.astype(jnp.bfloat16), spread[...], NT, preferred_element_type=jnp.float32)
        return jnp.where(same_block, wide, 0.0).astype(jnp.bfloat16)

    point_wide[...] = widened(dot32(spread[...], point_ref[...]))
    point_wide_t[...] = widened(
        lax.dot_general(spread[...], point_ref[...], NT, preferred_element_type=jnp.float32)
    )
    pointwise_into(field, point_wide)

    early = 3
    lax.fori_loop(0, early, fold_weights, 0)
    exchange_wait(0)
    forward_modes(0, coef_in)
    samples_start(0)
    lax.fori_loop(0, early - 1, mix_in, 0)
    lax.fori_loop(early, x_length, mix_and_fold, 0)
    mix_in(x_length - 1, 0)
    inverse_modes(1)
    exchange_start(1)
    load_cot.wait()
    exchange_wait(1)
    inverse_planes(arrive.at[1], inv_z, mid, stacked, norm_scale)
    add_spectrum()

    def activate(index, carry):
        rows = pl.ds(pl.multiple_of(index * 16, 16), 16)
        pre_act = accum[rows, :]
        square = pre_act * pre_act
        half_gate = 0.5 + 0.5 * jnp.tanh(pre_act * (ROOT_CONST + ROOT_CONST * GELU_COEF * square))
        activated = pre_act * half_gate
        inner_slope = 2.0 * ROOT_CONST + 6.0 * ROOT_CONST * GELU_COEF * square
        gelu_slope = half_gate + activated * (1.0 - half_gate) * inner_slope
        out_block[rows, :] = activated.astype(jnp.bfloat16)
        grad_block[rows, :] = (cot[rows, :].astype(jnp.float32) * gelu_slope).astype(jnp.bfloat16)
        return carry

    lax.fori_loop(0, accum.shape[0] // 16, activate, 0)
    store_out = pltpu.make_async_copy(out_block, field_out.at[0, 0], load_sem.at[2])
    store_out.start()

    forward_planes(grad_block, table_y, fwd_z, mid, send.at[2])
    exchange_start(2)
    pointwise_into(grad_block, point_wide_t)
    exchange_wait(2)
    forward_modes(2, coef_grad)
    samples_start(1)
    lax.fori_loop(0, x_length, mix_back, 0, unroll=2)
    inverse_modes(3)
    exchange_start(3)
    exchange_wait(3)
    inverse_planes(arrive.at[3], inv_z, mid, stacked, norm_scale)
    add_spectrum()
    tail_block[...] = accum[...].astype(jnp.bfloat16)
    store_grad = pltpu.make_async_copy(tail_block, field_grad.at[0, 0], load_sem.at[3])
    store_grad.start()

    for turn in range(4):
        for hop in range(1, group_size):
            plane_copy(turn, hop).wait_send()
    for which in range(2):
        own_copy(which).wait()
        for hop in range(1, sample_count):
            sample_copy(which, hop).wait()
    store_out.wait()
    store_grad.wait()


def weight_kernel(
    left_hbm, right_hbm, first_hbm, second_hbm, weight_out, first_out, second_out,
    left_ref, right_ref, blocks, load_sem, pass_sem, block_sem,
):
    loads = [
        pltpu.make_async_copy(left_hbm, left_ref, load_sem.at[0]),
        pltpu.make_async_copy(right_hbm, right_ref, load_sem.at[1]),
    ]
    passes = [
        pltpu.make_async_copy(first_hbm, first_out, pass_sem.at[0]),
        pltpu.make_async_copy(second_hbm, second_out, pass_sem.at[1]),
    ]
    for copy in loads + passes:
        copy.start()
    for copy in loads:
        copy.wait()
    sample_count, x_length, mode_block = left_ref.shape[:3]
    depth = 2 * sample_count * 16
    groups = mode_block // 16
    own_lane = lax.broadcasted_iota(jnp.int32, (64, depth), 1) % 16

    def block_copy(index):
        return pltpu.make_async_copy(blocks.at[index], weight_out.at[index], block_sem.at[index])

    def step(residue, carry):
        for group in range(groups):
            index = residue * groups + group
            rows = slice(group * 16, group * 16 + 16)
            left = jnp.concatenate([left_ref[s, residue, rows, :] for s in range(sample_count)], 0)
            right = jnp.concatenate([right_ref[s, residue, rows, :] for s in range(sample_count)], 0)
            flipped = left.astype(jnp.float32).T
            flipped = jnp.concatenate([flipped[:64], flipped[64:]], axis=1)
            wide = right.astype(jnp.float32)
            stack = jnp.concatenate([wide, turned(wide)], 0).astype(jnp.bfloat16)
            kept = jnp.concatenate(
                [jnp.where(own_lane == mode, flipped, 0.0).astype(jnp.bfloat16) for mode in range(16)], 0
            )
            blocks[index] = dot32(kept, stack)
            block_copy(index).start()
        return carry

    lax.fori_loop(0, x_length, step, 0)

    def finish(index, carry):
        block_copy(index).wait()
        return carry

    lax.fori_loop(0, x_length * groups, finish, 0)
    for copy in passes:
        copy.wait()


def fused_device(field_in, cotangent, mode_weights, point_weights):
    y_count, last_width = field_in.shape[2:]
    channels = point_weights.shape[0]
    z_count = last_width // channels
    kx_count, mode_block = mode_weights.shape[:2]
    group_size = lax.axis_size("gx")
    sample_count = lax.axis_size("sa")
    x_length = group_size
    pair_width = 2 * channels
    norm_scale = 1.0 / math.sqrt(x_length * y_count * z_count)
    cos_x, sin_x = x_tables(kx_count, x_length)
    bf16, f32 = jnp.bfloat16, jnp.float32
    plane = (y_count, last_width)
    coef_shape = (x_length, mode_block, pair_width)
    anywhere = pl.BlockSpec(memory_space=pl.ANY)
    vmem = pl.BlockSpec(memory_space=pltpu.VMEM)
    field_out, field_grad, shared_in, shared_grad = pl.pallas_call(
        functools.partial(
            fused_kernel, cos_x, sin_x, norm_scale, group_size, sample_count, kx_count // x_length
        ),
        out_shape=[
            jax.ShapeDtypeStruct((1, 1) + plane, bf16),
            jax.ShapeDtypeStruct((1, 1) + plane, bf16),
            jax.ShapeDtypeStruct((sample_count,) + coef_shape, bf16),
            jax.ShapeDtypeStruct((sample_count,) + coef_shape, bf16),
        ],
        in_specs=[anywhere] * 3 + [vmem] * 6,
        out_specs=[anywhere] * 4,
        scratch_shapes=[
            pltpu.VMEM(plane, bf16),
            pltpu.VMEM(plane, bf16),
            pltpu.VMEM((kx_count, mode_block * channels, pair_width), bf16),
            pltpu.VMEM((x_length, mode_block * channels, pair_width), bf16),
            pltpu.VMEM((4,) + coef_shape, bf16),
            pltpu.VMEM((4,) + coef_shape, bf16),
            pltpu.VMEM(coef_shape, bf16),
            pltpu.VMEM(coef_shape, bf16),
            pltpu.VMEM(coef_shape, f32),
            pltpu.VMEM((KY, z_count, pair_width), f32),
            pltpu.VMEM((2 * KY, last_width), bf16),
            pltpu.VMEM(plane, f32),
            pltpu.VMEM(plane, bf16),
            pltpu.VMEM(plane, bf16),
            pltpu.VMEM(plane, bf16),
            pltpu.VMEM((256, 256), bf16),
            pltpu.VMEM((256, 256), bf16),
            pltpu.SemaphoreType.DMA((4,)),
            pltpu.SemaphoreType.DMA((kx_count,)),
            pltpu.SemaphoreType.DMA((4, group_size)),
            pltpu.SemaphoreType.DMA((4, group_size)),
            pltpu.SemaphoreType.DMA((2, sample_count)),
            pltpu.SemaphoreType.DMA((2, sample_count)),
            pltpu.SemaphoreType.DMA((2,)),
        ],
        compiler_params=pltpu.CompilerParams(
            collective_id=0, has_side_effects=True, vmem_limit_bytes=56 * 1024 * 1024
        ),
        name="fourier_layer",
    )(
        field_in, cotangent,
        mode_weights.reshape(kx_count, mode_block * channels, pair_width),
        point_weights, *host_tables(y_count, z_count, channels),
    )
    groups = mode_block // 16
    weight_grad, field_out, field_grad = pl.pallas_call(
        weight_kernel,
        out_shape=[
            jax.ShapeDtypeStruct((x_length * groups, 16 * channels, pair_width), f32),
            jax.ShapeDtypeStruct((1, 1) + plane, bf16),
            jax.ShapeDtypeStruct((1, 1) + plane, bf16),
        ],
        in_specs=[anywhere] * 4,
        out_specs=[anywhere] * 3,
        scratch_shapes=[
            pltpu.VMEM((sample_count,) + coef_shape, bf16),
            pltpu.VMEM((sample_count,) + coef_shape, bf16),
            pltpu.VMEM((x_length * groups, 16 * channels, pair_width), f32),
            pltpu.SemaphoreType.DMA((2,)),
            pltpu.SemaphoreType.DMA((2,)),
            pltpu.SemaphoreType.DMA((x_length * groups,)),
        ],
        compiler_params=pltpu.CompilerParams(vmem_limit_bytes=56 * 1024 * 1024),
        name="weight_gradient",
    )(shared_in, shared_grad, field_out, field_grad)
    return (
        field_out, field_grad,
        weight_grad.reshape(x_length, mode_block, channels, pair_width),
    )


def folds(field_in, mode_weights, point_weights):
    group_size, sample_count = lax.axis_size("gx"), lax.axis_size("sa")
    kx_count, mode_block, channels = mode_weights.shape[:3]
    planes, y_count, last_width = field_in.shape[1:]
    return (
        planes == 1
        and field_in.shape[0] == 1
        and channels == 64
        and last_width == 16 * channels
        and y_count % 16 == 0
        and mode_block % 16 == 0
        and 256 % mode_block == 0
        and group_size % 4 == 0
        and kx_count % group_size == 0
        and kx_count == sample_count * group_size
    )


def on_device(field_in, cotangent, mode_weights, point_weights):
    if folds(field_in, mode_weights, point_weights):
        return fused_device(field_in, cotangent, mode_weights, point_weights)
    local_field = field_in[0]
    planes, y_count, last_width = local_field.shape
    channels = point_weights.shape[0]
    z_count = last_width // channels
    kx_count = mode_weights.shape[0]
    x_length = planes * lax.axis_size("gx")
    norm_scale = 1.0 / math.sqrt(x_length * y_count * z_count)
    coeffs_in = forward_x(toward_modes(forward_yz(local_field, channels)), kx_count, norm_scale)
    mixed_modes = mix_forward(coeffs_in, mode_weights)
    spec_out = inverse_yz(
        toward_planes(inverse_x(mixed_modes, x_length)), y_count, z_count, norm_scale
    )
    pre_act = spec_out + pointwise(local_field, point_weights)
    activated, gelu_slope = gelu_parts(pre_act)
    out_grad = (cotangent[0].astype(jnp.float32) * gelu_slope).astype(jnp.bfloat16)
    coeffs_grad = forward_x(toward_modes(forward_yz(out_grad, channels)), kx_count, norm_scale)
    back_modes = mix_backward(coeffs_grad, mode_weights)
    spec_grad = inverse_yz(
        toward_planes(inverse_x(back_modes, x_length)), y_count, z_count, norm_scale
    )
    field_grad = (spec_grad + pointwise(out_grad, point_weights.T)).astype(jnp.bfloat16)
    shared_in, shared_grad = (
        lax.all_to_all(coeffs_in[None], "sa", split_axis=1, concat_axis=0, tiled=True),
        lax.all_to_all(coeffs_grad[None], "sa", split_axis=1, concat_axis=0, tiled=True),
    )
    weight_grad = sample_sum(shared_in, shared_grad)
    return (activated.astype(jnp.bfloat16)[None], field_grad[None], weight_grad)


def solution(mesh):
    in_specs = (
        P("sa", "gx", None, None),
        P("sa", "gx", None, None),
        P(None, "gx", None, None),
        P(),
    )
    out_specs = (P("sa", "gx", None, None), P("sa", "gx", None, None), P("sa", "gx", None, None))
    return jax.shard_map(
        on_device, mesh=mesh, in_specs=in_specs, out_specs=out_specs, check_vma=False
    )
```

```python
import functools
import math

import jax
import jax.numpy as jnp
import numpy as np
from jax import lax
from jax.experimental import pallas as pl
from jax.experimental.pallas import tpu as pltpu
from jax.sharding import PartitionSpec as P

KY = 32
KZ = 16


HIGHEST_PREC = lax.Precision.HIGHEST
GELU_COEF = 0.044715


def partner(block, axis, distance):
    count = lax.axis_size(axis)
    route = []
    for low in range(count):
        high = low | 1 << distance
        if high != low and high < count:
            route += [(low, high), (high, low)]
    return lax.ppermute(block, axis, route)


def angles(freq_count, grid_count):
    frequency = jnp.arange(freq_count, dtype=jnp.int32) - freq_count // 2
    places = jnp.arange(grid_count, dtype=jnp.int32)
    turn_index = jnp.mod(frequency[:, None] * places[None, :], grid_count)
    return turn_index.astype(jnp.float32) * (2.0 * math.pi / grid_count)


def gelu_parts(pre_act):
    root_const = math.sqrt(2.0 / math.pi)
    inner_arg = root_const * (pre_act + GELU_COEF * pre_act * pre_act * pre_act)
    tangent = jnp.tanh(inner_arg)
    activated = 0.5 * pre_act * (1.0 + tangent)
    gelu_slope = 0.5 * (1.0 + tangent) + 0.5 * pre_act * (1.0 - tangent * tangent) * root_const * (
        1.0 + 3.0 * GELU_COEF * pre_act * pre_act
    )
    return (activated, gelu_slope)


def along_z_forward(data_in, table_z):
    return jnp.einsum("pyzc,kz->pykc", data_in, table_z, precision=HIGHEST_PREC)


def along_z_inverse(data_in, table_z):
    return jnp.einsum("pykc,kz->pyzc", data_in, table_z, precision=HIGHEST_PREC)


def forward_yz(local_field, channels):
    planes, y_count, last_width = local_field.shape
    z_count = last_width // channels
    theta_y = angles(KY, y_count)
    table_y = jnp.concatenate([jnp.cos(theta_y), -jnp.sin(theta_y)], 0).astype(jnp.bfloat16)
    first_pass = jnp.einsum("fy,pyq->pfq", table_y, local_field, preferred_element_type=jnp.float32)
    first_pass = first_pass.reshape(planes, 2, KY, z_count, channels)
    theta_z = angles(KZ, z_count)
    cos_z = jnp.cos(theta_z)
    sin_z = jnp.sin(theta_z)
    real_in = first_pass[:, 0]
    imag_in = first_pass[:, 1]
    real_out = along_z_forward(real_in, cos_z) + along_z_forward(imag_in, sin_z)
    imag_out = along_z_forward(imag_in, cos_z) - along_z_forward(real_in, sin_z)
    mode_data = jnp.concatenate([real_out, imag_out], -1)
    return mode_data.reshape(planes, KY * KZ, 2 * channels).astype(jnp.bfloat16)


def forward_x(mode_data, kx_count, norm_scale):
    x_length, mode_block, pair_width = mode_data.shape
    channels = pair_width // 2
    theta_x = angles(kx_count, x_length)
    flat_data = mode_data.reshape(x_length, mode_block * pair_width)
    cos_part = jnp.dot(
        jnp.cos(theta_x).astype(jnp.bfloat16), flat_data, preferred_element_type=jnp.float32
    ).reshape(kx_count, mode_block, pair_width)
    sin_part = jnp.dot(
        jnp.sin(theta_x).astype(jnp.bfloat16), flat_data, preferred_element_type=jnp.float32
    ).reshape(kx_count, mode_block, pair_width)
    real_out = cos_part[..., :channels] + sin_part[..., channels:]
    imag_out = cos_part[..., channels:] - sin_part[..., :channels]
    return (jnp.concatenate([real_out, imag_out], -1) * norm_scale).astype(jnp.bfloat16)


def inverse_x(mixed_modes, x_length):
    kx_count, mode_block, pair_width = mixed_modes.shape
    channels = pair_width // 2
    theta_x = angles(kx_count, x_length).T
    flat_data = mixed_modes.reshape(kx_count, mode_block * pair_width)
    cos_part = jnp.dot(
        jnp.cos(theta_x).astype(jnp.bfloat16), flat_data, preferred_element_type=jnp.float32
    ).reshape(x_length, mode_block, pair_width)
    sin_part = jnp.dot(
        jnp.sin(theta_x).astype(jnp.bfloat16), flat_data, preferred_element_type=jnp.float32
    ).reshape(x_length, mode_block, pair_width)
    real_out = cos_part[..., :channels] - sin_part[..., channels:]
    imag_out = cos_part[..., channels:] + sin_part[..., :channels]
    return jnp.concatenate([real_out, imag_out], -1).astype(jnp.bfloat16)


def inverse_yz(planes_data, y_count, z_count, norm_scale):
    planes, mode_total, pair_width = planes_data.shape
    channels = pair_width // 2
    wide_data = planes_data.astype(jnp.float32).reshape(planes, KY, KZ, pair_width)
    real_in = wide_data[..., :channels]
    imag_in = wide_data[..., channels:]
    theta_z = angles(KZ, z_count)
    cos_z = jnp.cos(theta_z)
    sin_z = jnp.sin(theta_z)
    real_mid = along_z_inverse(real_in, cos_z) - along_z_inverse(imag_in, sin_z)
    imag_mid = along_z_inverse(imag_in, cos_z) + along_z_inverse(real_in, sin_z)
    stacked = jnp.concatenate([real_mid, imag_mid], 1).reshape(planes, 2 * KY, z_count * channels)
    theta_y = angles(KY, y_count)
    table_y = jnp.concatenate([jnp.cos(theta_y), -jnp.sin(theta_y)], 0)
    return jnp.einsum("pfq,fy->pyq", stacked, table_y, precision=HIGHEST_PREC) * norm_scale


def mix_forward(coeffs, weights_local):
    channels = weights_local.shape[2]
    real_part = jnp.einsum(
        "kmc,kmcp->kmp", coeffs[..., :channels], weights_local, preferred_element_type=jnp.float32
    )
    imag_part = jnp.einsum(
        "kmc,kmcp->kmp", coeffs[..., channels:], weights_local, preferred_element_type=jnp.float32
    )
    out_real = real_part[..., :channels] - imag_part[..., channels:]
    out_imag = real_part[..., channels:] + imag_part[..., :channels]
    return jnp.concatenate([out_real, out_imag], -1).astype(jnp.bfloat16)


def mix_backward(coeffs, weights_local):
    channels = weights_local.shape[2]
    swapped = jnp.concatenate([coeffs[..., channels:], -coeffs[..., :channels]], -1)
    first_half = jnp.einsum(
        "kmp,kmcp->kmc", coeffs, weights_local, preferred_element_type=jnp.float32
    )
    second_half = jnp.einsum(
        "kmp,kmcp->kmc", swapped, weights_local, preferred_element_type=jnp.float32
    )
    return jnp.concatenate([first_half, second_half], -1).astype(jnp.bfloat16)


def pointwise(local_field, weights_small):
    planes, y_count, last_width = local_field.shape
    channels = weights_small.shape[0]
    paired = jnp.kron(jnp.eye(2, dtype=weights_small.dtype), weights_small)
    cell_pairs = local_field.reshape(planes * y_count * last_width // (2 * channels), 2 * channels)
    return jnp.dot(cell_pairs, paired, preferred_element_type=jnp.float32).reshape(
        planes, y_count, last_width
    )


def sample_sum(left_side, right_side):
    channels = left_side.shape[-1] // 2
    left_real = left_side[..., :channels]
    left_imag = left_side[..., channels:]
    right_real = right_side[..., :channels]
    right_imag = right_side[..., channels:]

    def outer_sum(left_op, right_op):
        return jnp.einsum("skmc,skmo->kmco", left_op, right_op, preferred_element_type=jnp.float32)

    real_sum = outer_sum(left_real, right_real) + outer_sum(left_imag, right_imag)
    imag_sum = outer_sum(left_real, right_imag) - outer_sum(left_imag, right_real)
    return jnp.concatenate([real_sum, imag_sum], -1)


def partner_rounds(slot_buffer):
    slot_count = slot_buffer.shape[0]
    my_index = lax.axis_index("gx")
    for bit_pos in range(slot_count.bit_length() - 1):
        shaped = slot_buffer.reshape(
            (slot_count >> bit_pos + 1, 2, 1 << bit_pos) + slot_buffer.shape[1:]
        )
        lower_half = shaped[:, 0]
        upper_half = shaped[:, 1]
        own_bit = jnp.bitwise_and(jnp.right_shift(my_index, bit_pos), 1) == 1
        outgoing = jnp.where(own_bit, lower_half, upper_half)
        incoming = partner(outgoing, "gx", bit_pos)
        new_lower = jnp.where(own_bit, incoming, lower_half)
        new_upper = jnp.where(own_bit, upper_half, incoming)
        slot_buffer = jnp.stack([new_lower, new_upper], 1).reshape(slot_buffer.shape)
    return slot_buffer


def toward_modes(mode_data):
    planes, mode_total, pair_width = mode_data.shape
    group_size = lax.axis_size("gx")
    slot_buffer = mode_data.reshape(
        planes, group_size, mode_total // group_size, pair_width
    ).transpose(1, 0, 2, 3)
    return partner_rounds(slot_buffer).reshape(
        planes * group_size, mode_total // group_size, pair_width
    )


def toward_planes(back_planes):
    x_length, mode_block, pair_width = back_planes.shape
    group_size = lax.axis_size("gx")
    slot_buffer = back_planes.reshape(group_size, x_length // group_size, mode_block, pair_width)
    arrived = partner_rounds(slot_buffer)
    return arrived.transpose(1, 0, 2, 3).reshape(
        x_length // group_size, group_size * mode_block, pair_width
    )


MESH = pl.DeviceIdType.MESH
NT = (((1,), (1,)), ((), ()))
ROOT_CONST = math.sqrt(2.0 / math.pi)


def angles_host(freq_count, grid_count):
    frequency = np.arange(freq_count) - freq_count // 2
    turn_index = np.mod(frequency[:, None] * np.arange(grid_count)[None, :], grid_count)
    return turn_index.astype(np.float32) * np.float32(2.0 * math.pi / grid_count)


def host_tables(y_count, z_count, channels):
    theta_y = angles_host(KY, y_count)
    table_y = np.concatenate([np.cos(theta_y), -np.sin(theta_y)], 0)
    theta_z = angles_host(KZ, z_count)
    eye = np.eye(16, dtype=np.float32)
    fwd_z = np.concatenate([np.kron(eye, np.cos(theta_z)), np.kron(eye, np.sin(theta_z))], 0)
    inv_z = np.concatenate([np.kron(eye, np.cos(theta_z).T), np.kron(eye, np.sin(theta_z).T)], 0)
    spread = np.tile(np.eye(channels, dtype=np.float32), (256 // channels, 1))
    return [jnp.asarray(t, jnp.bfloat16) for t in (table_y, table_y.T, fwd_z, inv_z, spread)]


def x_tables(kx_count, x_length):
    theta_x = angles_host(kx_count, x_length)[:x_length]
    rounded = [np.asarray(f(theta_x), jnp.bfloat16).astype(np.float32) for f in (np.cos, np.sin)]
    return [np.where(np.abs(t) < 1e-5, 0.0, t) for t in rounded]


def dot32(left, right):
    return jnp.dot(left, right, preferred_element_type=jnp.float32)


def lanes_low(shape):
    return lax.broadcasted_iota(jnp.int32, shape, 1) < 64


def swap(block):
    return pltpu.roll(block, 64, 1)


def turned(block):
    swapped = swap(block)
    return jnp.where(lanes_low(block.shape), swapped, -swapped)


def x_pass(read, write, cos_t, sin_t, mode_block):
    length = cos_t.shape[0]
    half = length // 2

    def step(index, carry):
        rows = pl.ds(pl.multiple_of(index * 16, 16), 16)
        data = [read(j, rows) for j in range(length)]
        folded = [
            [data[j] + data[j + half] for j in range(half)],
            [data[j] - data[j + half] for j in range(half)],
        ]
        spun = [[turned(block) for block in group] for group in folded]
        for k in range(length):
            total = None
            for j in range(half):
                for coef, block in ((cos_t[k, j], folded[k % 2][j]), (sin_t[k, j], spun[k % 2][j])):
                    coef = float(coef)
                    if coef == 0.0:
                        continue
                    term = block if coef == 1.0 else -block if coef == -1.0 else block * coef
                    total = term if total is None else total + term
            write(k, rows, total)
        return carry

    lax.fori_loop(0, mode_block // 16, step, 0)


def forward_planes(source, table_y, fwd_z, mid, send):
    first_pass = dot32(table_y[...], source[...])
    low = lanes_low((KY, 128))
    for pair in range(first_pass.shape[1] // 128):
        real_in = first_pass[:KY, pair * 128 : pair * 128 + 128]
        imag_in = first_pass[KY:, pair * 128 : pair * 128 + 128]
        mid[:, 2 * pair, :] = jnp.where(low, real_in, swap(imag_in))
        mid[:, 2 * pair + 1, :] = jnp.where(low, swap(real_in), imag_in)
    group_size, mode_block, pair_width = send.shape
    per_half = 256 // mode_block
    for half in range(2):
        block = mid[16 * half : 16 * half + 16].reshape(256, pair_width).astype(jnp.bfloat16)
        both = dot32(fwd_z[...], block)
        data = both[:256] + turned(both[256:])
        send[half * per_half : (half + 1) * per_half] = data.reshape(
            per_half, mode_block, pair_width
        ).astype(jnp.bfloat16)


def inverse_planes(arrived, inv_z, mid, stacked, norm_scale):
    group_size, mode_block, pair_width = arrived.shape
    per_half = 256 // mode_block
    for half in range(2):
        block = arrived[half * per_half : (half + 1) * per_half].reshape(256, pair_width)
        both = dot32(inv_z[...], block)
        mid[16 * half : 16 * half + 16] = (
            (both[:256] - turned(both[256:])) * norm_scale
        ).reshape(16, 16, pair_width)
    low = lanes_low((KY, 128))
    for pair in range(stacked.shape[1] // 128):
        even = mid[:, 2 * pair, :]
        odd = mid[:, 2 * pair + 1, :]
        columns = slice(pair * 128, pair * 128 + 128)
        stacked[:KY, columns] = jnp.where(low, even, swap(odd)).astype(jnp.bfloat16)
        stacked[KY:, columns] = jnp.where(low, swap(even), odd).astype(jnp.bfloat16)


def fused_kernel(
    cos_x, sin_x, norm_scale, group_size, sample_count, alias_count,
    field_hbm, cot_hbm, weights_hbm, point_ref, table_y, table_y_t, fwd_z, inv_z, spread,
    field_out, field_grad, shared_in, shared_grad,
    field, cot, weights, folded, send, arrive, coef_in, coef_grad, mixed, mid, stacked, accum,
    out_block, grad_block, tail_block, point_wide, point_wide_t,
    load_sem, weight_sem, send_sem, recv_sem, sa_send, sa_recv, own_sem,
):
    me = lax.axis_index("gx")
    mine = lax.axis_index("sa")
    x_length = group_size
    mode_block = send.shape[2]
    groups = mode_block // 16

    load_field = pltpu.make_async_copy(field_hbm.at[0, 0], field, load_sem.at[0])
    load_cot = pltpu.make_async_copy(cot_hbm.at[0, 0], cot, load_sem.at[1])
    load_field.start()
    load_cot.start()

    def weight_copy(kx):
        return pltpu.make_async_copy(weights_hbm.at[kx], weights.at[kx], weight_sem.at[kx])

    for residue in range(x_length):
        for alias in range(alias_count):
            weight_copy(residue + x_length * alias).start()

    barrier = pltpu.get_barrier_semaphore()
    for hop in range(1, group_size):
        pl.semaphore_signal(
            barrier, inc=1, device_id={"gx": lax.rem(me + hop, group_size)}, device_id_type=MESH
        )
    for hop in range(1, sample_count):
        pl.semaphore_signal(
            barrier, inc=1, device_id={"sa": lax.rem(mine + hop, sample_count)}, device_id_type=MESH
        )

    def plane_copy(turn, hop):
        target = lax.rem(me + hop, group_size)
        return pltpu.make_async_remote_copy(
            src_ref=send.at[turn, target],
            dst_ref=arrive.at[turn, me],
            send_sem=send_sem.at[turn, hop],
            recv_sem=recv_sem.at[turn, hop],
            device_id={"gx": target},
            device_id_type=MESH,
        )

    def exchange_start(turn):
        for hop in range(1, group_size):
            plane_copy(turn, hop).start()
        arrive[turn, me] = send[turn, me]

    def exchange_wait(turn):
        for hop in range(1, group_size):
            plane_copy(turn, hop).wait_recv()

    def sample_copy(which, hop):
        source, target = ((coef_in, shared_in), (coef_grad, shared_grad))[which]
        return pltpu.make_async_remote_copy(
            src_ref=source,
            dst_ref=target.at[mine],
            send_sem=sa_send.at[which, hop],
            recv_sem=sa_recv.at[which, hop],
            device_id={"sa": lax.rem(mine + hop, sample_count)},
            device_id_type=MESH,
        )

    def own_copy(which):
        source, target = ((coef_in, shared_in), (coef_grad, shared_grad))[which]
        return pltpu.make_async_copy(source, target.at[mine], own_sem.at[which])

    def samples_start(which):
        for hop in range(1, sample_count):
            sample_copy(which, hop).start()
        own_copy(which).start()

    def forward_modes(turn, coef):
        def read(j, rows):
            return arrive[turn, j, rows, :].astype(jnp.float32)

        def write(k, rows, value):
            coef[k, rows, :] = (value * norm_scale).astype(jnp.bfloat16)

        x_pass(read, write, cos_x, sin_x, mode_block)

    def inverse_modes(turn):
        def read(j, rows):
            return mixed[j, rows, :]

        def write(k, rows, value):
            send[turn, k, rows, :] = value.astype(jnp.bfloat16)

        x_pass(read, write, cos_x.T, -sin_x.T, mode_block)

    def wait_weights(residue):
        for alias in range(alias_count):
            weight_copy(residue + x_length * alias).wait()

    def fold_rows(pair, start):
        for part in range(1024 // 128):
            rows = pl.ds(pl.multiple_of(start + part * 128, 128), 128)
            for side in range(2):
                residue = 2 * pair + side
                total = weights[residue, rows, :].astype(jnp.float32)
                for alias in range(1, alias_count):
                    total = total + weights[residue + x_length * alias, rows, :].astype(jnp.float32)
                folded[pair, rows, side * 128 : side * 128 + 128] = total.astype(jnp.bfloat16)

    row_index = lax.broadcasted_iota(jnp.int32, (8, 128), 0)
    low16 = lanes_low((16, 128))
    own_half = (row_index + lax.broadcasted_iota(jnp.int32, (8, 128), 1) // 64) % 2 == 0
    own_pair = [row_index // 2 == pair for pair in range(4)]

    def diagonal(block):
        empty = jnp.zeros((8, 128), jnp.float32)
        columns = []
        for part in range(8):
            half = block[:8] if part < 4 else block[8:]
            kept = jnp.where(own_pair[part % 4], jnp.where(own_half, half, 0.0), 0.0)
            stacked_rows = [kept, empty] if part < 4 else [empty, kept]
            columns.append(jnp.concatenate(stacked_rows, 0).astype(jnp.bfloat16))
        return jnp.concatenate(columns, 1)

    def gathered(block):
        halves = []
        for half in range(2):
            rows = slice(half * 8, half * 8 + 8)
            kept = block[rows, half * 512 : half * 512 + 128]
            for part in range(1, 4):
                start = half * 512 + part * 128
                kept = jnp.where(own_pair[part], block[rows, start : start + 128], kept)
            halves.append(jnp.where(own_half, kept, 0.0))
        total = jnp.concatenate(halves, 0)
        return total + swap(total)

    def mix_in_group(pair, group):
        rows = slice(group * 16, group * 16 + 16)
        parts = []
        for side in range(2):
            coef = coef_in[2 * pair + side, rows, :].astype(jnp.float32)
            other = swap(coef)
            parts += [diagonal(jnp.where(low16, coef, other)), diagonal(jnp.where(low16, other, coef))]
        product = dot32(
            jnp.concatenate(parts, 0), folded[pair, group * 1024 : group * 1024 + 1024, :]
        )
        for side in range(2):
            own = product[side * 32 : side * 32 + 32, side * 128 : side * 128 + 128]
            mixed[2 * pair + side, rows, :] = own[:16] - turned(own[16:])

    def wait_pair(pair):
        wait_weights(2 * pair)
        wait_weights(2 * pair + 1)

    def fold_first(pair):
        wait_pair(pair)

        def step(index, inner):
            fold_rows(pair, index * 1024)
            return inner

        lax.fori_loop(0, groups, step, 0)

    def mix_and_fold(pair, carry):
        wait_pair(pair)
        for group in range(groups):
            mix_in_group(pair - 1, group)
            fold_rows(pair, group * 1024)
        return carry

    def mix_back(pair, carry):
        empty = jnp.zeros((32, 128), jnp.bfloat16)
        for group in range(groups):
            rows = slice(group * 16, group * 16 + 16)
            parts = []
            for side in range(2):
                coef = coef_grad[2 * pair + side, rows, :].astype(jnp.float32)
                both = jnp.concatenate([coef, turned(coef)], 0).astype(jnp.bfloat16)
                parts.append(jnp.concatenate([both, empty] if side == 0 else [empty, both], 1))
            product = lax.dot_general(
                jnp.concatenate(parts, 0), folded[pair, group * 1024 : group * 1024 + 1024, :],
                NT, preferred_element_type=jnp.float32,
            )
            for side in range(2):
                start = side * 32
                mixed[2 * pair + side, rows, :] = jnp.where(
                    low16, gathered(product[start : start + 16]),
                    gathered(product[start + 16 : start + 32]),
                )
        return carry

    def pointwise_into(source, wide):
        for part in range(accum.shape[1] // 256):
            columns = slice(part * 256, part * 256 + 256)
            accum[:, columns] = dot32(source[:, columns], wide[...])

    def add_spectrum():
        for part in range(accum.shape[1] // 256):
            columns = slice(part * 256, part * 256 + 256)
            accum[:, columns] += dot32(table_y_t[...], stacked[:, columns])

    load_field.wait()
    forward_planes(field, table_y, fwd_z, mid, send.at[0])
    pl.semaphore_wait(barrier, group_size + sample_count - 2)
    exchange_start(0)

    same_block = (
        lax.broadcasted_iota(jnp.int32, (256, 256), 0) // 64
        == lax.broadcasted_iota(jnp.int32, (256, 256), 1) // 64
    )

    def widened(block):
        wide = lax.dot_general(block.astype(jnp.bfloat16), spread[...], NT, preferred_element_type=jnp.float32)
        return jnp.where(same_block, wide, 0.0).astype(jnp.bfloat16)

    point_wide[...] = widened(dot32(spread[...], point_ref[...]))
    point_wide_t[...] = widened(
        lax.dot_general(spread[...], point_ref[...], NT, preferred_element_type=jnp.float32)
    )
    pointwise_into(field, point_wide)

    fold_first(0)
    exchange_wait(0)
    forward_modes(0, coef_in)
    samples_start(0)
    lax.fori_loop(1, x_length // 2, mix_and_fold, 0)
    for group in range(groups):
        mix_in_group(x_length // 2 - 1, group)
    inverse_modes(1)
    exchange_start(1)
    load_cot.wait()
    exchange_wait(1)
    inverse_planes(arrive.at[1], inv_z, mid, stacked, norm_scale)
    add_spectrum()

    def activate(index, carry):
        rows = pl.ds(pl.multiple_of(index * 16, 16), 16)
        pre_act = accum[rows, :]
        square = pre_act * pre_act
        half_gate = 0.5 + 0.5 * jnp.tanh(pre_act * (ROOT_CONST + ROOT_CONST * GELU_COEF * square))
        activated = pre_act * half_gate
        inner_slope = 2.0 * ROOT_CONST + 6.0 * ROOT_CONST * GELU_COEF * square
        gelu_slope = half_gate + activated * (1.0 - half_gate) * inner_slope
        out_block[rows, :] = activated.astype(jnp.bfloat16)
        grad_block[rows, :] = (cot[rows, :].astype(jnp.float32) * gelu_slope).astype(jnp.bfloat16)
        return carry

    lax.fori_loop(0, accum.shape[0] // 16, activate, 0)
    store_out = pltpu.make_async_copy(out_block, field_out.at[0, 0], load_sem.at[2])
    store_out.start()

    forward_planes(grad_block, table_y, fwd_z, mid, send.at[2])
    exchange_start(2)
    pointwise_into(grad_block, point_wide_t)
    exchange_wait(2)
    forward_modes(2, coef_grad)
    samples_start(1)
    lax.fori_loop(0, x_length // 2, mix_back, 0)
    inverse_modes(3)
    exchange_start(3)
    exchange_wait(3)
    inverse_planes(arrive.at[3], inv_z, mid, stacked, norm_scale)
    add_spectrum()
    tail_block[...] = accum[...].astype(jnp.bfloat16)
    store_grad = pltpu.make_async_copy(tail_block, field_grad.at[0, 0], load_sem.at[3])
    store_grad.start()

    for turn in range(4):
        for hop in range(1, group_size):
            plane_copy(turn, hop).wait_send()
    for which in range(2):
        own_copy(which).wait()
        for hop in range(1, sample_count):
            sample_copy(which, hop).wait()
    store_out.wait()
    store_grad.wait()


def weight_kernel(
    left_hbm, right_hbm, first_hbm, second_hbm, weight_out, first_out, second_out,
    left_ref, right_ref, first_ref, second_ref, blocks, load_sem, pass_sem, block_sem,
):
    loads = [
        pltpu.make_async_copy(left_hbm, left_ref, load_sem.at[0]),
        pltpu.make_async_copy(right_hbm, right_ref, load_sem.at[1]),
    ]
    fetches = [
        pltpu.make_async_copy(first_hbm, first_ref, load_sem.at[2]),
        pltpu.make_async_copy(second_hbm, second_ref, load_sem.at[3]),
    ]
    passes = [
        pltpu.make_async_copy(first_ref, first_out, pass_sem.at[0]),
        pltpu.make_async_copy(second_ref, second_out, pass_sem.at[1]),
    ]
    for copy in loads + fetches:
        copy.start()
    for copy in loads:
        copy.wait()
    sample_count, x_length, mode_block = left_ref.shape[:3]
    depth = 2 * sample_count * 16
    groups = mode_block // 16
    own_lane = lax.broadcasted_iota(jnp.int32, (64, depth), 1) % 16

    def block_copy(index):
        return pltpu.make_async_copy(blocks.at[index], weight_out.at[index], block_sem.at[index])

    def step(residue, carry):
        for group in range(groups):
            index = residue * groups + group
            rows = slice(group * 16, group * 16 + 16)
            left = jnp.concatenate([left_ref[s, residue, rows, :] for s in range(sample_count)], 0)
            right = jnp.concatenate([right_ref[s, residue, rows, :] for s in range(sample_count)], 0)
            flipped = left.astype(jnp.float32).T
            flipped = jnp.concatenate([flipped[:64], flipped[64:]], axis=1)
            wide = right.astype(jnp.float32)
            stack = jnp.concatenate([wide, turned(wide)], 0).astype(jnp.bfloat16)
            kept = jnp.concatenate(
                [jnp.where(own_lane == mode, flipped, 0.0).astype(jnp.bfloat16) for mode in range(16)], 0
            )
            blocks[index] = dot32(kept, stack)
            block_copy(index).start()
        return carry

    step(0, 0)
    for fetch, copy in zip(fetches, passes):
        fetch.wait()
        copy.start()
    lax.fori_loop(1, x_length, step, 0)

    def finish(index, carry):
        block_copy(index).wait()
        return carry

    lax.fori_loop(0, x_length * groups, finish, 0)
    for copy in passes:
        copy.wait()


def fused_device(field_in, cotangent, mode_weights, point_weights):
    y_count, last_width = field_in.shape[2:]
    channels = point_weights.shape[0]
    z_count = last_width // channels
    kx_count, mode_block = mode_weights.shape[:2]
    group_size = lax.axis_size("gx")
    sample_count = lax.axis_size("sa")
    x_length = group_size
    pair_width = 2 * channels
    norm_scale = 1.0 / math.sqrt(x_length * y_count * z_count)
    cos_x, sin_x = x_tables(kx_count, x_length)
    bf16, f32 = jnp.bfloat16, jnp.float32
    plane = (y_count, last_width)
    coef_shape = (x_length, mode_block, pair_width)
    anywhere = pl.BlockSpec(memory_space=pl.ANY)
    vmem = pl.BlockSpec(memory_space=pltpu.VMEM)
    field_out, field_grad, shared_in, shared_grad = pl.pallas_call(
        functools.partial(
            fused_kernel, cos_x, sin_x, norm_scale, group_size, sample_count, kx_count // x_length
        ),
        out_shape=[
            jax.ShapeDtypeStruct((1, 1) + plane, bf16),
            jax.ShapeDtypeStruct((1, 1) + plane, bf16),
            jax.ShapeDtypeStruct((sample_count,) + coef_shape, bf16),
            jax.ShapeDtypeStruct((sample_count,) + coef_shape, bf16),
        ],
        in_specs=[anywhere] * 3 + [vmem] * 6,
        out_specs=[anywhere] * 4,
        scratch_shapes=[
            pltpu.VMEM(plane, bf16),
            pltpu.VMEM(plane, bf16),
            pltpu.VMEM((kx_count, mode_block * channels, pair_width), bf16),
            pltpu.VMEM((x_length // 2, mode_block * channels, 2 * pair_width), bf16),
            pltpu.VMEM((4,) + coef_shape, bf16),
            pltpu.VMEM((4,) + coef_shape, bf16),
            pltpu.VMEM(coef_shape, bf16),
            pltpu.VMEM(coef_shape, bf16),
            pltpu.VMEM(coef_shape, f32),
            pltpu.VMEM((KY, z_count, pair_width), f32),
            pltpu.VMEM((2 * KY, last_width), bf16),
            pltpu.VMEM(plane, f32),
            pltpu.VMEM(plane, bf16),
            pltpu.VMEM(plane, bf16),
            pltpu.VMEM(plane, bf16),
            pltpu.VMEM((256, 256), bf16),
            pltpu.VMEM((256, 256), bf16),
            pltpu.SemaphoreType.DMA((4,)),
            pltpu.SemaphoreType.DMA((kx_count,)),
            pltpu.SemaphoreType.DMA((4, group_size)),
            pltpu.SemaphoreType.DMA((4, group_size)),
            pltpu.SemaphoreType.DMA((2, sample_count)),
            pltpu.SemaphoreType.DMA((2, sample_count)),
            pltpu.SemaphoreType.DMA((2,)),
        ],
        compiler_params=pltpu.CompilerParams(
            collective_id=0, has_side_effects=True, vmem_limit_bytes=56 * 1024 * 1024
        ),
        name="fourier_layer",
    )(
        field_in, cotangent,
        mode_weights.reshape(kx_count, mode_block * channels, pair_width),
        point_weights, *host_tables(y_count, z_count, channels),
    )
    groups = mode_block // 16
    weight_grad, field_out, field_grad = pl.pallas_call(
        weight_kernel,
        out_shape=[
            jax.ShapeDtypeStruct((x_length * groups, 16 * channels, pair_width), f32),
            jax.ShapeDtypeStruct((1, 1) + plane, bf16),
            jax.ShapeDtypeStruct((1, 1) + plane, bf16),
        ],
        in_specs=[anywhere] * 4,
        out_specs=[anywhere] * 3,
        scratch_shapes=[
            pltpu.VMEM((sample_count,) + coef_shape, bf16),
            pltpu.VMEM((sample_count,) + coef_shape, bf16),
            pltpu.VMEM((1, 1) + plane, bf16),
            pltpu.VMEM((1, 1) + plane, bf16),
            pltpu.VMEM((x_length * groups, 16 * channels, pair_width), f32),
            pltpu.SemaphoreType.DMA((4,)),
            pltpu.SemaphoreType.DMA((2,)),
            pltpu.SemaphoreType.DMA((x_length * groups,)),
        ],
        compiler_params=pltpu.CompilerParams(vmem_limit_bytes=56 * 1024 * 1024),
        name="weight_gradient",
    )(shared_in, shared_grad, field_out, field_grad)
    return (
        field_out, field_grad,
        weight_grad.reshape(x_length, mode_block, channels, pair_width),
    )


def folds(field_in, mode_weights, point_weights):
    group_size, sample_count = lax.axis_size("gx"), lax.axis_size("sa")
    kx_count, mode_block, channels = mode_weights.shape[:3]
    planes, y_count, last_width = field_in.shape[1:]
    return (
        planes == 1
        and field_in.shape[0] == 1
        and channels == 64
        and last_width == 16 * channels
        and y_count % 16 == 0
        and group_size % 4 == 0
        and mode_block == 64
        and kx_count % group_size == 0
        and kx_count == sample_count * group_size
    )


def on_device(field_in, cotangent, mode_weights, point_weights):
    if folds(field_in, mode_weights, point_weights):
        return fused_device(field_in, cotangent, mode_weights, point_weights)
    local_field = field_in[0]
    planes, y_count, last_width = local_field.shape
    channels = point_weights.shape[0]
    z_count = last_width // channels
    kx_count = mode_weights.shape[0]
    x_length = planes * lax.axis_size("gx")
    norm_scale = 1.0 / math.sqrt(x_length * y_count * z_count)
    coeffs_in = forward_x(toward_modes(forward_yz(local_field, channels)), kx_count, norm_scale)
    mixed_modes = mix_forward(coeffs_in, mode_weights)
    spec_out = inverse_yz(
        toward_planes(inverse_x(mixed_modes, x_length)), y_count, z_count, norm_scale
    )
    pre_act = spec_out + pointwise(local_field, point_weights)
    activated, gelu_slope = gelu_parts(pre_act)
    out_grad = (cotangent[0].astype(jnp.float32) * gelu_slope).astype(jnp.bfloat16)
    coeffs_grad = forward_x(toward_modes(forward_yz(out_grad, channels)), kx_count, norm_scale)
    back_modes = mix_backward(coeffs_grad, mode_weights)
    spec_grad = inverse_yz(
        toward_planes(inverse_x(back_modes, x_length)), y_count, z_count, norm_scale
    )
    field_grad = (spec_grad + pointwise(out_grad, point_weights.T)).astype(jnp.bfloat16)
    shared_in, shared_grad = (
        lax.all_to_all(coeffs_in[None], "sa", split_axis=1, concat_axis=0, tiled=True),
        lax.all_to_all(coeffs_grad[None], "sa", split_axis=1, concat_axis=0, tiled=True),
    )
    weight_grad = sample_sum(shared_in, shared_grad)
    return (activated.astype(jnp.bfloat16)[None], field_grad[None], weight_grad)


def solution(mesh):
    in_specs = (
        P("sa", "gx", None, None),
        P("sa", "gx", None, None),
        P(None, "gx", None, None),
        P(),
    )
    out_specs = (P("sa", "gx", None, None), P("sa", "gx", None, None), P("sa", "gx", None, None))
    return jax.shard_map(
        on_device, mesh=mesh, in_specs=in_specs, out_specs=out_specs, check_vma=False
    )
```

```python
import functools
import math

import jax
import jax.numpy as jnp
import numpy as np
from jax import lax
from jax.experimental import pallas as pl
from jax.experimental.pallas import tpu as pltpu
from jax.sharding import PartitionSpec as P

KY = 32
KZ = 16


HIGHEST_PREC = lax.Precision.HIGHEST
GELU_COEF = 0.044715


def partner(block, axis, distance):
    count = lax.axis_size(axis)
    route = []
    for low in range(count):
        high = low | 1 << distance
        if high != low and high < count:
            route += [(low, high), (high, low)]
    return lax.ppermute(block, axis, route)


def angles(freq_count, grid_count):
    frequency = jnp.arange(freq_count, dtype=jnp.int32) - freq_count // 2
    places = jnp.arange(grid_count, dtype=jnp.int32)
    turn_index = jnp.mod(frequency[:, None] * places[None, :], grid_count)
    return turn_index.astype(jnp.float32) * (2.0 * math.pi / grid_count)


def gelu_parts(pre_act):
    root_const = math.sqrt(2.0 / math.pi)
    inner_arg = root_const * (pre_act + GELU_COEF * pre_act * pre_act * pre_act)
    tangent = jnp.tanh(inner_arg)
    activated = 0.5 * pre_act * (1.0 + tangent)
    gelu_slope = 0.5 * (1.0 + tangent) + 0.5 * pre_act * (1.0 - tangent * tangent) * root_const * (
        1.0 + 3.0 * GELU_COEF * pre_act * pre_act
    )
    return (activated, gelu_slope)


def along_z_forward(data_in, table_z):
    return jnp.einsum("pyzc,kz->pykc", data_in, table_z, precision=HIGHEST_PREC)


def along_z_inverse(data_in, table_z):
    return jnp.einsum("pykc,kz->pyzc", data_in, table_z, precision=HIGHEST_PREC)


def forward_yz(local_field, channels):
    planes, y_count, last_width = local_field.shape
    z_count = last_width // channels
    theta_y = angles(KY, y_count)
    table_y = jnp.concatenate([jnp.cos(theta_y), -jnp.sin(theta_y)], 0).astype(jnp.bfloat16)
    first_pass = jnp.einsum("fy,pyq->pfq", table_y, local_field, preferred_element_type=jnp.float32)
    first_pass = first_pass.reshape(planes, 2, KY, z_count, channels)
    theta_z = angles(KZ, z_count)
    cos_z = jnp.cos(theta_z)
    sin_z = jnp.sin(theta_z)
    real_in = first_pass[:, 0]
    imag_in = first_pass[:, 1]
    real_out = along_z_forward(real_in, cos_z) + along_z_forward(imag_in, sin_z)
    imag_out = along_z_forward(imag_in, cos_z) - along_z_forward(real_in, sin_z)
    mode_data = jnp.concatenate([real_out, imag_out], -1)
    return mode_data.reshape(planes, KY * KZ, 2 * channels).astype(jnp.bfloat16)


def forward_x(mode_data, kx_count, norm_scale):
    x_length, mode_block, pair_width = mode_data.shape
    channels = pair_width // 2
    theta_x = angles(kx_count, x_length)
    flat_data = mode_data.reshape(x_length, mode_block * pair_width)
    cos_part = jnp.dot(
        jnp.cos(theta_x).astype(jnp.bfloat16), flat_data, preferred_element_type=jnp.float32
    ).reshape(kx_count, mode_block, pair_width)
    sin_part = jnp.dot(
        jnp.sin(theta_x).astype(jnp.bfloat16), flat_data, preferred_element_type=jnp.float32
    ).reshape(kx_count, mode_block, pair_width)
    real_out = cos_part[..., :channels] + sin_part[..., channels:]
    imag_out = cos_part[..., channels:] - sin_part[..., :channels]
    return (jnp.concatenate([real_out, imag_out], -1) * norm_scale).astype(jnp.bfloat16)


def inverse_x(mixed_modes, x_length):
    kx_count, mode_block, pair_width = mixed_modes.shape
    channels = pair_width // 2
    theta_x = angles(kx_count, x_length).T
    flat_data = mixed_modes.reshape(kx_count, mode_block * pair_width)
    cos_part = jnp.dot(
        jnp.cos(theta_x).astype(jnp.bfloat16), flat_data, preferred_element_type=jnp.float32
    ).reshape(x_length, mode_block, pair_width)
    sin_part = jnp.dot(
        jnp.sin(theta_x).astype(jnp.bfloat16), flat_data, preferred_element_type=jnp.float32
    ).reshape(x_length, mode_block, pair_width)
    real_out = cos_part[..., :channels] - sin_part[..., channels:]
    imag_out = cos_part[..., channels:] + sin_part[..., :channels]
    return jnp.concatenate([real_out, imag_out], -1).astype(jnp.bfloat16)


def inverse_yz(planes_data, y_count, z_count, norm_scale):
    planes, mode_total, pair_width = planes_data.shape
    channels = pair_width // 2
    wide_data = planes_data.astype(jnp.float32).reshape(planes, KY, KZ, pair_width)
    real_in = wide_data[..., :channels]
    imag_in = wide_data[..., channels:]
    theta_z = angles(KZ, z_count)
    cos_z = jnp.cos(theta_z)
    sin_z = jnp.sin(theta_z)
    real_mid = along_z_inverse(real_in, cos_z) - along_z_inverse(imag_in, sin_z)
    imag_mid = along_z_inverse(imag_in, cos_z) + along_z_inverse(real_in, sin_z)
    stacked = jnp.concatenate([real_mid, imag_mid], 1).reshape(planes, 2 * KY, z_count * channels)
    theta_y = angles(KY, y_count)
    table_y = jnp.concatenate([jnp.cos(theta_y), -jnp.sin(theta_y)], 0)
    return jnp.einsum("pfq,fy->pyq", stacked, table_y, precision=HIGHEST_PREC) * norm_scale


def mix_forward(coeffs, weights_local):
    channels = weights_local.shape[2]
    real_part = jnp.einsum(
        "kmc,kmcp->kmp", coeffs[..., :channels], weights_local, preferred_element_type=jnp.float32
    )
    imag_part = jnp.einsum(
        "kmc,kmcp->kmp", coeffs[..., channels:], weights_local, preferred_element_type=jnp.float32
    )
    out_real = real_part[..., :channels] - imag_part[..., channels:]
    out_imag = real_part[..., channels:] + imag_part[..., :channels]
    return jnp.concatenate([out_real, out_imag], -1).astype(jnp.bfloat16)


def mix_backward(coeffs, weights_local):
    channels = weights_local.shape[2]
    swapped = jnp.concatenate([coeffs[..., channels:], -coeffs[..., :channels]], -1)
    first_half = jnp.einsum(
        "kmp,kmcp->kmc", coeffs, weights_local, preferred_element_type=jnp.float32
    )
    second_half = jnp.einsum(
        "kmp,kmcp->kmc", swapped, weights_local, preferred_element_type=jnp.float32
    )
    return jnp.concatenate([first_half, second_half], -1).astype(jnp.bfloat16)


def pointwise(local_field, weights_small):
    planes, y_count, last_width = local_field.shape
    channels = weights_small.shape[0]
    paired = jnp.kron(jnp.eye(2, dtype=weights_small.dtype), weights_small)
    cell_pairs = local_field.reshape(planes * y_count * last_width // (2 * channels), 2 * channels)
    return jnp.dot(cell_pairs, paired, preferred_element_type=jnp.float32).reshape(
        planes, y_count, last_width
    )


def sample_sum(left_side, right_side):
    channels = left_side.shape[-1] // 2
    left_real = left_side[..., :channels]
    left_imag = left_side[..., channels:]
    right_real = right_side[..., :channels]
    right_imag = right_side[..., channels:]

    def outer_sum(left_op, right_op):
        return jnp.einsum("skmc,skmo->kmco", left_op, right_op, preferred_element_type=jnp.float32)

    real_sum = outer_sum(left_real, right_real) + outer_sum(left_imag, right_imag)
    imag_sum = outer_sum(left_real, right_imag) - outer_sum(left_imag, right_real)
    return jnp.concatenate([real_sum, imag_sum], -1)


def partner_rounds(slot_buffer):
    slot_count = slot_buffer.shape[0]
    my_index = lax.axis_index("gx")
    for bit_pos in range(slot_count.bit_length() - 1):
        shaped = slot_buffer.reshape(
            (slot_count >> bit_pos + 1, 2, 1 << bit_pos) + slot_buffer.shape[1:]
        )
        lower_half = shaped[:, 0]
        upper_half = shaped[:, 1]
        own_bit = jnp.bitwise_and(jnp.right_shift(my_index, bit_pos), 1) == 1
        outgoing = jnp.where(own_bit, lower_half, upper_half)
        incoming = partner(outgoing, "gx", bit_pos)
        new_lower = jnp.where(own_bit, incoming, lower_half)
        new_upper = jnp.where(own_bit, upper_half, incoming)
        slot_buffer = jnp.stack([new_lower, new_upper], 1).reshape(slot_buffer.shape)
    return slot_buffer


def toward_modes(mode_data):
    planes, mode_total, pair_width = mode_data.shape
    group_size = lax.axis_size("gx")
    slot_buffer = mode_data.reshape(
        planes, group_size, mode_total // group_size, pair_width
    ).transpose(1, 0, 2, 3)
    return partner_rounds(slot_buffer).reshape(
        planes * group_size, mode_total // group_size, pair_width
    )


def toward_planes(back_planes):
    x_length, mode_block, pair_width = back_planes.shape
    group_size = lax.axis_size("gx")
    slot_buffer = back_planes.reshape(group_size, x_length // group_size, mode_block, pair_width)
    arrived = partner_rounds(slot_buffer)
    return arrived.transpose(1, 0, 2, 3).reshape(
        x_length // group_size, group_size * mode_block, pair_width
    )


MESH = pl.DeviceIdType.MESH
NT = (((1,), (1,)), ((), ()))
ROOT_CONST = math.sqrt(2.0 / math.pi)


def angles_host(freq_count, grid_count):
    frequency = np.arange(freq_count) - freq_count // 2
    turn_index = np.mod(frequency[:, None] * np.arange(grid_count)[None, :], grid_count)
    return turn_index.astype(np.float32) * np.float32(2.0 * math.pi / grid_count)


def host_tables(y_count, z_count, channels):
    theta_y = angles_host(KY, y_count)
    table_y = np.concatenate([np.cos(theta_y), -np.sin(theta_y)], 0)
    theta_z = angles_host(KZ, z_count)
    eye = np.eye(16, dtype=np.float32)
    fwd_z = np.concatenate([np.kron(eye, np.cos(theta_z)), np.kron(eye, np.sin(theta_z))], 0)
    inv_z = np.concatenate([np.kron(eye, np.cos(theta_z).T), np.kron(eye, np.sin(theta_z).T)], 0)
    spread = np.tile(np.eye(channels, dtype=np.float32), (256 // channels, 1))
    return [jnp.asarray(t, jnp.bfloat16) for t in (table_y, table_y.T, fwd_z, inv_z, spread)]


def x_tables(kx_count, x_length):
    theta_x = angles_host(kx_count, x_length)[:x_length]
    rounded = [np.asarray(f(theta_x), jnp.bfloat16).astype(np.float32) for f in (np.cos, np.sin)]
    return [np.where(np.abs(t) < 1e-5, 0.0, t) for t in rounded]


def dot32(left, right):
    return jnp.dot(left, right, preferred_element_type=jnp.float32)


def lanes_low(shape):
    return lax.broadcasted_iota(jnp.int32, shape, 1) < 64


def swap(block):
    return pltpu.roll(block, 64, 1)


def turned(block):
    swapped = swap(block)
    return jnp.where(lanes_low(block.shape), swapped, -swapped)


def x_pass(read, write, cos_t, sin_t, mode_block):
    length = cos_t.shape[0]
    half = length // 2

    def step(index, carry):
        rows = pl.ds(pl.multiple_of(index * 16, 16), 16)
        data = [read(j, rows) for j in range(length)]
        folded = [
            [data[j] + data[j + half] for j in range(half)],
            [data[j] - data[j + half] for j in range(half)],
        ]
        spun = [[turned(block) for block in group] for group in folded]
        for k in range(length):
            total = None
            for j in range(half):
                for coef, block in ((cos_t[k, j], folded[k % 2][j]), (sin_t[k, j], spun[k % 2][j])):
                    coef = float(coef)
                    if coef == 0.0:
                        continue
                    term = block if coef == 1.0 else -block if coef == -1.0 else block * coef
                    total = term if total is None else total + term
            write(k, rows, total)
        return carry

    lax.fori_loop(0, mode_block // 16, step, 0, unroll=2)


def spread_cells(first_pass, mid, first_cell):
    low = lanes_low((KY, 128))
    for pair in range(first_pass.shape[1] // 128):
        real_in = first_pass[:KY, pair * 128 : pair * 128 + 128]
        imag_in = first_pass[KY:, pair * 128 : pair * 128 + 128]
        mid[:, first_cell + 2 * pair, :] = jnp.where(low, real_in, swap(imag_in))
        mid[:, first_cell + 2 * pair + 1, :] = jnp.where(low, swap(real_in), imag_in)


def forward_z(fwd_z, mid, send):
    group_size, mode_block, pair_width = send.shape
    per_half = 256 // mode_block
    for half in range(2):
        block = mid[16 * half : 16 * half + 16].reshape(256, pair_width).astype(jnp.bfloat16)
        both = dot32(fwd_z[...], block)
        data = both[:256] + turned(both[256:])
        send[half * per_half : (half + 1) * per_half] = data.reshape(
            per_half, mode_block, pair_width
        ).astype(jnp.bfloat16)


def inverse_planes(arrived, inv_z, mid, stacked, norm_scale):
    group_size, mode_block, pair_width = arrived.shape
    per_half = 256 // mode_block
    for half in range(2):
        block = arrived[half * per_half : (half + 1) * per_half].reshape(256, pair_width)
        both = dot32(inv_z[...], block)
        mid[16 * half : 16 * half + 16] = (
            (both[:256] - turned(both[256:])) * norm_scale
        ).reshape(16, 16, pair_width)
    low = lanes_low((KY, 128))
    for pair in range(stacked.shape[1] // 128):
        even = mid[:, 2 * pair, :]
        odd = mid[:, 2 * pair + 1, :]
        columns = slice(pair * 128, pair * 128 + 128)
        stacked[:KY, columns] = jnp.where(low, even, swap(odd)).astype(jnp.bfloat16)
        stacked[KY:, columns] = jnp.where(low, swap(even), odd).astype(jnp.bfloat16)


def fused_kernel(
    cos_x, sin_x, norm_scale, group_size, sample_count, alias_count,
    field_hbm, cot_hbm, weights_hbm, point_hbm, y_hbm, y_t_hbm, fwd_hbm, inv_hbm, spread_hbm,
    field_out, field_grad, shared_in, shared_grad,
    point_ref, table_y, table_y_t, fwd_z, inv_z, spread,
    field, cot, weights, folded, send, arrive, coef_in, coef_grad, mixed, mid, mid_next, stacked, accum,
    out_block, grad_block, tail_block, point_wide, point_wide_t,
    load_sem, table_sem, weight_sem, send_sem, recv_sem, sa_send, sa_recv, own_sem,
):
    me = lax.axis_index("gx")
    mine = lax.axis_index("sa")
    x_length = group_size
    mode_block = send.shape[2]
    groups = mode_block // 16

    load_field = pltpu.make_async_copy(field_hbm.at[0, 0], field, load_sem.at[0])
    load_cot = pltpu.make_async_copy(cot_hbm.at[0, 0], cot, load_sem.at[1])
    load_tables = [
        pltpu.make_async_copy(source, target, table_sem.at[index])
        for index, (source, target) in enumerate((
            (y_hbm, table_y), (fwd_hbm, fwd_z), (point_hbm, point_ref),
            (spread_hbm, spread), (inv_hbm, inv_z), (y_t_hbm, table_y_t),
        ))
    ]
    load_field.start()
    for load in load_tables:
        load.start()
    load_cot.start()

    def weight_copy(kx):
        return pltpu.make_async_copy(weights_hbm.at[kx], weights.at[kx], weight_sem.at[kx])

    for residue in range(x_length):
        for alias in range(alias_count):
            weight_copy(residue + x_length * alias).start()

    barrier = pltpu.get_barrier_semaphore()
    for hop in range(1, group_size):
        pl.semaphore_signal(
            barrier, inc=1, device_id={"gx": lax.rem(me + hop, group_size)}, device_id_type=MESH
        )
    for hop in range(1, sample_count):
        pl.semaphore_signal(
            barrier, inc=1, device_id={"sa": lax.rem(mine + hop, sample_count)}, device_id_type=MESH
        )

    def plane_copy(turn, hop):
        target = lax.rem(me + hop, group_size)
        return pltpu.make_async_remote_copy(
            src_ref=send.at[turn, target],
            dst_ref=arrive.at[turn, me],
            send_sem=send_sem.at[turn, hop],
            recv_sem=recv_sem.at[turn, hop],
            device_id={"gx": target},
            device_id_type=MESH,
        )

    def exchange_start(turn):
        for hop in range(1, group_size):
            plane_copy(turn, hop).start()
        arrive[turn, me] = send[turn, me]

    def exchange_wait(turn):
        for hop in range(1, group_size):
            plane_copy(turn, hop).wait_recv()

    def sample_copy(which, half, hop):
        source, target = ((coef_in, shared_in), (coef_grad, shared_grad))[which]
        span = pl.ds(half * (x_length // 2), x_length // 2)
        return pltpu.make_async_remote_copy(
            src_ref=source.at[span],
            dst_ref=target.at[mine, span],
            send_sem=sa_send.at[which, half, hop],
            recv_sem=sa_recv.at[which, half, hop],
            device_id={"sa": lax.rem(mine + hop, sample_count)},
            device_id_type=MESH,
        )

    def own_copy(which):
        source, target = ((coef_in, shared_in), (coef_grad, shared_grad))[which]
        return pltpu.make_async_copy(source, target.at[mine], own_sem.at[which])

    def samples_start(which, half):
        for hop in range(1, sample_count):
            sample_copy(which, half, hop).start()
        if half == 0:
            own_copy(which).start()

    def forward_modes(turn, coef):
        def read(j, rows):
            return arrive[turn, j, rows, :].astype(jnp.float32)

        def write(k, rows, value):
            coef[k, rows, :] = (value * norm_scale).astype(jnp.bfloat16)

        x_pass(read, write, cos_x, sin_x, mode_block)

    def inverse_modes(turn):
        def read(j, rows):
            return mixed[j, rows, :]

        def write(k, rows, value):
            send[turn, k, rows, :] = value.astype(jnp.bfloat16)

        x_pass(read, write, cos_x.T, -sin_x.T, mode_block)

    def wait_weights(residue):
        for alias in range(alias_count):
            weight_copy(residue + x_length * alias).wait()

    def fold_rows(pair, start):
        for part in range(1024 // 128):
            rows = pl.ds(pl.multiple_of(start + part * 128, 128), 128)
            for side in range(2):
                residue = 2 * pair + side
                total = weights[residue, rows, :].astype(jnp.float32)
                for alias in range(1, alias_count):
                    total = total + weights[residue + x_length * alias, rows, :].astype(jnp.float32)
                folded[pair, rows, side * 128 : side * 128 + 128] = total.astype(jnp.bfloat16)

    row_index = lax.broadcasted_iota(jnp.int32, (8, 128), 0)
    low16 = lanes_low((16, 128))
    own_half = (row_index + lax.broadcasted_iota(jnp.int32, (8, 128), 1) // 64) % 2 == 0
    own_pair = [row_index // 2 == pair for pair in range(4)]

    def diagonal(block):
        empty = jnp.zeros((8, 128), jnp.float32)
        columns = []
        for part in range(8):
            half = block[:8] if part < 4 else block[8:]
            kept = jnp.where(own_pair[part % 4], jnp.where(own_half, half, 0.0), 0.0)
            stacked_rows = [kept, empty] if part < 4 else [empty, kept]
            columns.append(jnp.concatenate(stacked_rows, 0).astype(jnp.bfloat16))
        return jnp.concatenate(columns, 1)

    def gathered(block):
        halves = []
        for half in range(2):
            rows = slice(half * 8, half * 8 + 8)
            kept = block[rows, half * 512 : half * 512 + 128]
            for part in range(1, 4):
                start = half * 512 + part * 128
                kept = jnp.where(own_pair[part], block[rows, start : start + 128], kept)
            halves.append(jnp.where(own_half, kept, 0.0))
        total = jnp.concatenate(halves, 0)
        return total + swap(total)

    def mix_in_group(pair, group):
        rows = slice(group * 16, group * 16 + 16)
        parts = []
        for side in range(2):
            coef = coef_in[2 * pair + side, rows, :].astype(jnp.float32)
            other = swap(coef)
            parts += [diagonal(jnp.where(low16, coef, other)), diagonal(jnp.where(low16, other, coef))]
        product = dot32(
            jnp.concatenate(parts, 0), folded[pair, group * 1024 : group * 1024 + 1024, :]
        )
        for side in range(2):
            own = product[side * 32 : side * 32 + 32, side * 128 : side * 128 + 128]
            mixed[2 * pair + side, rows, :] = own[:16] - turned(own[16:])

    def wait_pair(pair):
        wait_weights(2 * pair)
        wait_weights(2 * pair + 1)

    def fold_first(pair):
        wait_pair(pair)

        def step(index, inner):
            fold_rows(pair, index * 1024)
            return inner

        lax.fori_loop(0, groups, step, 0)

    def mix_and_fold(pair, carry):
        wait_pair(pair)
        for group in range(groups):
            mix_in_group(pair - 1, group)
            fold_rows(pair, group * 1024)
        return carry

    def mix_back(pair, carry):
        empty = jnp.zeros((32, 128), jnp.bfloat16)
        for group in range(groups):
            rows = slice(group * 16, group * 16 + 16)
            parts = []
            for side in range(2):
                coef = coef_grad[2 * pair + side, rows, :].astype(jnp.float32)
                both = jnp.concatenate([coef, turned(coef)], 0).astype(jnp.bfloat16)
                parts.append(jnp.concatenate([both, empty] if side == 0 else [empty, both], 1))
            product = lax.dot_general(
                jnp.concatenate(parts, 0), folded[pair, group * 1024 : group * 1024 + 1024, :],
                NT, preferred_element_type=jnp.float32,
            )
            for side in range(2):
                start = side * 32
                mixed[2 * pair + side, rows, :] = jnp.where(
                    low16, gathered(product[start : start + 16]),
                    gathered(product[start + 16 : start + 32]),
                )
        return carry

    def pointwise_into(source, wide):
        for part in range(accum.shape[1] // 256):
            columns = slice(part * 256, part * 256 + 256)
            accum[:, columns] = dot32(source[:, columns], wide[...])

    load_field.wait()
    load_tables[0].wait()
    spread_cells(dot32(table_y[...], field[...]), mid, 0)
    load_tables[1].wait()
    forward_z(fwd_z, mid, send.at[0])
    pl.semaphore_wait(barrier, group_size + sample_count - 2)
    exchange_start(0)

    same_block = (
        lax.broadcasted_iota(jnp.int32, (256, 256), 0) // 64
        == lax.broadcasted_iota(jnp.int32, (256, 256), 1) // 64
    )

    def widened(block):
        wide = lax.dot_general(block.astype(jnp.bfloat16), spread[...], NT, preferred_element_type=jnp.float32)
        return jnp.where(same_block, wide, 0.0).astype(jnp.bfloat16)

    for load in load_tables[2:]:
        load.wait()
    point_wide[...] = widened(dot32(spread[...], point_ref[...]))
    point_wide_t[...] = widened(
        lax.dot_general(spread[...], point_ref[...], NT, preferred_element_type=jnp.float32)
    )
    pointwise_into(field, point_wide)

    fold_first(0)
    exchange_wait(0)
    forward_modes(0, coef_in)
    samples_start(0, 0)
    lax.fori_loop(1, x_length // 2, mix_and_fold, 0)
    for group in range(groups):
        mix_in_group(x_length // 2 - 1, group)
    inverse_modes(1)
    exchange_start(1)
    load_cot.wait()
    exchange_wait(1)
    samples_start(0, 1)
    inverse_planes(arrive.at[1], inv_z, mid, stacked, norm_scale)
    for part in range(accum.shape[1] // 256):
        columns = slice(part * 256, part * 256 + 256)
        spectrum = dot32(table_y_t[...], stacked[:, columns])
        for start in range(0, accum.shape[0], 32):
            rows = slice(start, start + 32)
            pre_act = accum[rows, columns] + spectrum[rows]
            square = pre_act * pre_act
            half_gate = 0.5 + 0.5 * jnp.tanh(pre_act * (ROOT_CONST + ROOT_CONST * GELU_COEF * square))
            activated = pre_act * half_gate
            inner_slope = 2.0 * ROOT_CONST + 6.0 * ROOT_CONST * GELU_COEF * square
            gelu_slope = half_gate + activated * (1.0 - half_gate) * inner_slope
            out_block[rows, columns] = activated.astype(jnp.bfloat16)
            grad_block[rows, columns] = (cot[rows, columns].astype(jnp.float32) * gelu_slope).astype(
                jnp.bfloat16
            )
        spread_cells(dot32(table_y[...], grad_block[:, columns]), mid_next, 4 * part)
    forward_z(fwd_z, mid_next, send.at[2])
    exchange_start(2)
    store_out = pltpu.make_async_copy(out_block, field_out.at[0, 0], load_sem.at[2])
    store_out.start()

    pointwise_into(grad_block, point_wide_t)
    exchange_wait(2)
    forward_modes(2, coef_grad)
    samples_start(1, 0)
    lax.fori_loop(0, x_length // 2, mix_back, 0)
    inverse_modes(3)
    exchange_start(3)
    samples_start(1, 1)
    exchange_wait(3)
    inverse_planes(arrive.at[3], inv_z, mid, stacked, norm_scale)
    for part in range(accum.shape[1] // 256):
        columns = slice(part * 256, part * 256 + 256)
        tail_block[:, columns] = (
            accum[:, columns] + dot32(table_y_t[...], stacked[:, columns])
        ).astype(jnp.bfloat16)
    store_grad = pltpu.make_async_copy(tail_block, field_grad.at[0, 0], load_sem.at[3])
    store_grad.start()

    for turn in range(4):
        for hop in range(1, group_size):
            plane_copy(turn, hop).wait_send()
    for which in range(2):
        own_copy(which).wait()
        for half in range(2):
            for hop in range(1, sample_count):
                sample_copy(which, half, hop).wait()
    store_out.wait()
    store_grad.wait()


def weight_kernel(
    left_hbm, right_hbm, first_hbm, second_hbm, weight_out, first_out, second_out,
    left_ref, right_ref, first_ref, second_ref, blocks, load_sem, pass_sem, block_sem,
):
    loads = [
        pltpu.make_async_copy(left_hbm, left_ref, load_sem.at[0]),
        pltpu.make_async_copy(right_hbm, right_ref, load_sem.at[1]),
    ]
    fetches = [
        pltpu.make_async_copy(first_hbm, first_ref, load_sem.at[2]),
        pltpu.make_async_copy(second_hbm, second_ref, load_sem.at[3]),
    ]
    passes = [
        pltpu.make_async_copy(first_ref, first_out, pass_sem.at[0]),
        pltpu.make_async_copy(second_ref, second_out, pass_sem.at[1]),
    ]
    for copy in loads + fetches:
        copy.start()
    for copy in loads:
        copy.wait()
    sample_count, x_length, mode_block = left_ref.shape[:3]
    depth = 2 * sample_count * 16
    groups = mode_block // 16
    own_lane = lax.broadcasted_iota(jnp.int32, (64, depth), 1) % 16

    def block_copy(index):
        return pltpu.make_async_copy(blocks.at[index], weight_out.at[index], block_sem.at[index])

    def step(residue, carry):
        for group in range(groups):
            index = residue * groups + group
            rows = slice(group * 16, group * 16 + 16)
            left = jnp.concatenate([left_ref[s, residue, rows, :] for s in range(sample_count)], 0)
            right = jnp.concatenate([right_ref[s, residue, rows, :] for s in range(sample_count)], 0)
            flipped = left.astype(jnp.float32).T
            flipped = jnp.concatenate([flipped[:64], flipped[64:]], axis=1)
            wide = right.astype(jnp.float32)
            stack = jnp.concatenate([wide, turned(wide)], 0).astype(jnp.bfloat16)
            kept = jnp.concatenate(
                [jnp.where(own_lane == mode, flipped, 0.0).astype(jnp.bfloat16) for mode in range(16)], 0
            )
            blocks[index] = dot32(kept, stack)
            block_copy(index).start()
        return carry

    step(0, 0)
    for fetch, copy in zip(fetches, passes):
        fetch.wait()
        copy.start()
    lax.fori_loop(1, x_length, step, 0)

    def finish(index, carry):
        block_copy(index).wait()
        return carry

    lax.fori_loop(0, x_length * groups, finish, 0)
    for copy in passes:
        copy.wait()


def fused_device(field_in, cotangent, mode_weights, point_weights):
    y_count, last_width = field_in.shape[2:]
    channels = point_weights.shape[0]
    z_count = last_width // channels
    kx_count, mode_block = mode_weights.shape[:2]
    group_size = lax.axis_size("gx")
    sample_count = lax.axis_size("sa")
    x_length = group_size
    pair_width = 2 * channels
    norm_scale = 1.0 / math.sqrt(x_length * y_count * z_count)
    cos_x, sin_x = x_tables(kx_count, x_length)
    tables = host_tables(y_count, z_count, channels)
    bf16, f32 = jnp.bfloat16, jnp.float32
    plane = (y_count, last_width)
    coef_shape = (x_length, mode_block, pair_width)
    anywhere = pl.BlockSpec(memory_space=pl.ANY)
    field_out, field_grad, shared_in, shared_grad = pl.pallas_call(
        functools.partial(
            fused_kernel, cos_x, sin_x, norm_scale, group_size, sample_count, kx_count // x_length
        ),
        out_shape=[
            jax.ShapeDtypeStruct((1, 1) + plane, bf16),
            jax.ShapeDtypeStruct((1, 1) + plane, bf16),
            jax.ShapeDtypeStruct((sample_count,) + coef_shape, bf16),
            jax.ShapeDtypeStruct((sample_count,) + coef_shape, bf16),
        ],
        in_specs=[anywhere] * 9,
        out_specs=[anywhere] * 4,
        scratch_shapes=[
            pltpu.VMEM((channels, channels), bf16),
            *[pltpu.VMEM(table.shape, bf16) for table in tables],
            pltpu.VMEM(plane, bf16),
            pltpu.VMEM(plane, bf16),
            pltpu.VMEM((kx_count, mode_block * channels, pair_width), bf16),
            pltpu.VMEM((x_length // 2, mode_block * channels, 2 * pair_width), bf16),
            pltpu.VMEM((4,) + coef_shape, bf16),
            pltpu.VMEM((4,) + coef_shape, bf16),
            pltpu.VMEM(coef_shape, bf16),
            pltpu.VMEM(coef_shape, bf16),
            pltpu.VMEM(coef_shape, f32),
            pltpu.VMEM((KY, z_count, pair_width), f32),
            pltpu.VMEM((KY, z_count, pair_width), f32),
            pltpu.VMEM((2 * KY, last_width), bf16),
            pltpu.VMEM(plane, f32),
            pltpu.VMEM(plane, bf16),
            pltpu.VMEM(plane, bf16),
            pltpu.VMEM(plane, bf16),
            pltpu.VMEM((256, 256), bf16),
            pltpu.VMEM((256, 256), bf16),
            pltpu.SemaphoreType.DMA((4,)),
            pltpu.SemaphoreType.DMA((6,)),
            pltpu.SemaphoreType.DMA((kx_count,)),
            pltpu.SemaphoreType.DMA((4, group_size)),
            pltpu.SemaphoreType.DMA((4, group_size)),
            pltpu.SemaphoreType.DMA((2, 2, sample_count)),
            pltpu.SemaphoreType.DMA((2, 2, sample_count)),
            pltpu.SemaphoreType.DMA((2,)),
        ],
        compiler_params=pltpu.CompilerParams(
            collective_id=0, has_side_effects=True, vmem_limit_bytes=56 * 1024 * 1024
        ),
        name="fourier_layer",
    )(
        field_in, cotangent,
        mode_weights.reshape(kx_count, mode_block * channels, pair_width),
        point_weights, *tables,
    )
    groups = mode_block // 16
    weight_grad, field_out, field_grad = pl.pallas_call(
        weight_kernel,
        out_shape=[
            jax.ShapeDtypeStruct((x_length * groups, 16 * channels, pair_width), f32),
            jax.ShapeDtypeStruct((1, 1) + plane, bf16),
            jax.ShapeDtypeStruct((1, 1) + plane, bf16),
        ],
        in_specs=[anywhere] * 4,
        out_specs=[anywhere] * 3,
        scratch_shapes=[
            pltpu.VMEM((sample_count,) + coef_shape, bf16),
            pltpu.VMEM((sample_count,) + coef_shape, bf16),
            pltpu.VMEM((1, 1) + plane, bf16),
            pltpu.VMEM((1, 1) + plane, bf16),
            pltpu.VMEM((x_length * groups, 16 * channels, pair_width), f32),
            pltpu.SemaphoreType.DMA((4,)),
            pltpu.SemaphoreType.DMA((2,)),
            pltpu.SemaphoreType.DMA((x_length * groups,)),
        ],
        compiler_params=pltpu.CompilerParams(vmem_limit_bytes=56 * 1024 * 1024),
        name="weight_gradient",
    )(shared_in, shared_grad, field_out, field_grad)
    return (
        field_out, field_grad,
        weight_grad.reshape(x_length, mode_block, channels, pair_width),
    )


def folds(field_in, mode_weights, point_weights):
    group_size, sample_count = lax.axis_size("gx"), lax.axis_size("sa")
    kx_count, mode_block, channels = mode_weights.shape[:3]
    planes, y_count, last_width = field_in.shape[1:]
    return (
        planes == 1
        and field_in.shape[0] == 1
        and channels == 64
        and last_width == 16 * channels
        and y_count % 16 == 0
        and group_size % 4 == 0
        and mode_block == 64
        and kx_count % group_size == 0
        and kx_count == sample_count * group_size
    )


def on_device(field_in, cotangent, mode_weights, point_weights):
    if folds(field_in, mode_weights, point_weights):
        return fused_device(field_in, cotangent, mode_weights, point_weights)
    local_field = field_in[0]
    planes, y_count, last_width = local_field.shape
    channels = point_weights.shape[0]
    z_count = last_width // channels
    kx_count = mode_weights.shape[0]
    x_length = planes * lax.axis_size("gx")
    norm_scale = 1.0 / math.sqrt(x_length * y_count * z_count)
    coeffs_in = forward_x(toward_modes(forward_yz(local_field, channels)), kx_count, norm_scale)
    mixed_modes = mix_forward(coeffs_in, mode_weights)
    spec_out = inverse_yz(
        toward_planes(inverse_x(mixed_modes, x_length)), y_count, z_count, norm_scale
    )
    pre_act = spec_out + pointwise(local_field, point_weights)
    activated, gelu_slope = gelu_parts(pre_act)
    out_grad = (cotangent[0].astype(jnp.float32) * gelu_slope).astype(jnp.bfloat16)
    coeffs_grad = forward_x(toward_modes(forward_yz(out_grad, channels)), kx_count, norm_scale)
    back_modes = mix_backward(coeffs_grad, mode_weights)
    spec_grad = inverse_yz(
        toward_planes(inverse_x(back_modes, x_length)), y_count, z_count, norm_scale
    )
    field_grad = (spec_grad + pointwise(out_grad, point_weights.T)).astype(jnp.bfloat16)
    shared_in, shared_grad = (
        lax.all_to_all(coeffs_in[None], "sa", split_axis=1, concat_axis=0, tiled=True),
        lax.all_to_all(coeffs_grad[None], "sa", split_axis=1, concat_axis=0, tiled=True),
    )
    weight_grad = sample_sum(shared_in, shared_grad)
    return (activated.astype(jnp.bfloat16)[None], field_grad[None], weight_grad)


def solution(mesh):
    in_specs = (
        P("sa", "gx", None, None),
        P("sa", "gx", None, None),
        P(None, "gx", None, None),
        P(),
    )
    out_specs = (P("sa", "gx", None, None), P("sa", "gx", None, None), P("sa", "gx", None, None))
    return jax.shard_map(
        on_device, mesh=mesh, in_specs=in_specs, out_specs=out_specs, check_vma=False
    )
```

```python
import functools
import math

import jax
import jax.numpy as jnp
import numpy as np
from jax import lax
from jax.experimental import pallas as pl
from jax.experimental.pallas import tpu as pltpu
from jax.sharding import PartitionSpec as P

KY = 32
KZ = 16


HIGHEST_PREC = lax.Precision.HIGHEST
GELU_COEF = 0.044715


def partner(block, axis, distance):
    count = lax.axis_size(axis)
    route = []
    for low in range(count):
        high = low | 1 << distance
        if high != low and high < count:
            route += [(low, high), (high, low)]
    return lax.ppermute(block, axis, route)


def angles(freq_count, grid_count):
    frequency = jnp.arange(freq_count, dtype=jnp.int32) - freq_count // 2
    places = jnp.arange(grid_count, dtype=jnp.int32)
    turn_index = jnp.mod(frequency[:, None] * places[None, :], grid_count)
    return turn_index.astype(jnp.float32) * (2.0 * math.pi / grid_count)


def gelu_parts(pre_act):
    root_const = math.sqrt(2.0 / math.pi)
    inner_arg = root_const * (pre_act + GELU_COEF * pre_act * pre_act * pre_act)
    tangent = jnp.tanh(inner_arg)
    activated = 0.5 * pre_act * (1.0 + tangent)
    gelu_slope = 0.5 * (1.0 + tangent) + 0.5 * pre_act * (1.0 - tangent * tangent) * root_const * (
        1.0 + 3.0 * GELU_COEF * pre_act * pre_act
    )
    return (activated, gelu_slope)


def along_z_forward(data_in, table_z):
    return jnp.einsum("pyzc,kz->pykc", data_in, table_z, precision=HIGHEST_PREC)


def along_z_inverse(data_in, table_z):
    return jnp.einsum("pykc,kz->pyzc", data_in, table_z, precision=HIGHEST_PREC)


def forward_yz(local_field, channels):
    planes, y_count, last_width = local_field.shape
    z_count = last_width // channels
    theta_y = angles(KY, y_count)
    table_y = jnp.concatenate([jnp.cos(theta_y), -jnp.sin(theta_y)], 0).astype(jnp.bfloat16)
    first_pass = jnp.einsum("fy,pyq->pfq", table_y, local_field, preferred_element_type=jnp.float32)
    first_pass = first_pass.reshape(planes, 2, KY, z_count, channels)
    theta_z = angles(KZ, z_count)
    cos_z = jnp.cos(theta_z)
    sin_z = jnp.sin(theta_z)
    real_in = first_pass[:, 0]
    imag_in = first_pass[:, 1]
    real_out = along_z_forward(real_in, cos_z) + along_z_forward(imag_in, sin_z)
    imag_out = along_z_forward(imag_in, cos_z) - along_z_forward(real_in, sin_z)
    mode_data = jnp.concatenate([real_out, imag_out], -1)
    return mode_data.reshape(planes, KY * KZ, 2 * channels).astype(jnp.bfloat16)


def forward_x(mode_data, kx_count, norm_scale):
    x_length, mode_block, pair_width = mode_data.shape
    channels = pair_width // 2
    theta_x = angles(kx_count, x_length)
    flat_data = mode_data.reshape(x_length, mode_block * pair_width)
    cos_part = jnp.dot(
        jnp.cos(theta_x).astype(jnp.bfloat16), flat_data, preferred_element_type=jnp.float32
    ).reshape(kx_count, mode_block, pair_width)
    sin_part = jnp.dot(
        jnp.sin(theta_x).astype(jnp.bfloat16), flat_data, preferred_element_type=jnp.float32
    ).reshape(kx_count, mode_block, pair_width)
    real_out = cos_part[..., :channels] + sin_part[..., channels:]
    imag_out = cos_part[..., channels:] - sin_part[..., :channels]
    return (jnp.concatenate([real_out, imag_out], -1) * norm_scale).astype(jnp.bfloat16)


def inverse_x(mixed_modes, x_length):
    kx_count, mode_block, pair_width = mixed_modes.shape
    channels = pair_width // 2
    theta_x = angles(kx_count, x_length).T
    flat_data = mixed_modes.reshape(kx_count, mode_block * pair_width)
    cos_part = jnp.dot(
        jnp.cos(theta_x).astype(jnp.bfloat16), flat_data, preferred_element_type=jnp.float32
    ).reshape(x_length, mode_block, pair_width)
    sin_part = jnp.dot(
        jnp.sin(theta_x).astype(jnp.bfloat16), flat_data, preferred_element_type=jnp.float32
    ).reshape(x_length, mode_block, pair_width)
    real_out = cos_part[..., :channels] - sin_part[..., channels:]
    imag_out = cos_part[..., channels:] + sin_part[..., :channels]
    return jnp.concatenate([real_out, imag_out], -1).astype(jnp.bfloat16)


def inverse_yz(planes_data, y_count, z_count, norm_scale):
    planes, mode_total, pair_width = planes_data.shape
    channels = pair_width // 2
    wide_data = planes_data.astype(jnp.float32).reshape(planes, KY, KZ, pair_width)
    real_in = wide_data[..., :channels]
    imag_in = wide_data[..., channels:]
    theta_z = angles(KZ, z_count)
    cos_z = jnp.cos(theta_z)
    sin_z = jnp.sin(theta_z)
    real_mid = along_z_inverse(real_in, cos_z) - along_z_inverse(imag_in, sin_z)
    imag_mid = along_z_inverse(imag_in, cos_z) + along_z_inverse(real_in, sin_z)
    stacked = jnp.concatenate([real_mid, imag_mid], 1).reshape(planes, 2 * KY, z_count * channels)
    theta_y = angles(KY, y_count)
    table_y = jnp.concatenate([jnp.cos(theta_y), -jnp.sin(theta_y)], 0)
    return jnp.einsum("pfq,fy->pyq", stacked, table_y, precision=HIGHEST_PREC) * norm_scale


def mix_forward(coeffs, weights_local):
    channels = weights_local.shape[2]
    real_part = jnp.einsum(
        "kmc,kmcp->kmp", coeffs[..., :channels], weights_local, preferred_element_type=jnp.float32
    )
    imag_part = jnp.einsum(
        "kmc,kmcp->kmp", coeffs[..., channels:], weights_local, preferred_element_type=jnp.float32
    )
    out_real = real_part[..., :channels] - imag_part[..., channels:]
    out_imag = real_part[..., channels:] + imag_part[..., :channels]
    return jnp.concatenate([out_real, out_imag], -1).astype(jnp.bfloat16)


def mix_backward(coeffs, weights_local):
    channels = weights_local.shape[2]
    swapped = jnp.concatenate([coeffs[..., channels:], -coeffs[..., :channels]], -1)
    first_half = jnp.einsum(
        "kmp,kmcp->kmc", coeffs, weights_local, preferred_element_type=jnp.float32
    )
    second_half = jnp.einsum(
        "kmp,kmcp->kmc", swapped, weights_local, preferred_element_type=jnp.float32
    )
    return jnp.concatenate([first_half, second_half], -1).astype(jnp.bfloat16)


def pointwise(local_field, weights_small):
    planes, y_count, last_width = local_field.shape
    channels = weights_small.shape[0]
    paired = jnp.kron(jnp.eye(2, dtype=weights_small.dtype), weights_small)
    cell_pairs = local_field.reshape(planes * y_count * last_width // (2 * channels), 2 * channels)
    return jnp.dot(cell_pairs, paired, preferred_element_type=jnp.float32).reshape(
        planes, y_count, last_width
    )


def sample_sum(left_side, right_side):
    channels = left_side.shape[-1] // 2
    left_real = left_side[..., :channels]
    left_imag = left_side[..., channels:]
    right_real = right_side[..., :channels]
    right_imag = right_side[..., channels:]

    def outer_sum(left_op, right_op):
        return jnp.einsum("skmc,skmo->kmco", left_op, right_op, preferred_element_type=jnp.float32)

    real_sum = outer_sum(left_real, right_real) + outer_sum(left_imag, right_imag)
    imag_sum = outer_sum(left_real, right_imag) - outer_sum(left_imag, right_real)
    return jnp.concatenate([real_sum, imag_sum], -1)


def partner_rounds(slot_buffer):
    slot_count = slot_buffer.shape[0]
    my_index = lax.axis_index("gx")
    for bit_pos in range(slot_count.bit_length() - 1):
        shaped = slot_buffer.reshape(
            (slot_count >> bit_pos + 1, 2, 1 << bit_pos) + slot_buffer.shape[1:]
        )
        lower_half = shaped[:, 0]
        upper_half = shaped[:, 1]
        own_bit = jnp.bitwise_and(jnp.right_shift(my_index, bit_pos), 1) == 1
        outgoing = jnp.where(own_bit, lower_half, upper_half)
        incoming = partner(outgoing, "gx", bit_pos)
        new_lower = jnp.where(own_bit, incoming, lower_half)
        new_upper = jnp.where(own_bit, upper_half, incoming)
        slot_buffer = jnp.stack([new_lower, new_upper], 1).reshape(slot_buffer.shape)
    return slot_buffer


def toward_modes(mode_data):
    planes, mode_total, pair_width = mode_data.shape
    group_size = lax.axis_size("gx")
    slot_buffer = mode_data.reshape(
        planes, group_size, mode_total // group_size, pair_width
    ).transpose(1, 0, 2, 3)
    return partner_rounds(slot_buffer).reshape(
        planes * group_size, mode_total // group_size, pair_width
    )


def toward_planes(back_planes):
    x_length, mode_block, pair_width = back_planes.shape
    group_size = lax.axis_size("gx")
    slot_buffer = back_planes.reshape(group_size, x_length // group_size, mode_block, pair_width)
    arrived = partner_rounds(slot_buffer)
    return arrived.transpose(1, 0, 2, 3).reshape(
        x_length // group_size, group_size * mode_block, pair_width
    )


MESH = pl.DeviceIdType.MESH
NT = (((1,), (1,)), ((), ()))
ROOT_CONST = math.sqrt(2.0 / math.pi)


def angles_host(freq_count, grid_count):
    frequency = np.arange(freq_count) - freq_count // 2
    turn_index = np.mod(frequency[:, None] * np.arange(grid_count)[None, :], grid_count)
    return turn_index.astype(np.float32) * np.float32(2.0 * math.pi / grid_count)


def host_tables(y_count, z_count, channels):
    theta_y = angles_host(KY, y_count)
    table_y = np.concatenate([np.cos(theta_y), -np.sin(theta_y)], 0)
    theta_z = angles_host(KZ, z_count)
    eye = np.eye(16, dtype=np.float32)
    fwd_z = np.concatenate([np.kron(eye, np.cos(theta_z)), np.kron(eye, np.sin(theta_z))], 0)
    inv_z = np.concatenate([np.kron(eye, np.cos(theta_z).T), np.kron(eye, np.sin(theta_z).T)], 0)
    spread = np.tile(np.eye(channels, dtype=np.float32), (256 // channels, 1))
    return [jnp.asarray(t, jnp.bfloat16) for t in (table_y, table_y.T, fwd_z, inv_z, spread)]


def x_tables(kx_count, x_length):
    theta_x = angles_host(kx_count, x_length)[:x_length]
    rounded = [np.asarray(f(theta_x), jnp.bfloat16).astype(np.float32) for f in (np.cos, np.sin)]
    return [np.where(np.abs(t) < 1e-5, 0.0, t) for t in rounded]


def dot32(left, right):
    return jnp.dot(left, right, preferred_element_type=jnp.float32)


def lanes_low(shape):
    return lax.broadcasted_iota(jnp.int32, shape, 1) < 64


def swap(block):
    return pltpu.roll(block, 64, 1)


def turned(block):
    swapped = swap(block)
    return jnp.where(lanes_low(block.shape), swapped, -swapped)


def x_pass(read, write, cos_t, sin_t, mode_block):
    length = cos_t.shape[0]
    half = length // 2

    def step(index, carry):
        rows = pl.ds(pl.multiple_of(index * 16, 16), 16)
        data = [read(j, rows) for j in range(length)]
        folded = [
            [data[j] + data[j + half] for j in range(half)],
            [data[j] - data[j + half] for j in range(half)],
        ]
        spun = [[turned(block) for block in group] for group in folded]
        for k in range(length):
            total = None
            for j in range(half):
                for coef, block in ((cos_t[k, j], folded[k % 2][j]), (sin_t[k, j], spun[k % 2][j])):
                    coef = float(coef)
                    if coef == 0.0:
                        continue
                    term = block if coef == 1.0 else -block if coef == -1.0 else block * coef
                    total = term if total is None else total + term
            write(k, rows, total)
        return carry

    lax.fori_loop(0, mode_block // 16, step, 0, unroll=2)


def spread_cells(first_pass, mid, first_cell):
    low = lanes_low((KY, 128))
    for pair in range(first_pass.shape[1] // 128):
        real_in = first_pass[:KY, pair * 128 : pair * 128 + 128]
        imag_in = first_pass[KY:, pair * 128 : pair * 128 + 128]
        mid[:, first_cell + 2 * pair, :] = jnp.where(low, real_in, swap(imag_in))
        mid[:, first_cell + 2 * pair + 1, :] = jnp.where(low, swap(real_in), imag_in)


def forward_z(fwd_z, mid, send):
    group_size, mode_block, pair_width = send.shape
    per_half = 256 // mode_block
    for half in range(2):
        block = mid[16 * half : 16 * half + 16].reshape(256, pair_width).astype(jnp.bfloat16)
        both = dot32(fwd_z[...], block)
        data = both[:256] + turned(both[256:])
        send[half * per_half : (half + 1) * per_half] = data.reshape(
            per_half, mode_block, pair_width
        ).astype(jnp.bfloat16)


def inverse_planes(arrived, inv_z, mid, stacked, norm_scale):
    group_size, mode_block, pair_width = arrived.shape
    per_half = 256 // mode_block
    for half in range(2):
        block = arrived[half * per_half : (half + 1) * per_half].reshape(256, pair_width)
        both = dot32(inv_z[...], block)
        mid[16 * half : 16 * half + 16] = (
            (both[:256] - turned(both[256:])) * norm_scale
        ).reshape(16, 16, pair_width)
    low = lanes_low((KY, 128))
    for pair in range(stacked.shape[1] // 128):
        even = mid[:, 2 * pair, :]
        odd = mid[:, 2 * pair + 1, :]
        columns = slice(pair * 128, pair * 128 + 128)
        stacked[:KY, columns] = jnp.where(low, even, swap(odd)).astype(jnp.bfloat16)
        stacked[KY:, columns] = jnp.where(low, swap(even), odd).astype(jnp.bfloat16)


def fused_kernel(
    cos_x, sin_x, norm_scale, group_size, sample_count, alias_count,
    field_hbm, cot_hbm, weights_hbm, point_hbm, y_hbm, y_t_hbm, fwd_hbm, inv_hbm, spread_hbm,
    field_out, field_grad, shared_in, shared_grad,
    point_ref, table_y, table_y_t, fwd_z, inv_z, spread,
    field, cot, weights, folded, send, arrive, coef_in, coef_grad, mixed, mid, mid_next, stacked, accum,
    out_block, grad_block, tail_block, point_wide, point_wide_t,
    load_sem, table_sem, weight_sem, send_sem, recv_sem, sa_send, sa_recv, own_sem,
):
    me = lax.axis_index("gx")
    mine = lax.axis_index("sa")
    x_length = group_size
    mode_block = send.shape[2]
    groups = mode_block // 16

    load_field = pltpu.make_async_copy(field_hbm.at[0, 0], field, load_sem.at[0])
    load_cot = pltpu.make_async_copy(cot_hbm.at[0, 0], cot, load_sem.at[1])
    load_tables = [
        pltpu.make_async_copy(source, target, table_sem.at[index])
        for index, (source, target) in enumerate((
            (y_hbm, table_y), (fwd_hbm, fwd_z), (point_hbm, point_ref),
            (spread_hbm, spread), (inv_hbm, inv_z), (y_t_hbm, table_y_t),
        ))
    ]
    load_field.start()
    for load in load_tables:
        load.start()
    load_cot.start()

    def weight_copy(kx):
        return pltpu.make_async_copy(weights_hbm.at[kx], weights.at[kx], weight_sem.at[kx])

    for residue in range(x_length):
        for alias in range(alias_count):
            weight_copy(residue + x_length * alias).start()

    barrier = pltpu.get_barrier_semaphore()
    for hop in range(1, group_size):
        pl.semaphore_signal(
            barrier, inc=1, device_id={"gx": lax.rem(me + hop, group_size)}, device_id_type=MESH
        )
    for hop in range(1, sample_count):
        pl.semaphore_signal(
            barrier, inc=1, device_id={"sa": lax.rem(mine + hop, sample_count)}, device_id_type=MESH
        )

    def plane_copy(turn, hop):
        target = lax.rem(me + hop, group_size)
        return pltpu.make_async_remote_copy(
            src_ref=send.at[turn, target],
            dst_ref=arrive.at[turn, me],
            send_sem=send_sem.at[turn, hop],
            recv_sem=recv_sem.at[turn, hop],
            device_id={"gx": target},
            device_id_type=MESH,
        )

    def exchange_start(turn):
        for hop in range(1, group_size):
            plane_copy(turn, hop).start()
        arrive[turn, me] = send[turn, me]

    def exchange_wait(turn):
        for hop in range(1, group_size):
            plane_copy(turn, hop).wait_recv()

    def sample_copy(which, half, hop):
        source, target = ((coef_in, shared_in), (coef_grad, shared_grad))[which]
        span = pl.ds(half * (x_length // 2), x_length // 2)
        return pltpu.make_async_remote_copy(
            src_ref=source.at[span],
            dst_ref=target.at[mine, span],
            send_sem=sa_send.at[which, half, hop],
            recv_sem=sa_recv.at[which, half, hop],
            device_id={"sa": lax.rem(mine + hop, sample_count)},
            device_id_type=MESH,
        )

    def own_copy(which):
        source, target = ((coef_in, shared_in), (coef_grad, shared_grad))[which]
        return pltpu.make_async_copy(source, target.at[mine], own_sem.at[which])

    def samples_start(which, half):
        for hop in range(1, sample_count):
            sample_copy(which, half, hop).start()
        if half == 0:
            own_copy(which).start()

    def forward_modes(turn, coef):
        def read(j, rows):
            return arrive[turn, j, rows, :].astype(jnp.float32)

        def write(k, rows, value):
            coef[k, rows, :] = (value * norm_scale).astype(jnp.bfloat16)

        x_pass(read, write, cos_x, sin_x, mode_block)

    def inverse_modes(turn):
        def read(j, rows):
            return mixed[j, rows, :]

        def write(k, rows, value):
            send[turn, k, rows, :] = value.astype(jnp.bfloat16)

        x_pass(read, write, cos_x.T, -sin_x.T, mode_block)

    def wait_weights(residue):
        for alias in range(alias_count):
            weight_copy(residue + x_length * alias).wait()

    def fold_rows(pair, start):
        for part in range(1024 // 128):
            rows = pl.ds(pl.multiple_of(start + part * 128, 128), 128)
            for side in range(2):
                residue = 2 * pair + side
                terms = [
                    weights[residue + x_length * alias, rows, :] for alias in range(alias_count)
                ]
                while len(terms) > 1:
                    terms = [sum(terms[k + 1 : k + 2], terms[k]) for k in range(0, len(terms), 2)]
                folded[pair, rows, side * 128 : side * 128 + 128] = terms[0]

    row_index = lax.broadcasted_iota(jnp.int32, (8, 128), 0)
    low16 = lanes_low((16, 128))
    own_half = (row_index + lax.broadcasted_iota(jnp.int32, (8, 128), 1) // 64) % 2 == 0
    own_pair = [row_index // 2 == pair for pair in range(4)]

    def diagonal(block):
        empty = jnp.zeros((8, 128), jnp.float32)
        columns = []
        for part in range(8):
            half = block[:8] if part < 4 else block[8:]
            kept = jnp.where(own_pair[part % 4], jnp.where(own_half, half, 0.0), 0.0)
            stacked_rows = [kept, empty] if part < 4 else [empty, kept]
            columns.append(jnp.concatenate(stacked_rows, 0).astype(jnp.bfloat16))
        return jnp.concatenate(columns, 1)

    def gathered(block):
        halves = []
        for half in range(2):
            rows = slice(half * 8, half * 8 + 8)
            kept = block[rows, half * 512 : half * 512 + 128]
            for part in range(1, 4):
                start = half * 512 + part * 128
                kept = jnp.where(own_pair[part], block[rows, start : start + 128], kept)
            halves.append(jnp.where(own_half, kept, 0.0))
        total = jnp.concatenate(halves, 0)
        return total + swap(total)

    def mix_in_group(pair, group):
        rows = slice(group * 16, group * 16 + 16)
        parts = []
        for side in range(2):
            coef = coef_in[2 * pair + side, rows, :].astype(jnp.float32)
            other = swap(coef)
            parts += [diagonal(jnp.where(low16, coef, other)), diagonal(jnp.where(low16, other, coef))]
        product = dot32(
            jnp.concatenate(parts, 0), folded[pair, group * 1024 : group * 1024 + 1024, :]
        )
        for side in range(2):
            own = product[side * 32 : side * 32 + 32, side * 128 : side * 128 + 128]
            mixed[2 * pair + side, rows, :] = own[:16] - turned(own[16:])

    def wait_pair(pair):
        wait_weights(2 * pair)
        wait_weights(2 * pair + 1)

    def fold_first(pair):
        wait_pair(pair)

        def step(index, inner):
            fold_rows(pair, index * 1024)
            return inner

        lax.fori_loop(0, groups, step, 0)

    def mix_and_fold(pair, carry):
        wait_pair(pair)
        for group in range(groups):
            mix_in_group(pair - 1, group)
            fold_rows(pair, group * 1024)
        return carry

    def mix_back(pair, carry):
        empty = jnp.zeros((32, 128), jnp.bfloat16)
        for group in range(groups):
            rows = slice(group * 16, group * 16 + 16)
            parts = []
            for side in range(2):
                coef = coef_grad[2 * pair + side, rows, :].astype(jnp.float32)
                both = jnp.concatenate([coef, turned(coef)], 0).astype(jnp.bfloat16)
                parts.append(jnp.concatenate([both, empty] if side == 0 else [empty, both], 1))
            product = lax.dot_general(
                jnp.concatenate(parts, 0), folded[pair, group * 1024 : group * 1024 + 1024, :],
                NT, preferred_element_type=jnp.float32,
            )
            for side in range(2):
                start = side * 32
                mixed[2 * pair + side, rows, :] = jnp.where(
                    low16, gathered(product[start : start + 16]),
                    gathered(product[start + 16 : start + 32]),
                )
        return carry

    def pointwise_into(source, wide):
        for part in range(accum.shape[1] // 256):
            columns = slice(part * 256, part * 256 + 256)
            accum[:, columns] = dot32(source[:, columns], wide[...])

    load_field.wait()
    load_tables[0].wait()
    spread_cells(dot32(table_y[...], field[...]), mid, 0)
    load_tables[1].wait()
    forward_z(fwd_z, mid, send.at[0])
    pl.semaphore_wait(barrier, group_size + sample_count - 2)
    exchange_start(0)

    same_block = (
        lax.broadcasted_iota(jnp.int32, (256, 256), 0) // 64
        == lax.broadcasted_iota(jnp.int32, (256, 256), 1) // 64
    )

    def widened(block):
        wide = lax.dot_general(block.astype(jnp.bfloat16), spread[...], NT, preferred_element_type=jnp.float32)
        return jnp.where(same_block, wide, 0.0).astype(jnp.bfloat16)

    for load in load_tables[2:]:
        load.wait()
    point_wide[...] = widened(dot32(spread[...], point_ref[...]))
    point_wide_t[...] = widened(
        lax.dot_general(spread[...], point_ref[...], NT, preferred_element_type=jnp.float32)
    )
    pointwise_into(field, point_wide)

    fold_first(0)
    exchange_wait(0)
    forward_modes(0, coef_in)
    samples_start(0, 0)
    lax.fori_loop(1, x_length // 2, mix_and_fold, 0)
    for group in range(groups):
        mix_in_group(x_length // 2 - 1, group)
    inverse_modes(1)
    exchange_start(1)
    load_cot.wait()
    exchange_wait(1)
    samples_start(0, 1)
    inverse_planes(arrive.at[1], inv_z, mid, stacked, norm_scale)
    for part in range(accum.shape[1] // 256):
        columns = slice(part * 256, part * 256 + 256)
        spectrum = dot32(table_y_t[...], stacked[:, columns])
        for start in range(0, accum.shape[0], 32):
            rows = slice(start, start + 32)
            pre_act = accum[rows, columns] + spectrum[rows]
            square = pre_act * pre_act
            half_gate = 0.5 + 0.5 * jnp.tanh(pre_act * (ROOT_CONST + ROOT_CONST * GELU_COEF * square))
            activated = pre_act * half_gate
            inner_slope = 2.0 * ROOT_CONST + 6.0 * ROOT_CONST * GELU_COEF * square
            gelu_slope = half_gate + activated * (1.0 - half_gate) * inner_slope
            out_block[rows, columns] = activated.astype(jnp.bfloat16)
            grad_block[rows, columns] = (cot[rows, columns].astype(jnp.float32) * gelu_slope).astype(
                jnp.bfloat16
            )
        spread_cells(dot32(table_y[...], grad_block[:, columns]), mid_next, 4 * part)
    forward_z(fwd_z, mid_next, send.at[2])
    exchange_start(2)
    store_out = pltpu.make_async_copy(out_block, field_out.at[0, 0], load_sem.at[2])
    store_out.start()

    pointwise_into(grad_block, point_wide_t)
    exchange_wait(2)
    forward_modes(2, coef_grad)
    samples_start(1, 0)
    lax.fori_loop(0, x_length // 2, mix_back, 0)
    inverse_modes(3)
    exchange_start(3)
    samples_start(1, 1)
    exchange_wait(3)
    inverse_planes(arrive.at[3], inv_z, mid, stacked, norm_scale)
    for part in range(accum.shape[1] // 256):
        columns = slice(part * 256, part * 256 + 256)
        tail_block[:, columns] = (
            accum[:, columns] + dot32(table_y_t[...], stacked[:, columns])
        ).astype(jnp.bfloat16)
    store_grad = pltpu.make_async_copy(tail_block, field_grad.at[0, 0], load_sem.at[3])
    store_grad.start()

    for turn in range(4):
        for hop in range(1, group_size):
            plane_copy(turn, hop).wait_send()
    for which in range(2):
        own_copy(which).wait()
        for half in range(2):
            for hop in range(1, sample_count):
                sample_copy(which, half, hop).wait()
    store_out.wait()
    store_grad.wait()


def weight_kernel(
    left_hbm, right_hbm, first_hbm, second_hbm, weight_out, first_out, second_out,
    left_ref, right_ref, first_ref, second_ref, blocks, load_sem, pass_sem, block_sem,
):
    loads = [
        pltpu.make_async_copy(left_hbm, left_ref, load_sem.at[0]),
        pltpu.make_async_copy(right_hbm, right_ref, load_sem.at[1]),
    ]
    fetches = [
        pltpu.make_async_copy(first_hbm, first_ref, load_sem.at[2]),
        pltpu.make_async_copy(second_hbm, second_ref, load_sem.at[3]),
    ]
    passes = [
        pltpu.make_async_copy(first_ref, first_out, pass_sem.at[0]),
        pltpu.make_async_copy(second_ref, second_out, pass_sem.at[1]),
    ]
    for copy in loads + fetches:
        copy.start()
    for copy in loads:
        copy.wait()
    sample_count, x_length, mode_block = left_ref.shape[:3]
    depth = 2 * sample_count * 16
    groups = mode_block // 16
    own_lane = lax.broadcasted_iota(jnp.int32, (64, depth), 1) % 16

    def block_copy(index):
        return pltpu.make_async_copy(blocks.at[index], weight_out.at[index], block_sem.at[index])

    def operands(residue, rows):
        left = jnp.concatenate([left_ref[s, residue, rows, :] for s in range(sample_count)], 0)
        right = jnp.concatenate([right_ref[s, residue, rows, :] for s in range(sample_count)], 0)
        flipped = left.astype(jnp.float32).T
        flipped = jnp.concatenate([flipped[:64], flipped[64:]], axis=1)
        wide = right.astype(jnp.float32)
        stack = jnp.concatenate([wide, turned(wide)], 0).astype(jnp.bfloat16)
        kept = jnp.concatenate(
            [jnp.where(own_lane == mode, flipped, 0.0).astype(jnp.bfloat16) for mode in range(16)], 0
        )
        return kept, stack

    def step(pair, carry):
        for group in range(groups):
            rows = slice(group * 16, group * 16 + 16)
            kept_a, stack_a = operands(2 * pair, rows)
            kept_b, stack_b = operands(2 * pair + 1, rows)
            empty = jnp.zeros_like(stack_a)
            stack = jnp.concatenate(
                [jnp.concatenate([stack_a, empty], 1), jnp.concatenate([empty, stack_b], 1)], 0
            )
            product = dot32(jnp.concatenate([kept_a, kept_b], 1), stack)
            for side in range(2):
                index = (2 * pair + side) * groups + group
                blocks[index] = product[:, side * 128 : side * 128 + 128]
                block_copy(index).start()
        return carry

    step(0, 0)
    for fetch, copy in zip(fetches, passes):
        fetch.wait()
        copy.start()
    lax.fori_loop(1, x_length // 2, step, 0)

    def finish(index, carry):
        block_copy(index).wait()
        return carry

    lax.fori_loop(0, x_length * groups, finish, 0)
    for copy in passes:
        copy.wait()


def fused_device(field_in, cotangent, mode_weights, point_weights):
    y_count, last_width = field_in.shape[2:]
    channels = point_weights.shape[0]
    z_count = last_width // channels
    kx_count, mode_block = mode_weights.shape[:2]
    group_size = lax.axis_size("gx")
    sample_count = lax.axis_size("sa")
    x_length = group_size
    pair_width = 2 * channels
    norm_scale = 1.0 / math.sqrt(x_length * y_count * z_count)
    cos_x, sin_x = x_tables(kx_count, x_length)
    tables = host_tables(y_count, z_count, channels)
    bf16, f32 = jnp.bfloat16, jnp.float32
    plane = (y_count, last_width)
    coef_shape = (x_length, mode_block, pair_width)
    anywhere = pl.BlockSpec(memory_space=pl.ANY)
    field_out, field_grad, shared_in, shared_grad = pl.pallas_call(
        functools.partial(
            fused_kernel, cos_x, sin_x, norm_scale, group_size, sample_count, kx_count // x_length
        ),
        out_shape=[
            jax.ShapeDtypeStruct((1, 1) + plane, bf16),
            jax.ShapeDtypeStruct((1, 1) + plane, bf16),
            jax.ShapeDtypeStruct((sample_count,) + coef_shape, bf16),
            jax.ShapeDtypeStruct((sample_count,) + coef_shape, bf16),
        ],
        in_specs=[anywhere] * 9,
        out_specs=[anywhere] * 4,
        scratch_shapes=[
            pltpu.VMEM((channels, channels), bf16),
            *[pltpu.VMEM(table.shape, bf16) for table in tables],
            pltpu.VMEM(plane, bf16),
            pltpu.VMEM(plane, bf16),
            pltpu.VMEM((kx_count, mode_block * channels, pair_width), bf16),
            pltpu.VMEM((x_length // 2, mode_block * channels, 2 * pair_width), bf16),
            pltpu.VMEM((4,) + coef_shape, bf16),
            pltpu.VMEM((4,) + coef_shape, bf16),
            pltpu.VMEM(coef_shape, bf16),
            pltpu.VMEM(coef_shape, bf16),
            pltpu.VMEM(coef_shape, f32),
            pltpu.VMEM((KY, z_count, pair_width), f32),
            pltpu.VMEM((KY, z_count, pair_width), f32),
            pltpu.VMEM((2 * KY, last_width), bf16),
            pltpu.VMEM(plane, f32),
            pltpu.VMEM(plane, bf16),
            pltpu.VMEM(plane, bf16),
            pltpu.VMEM(plane, bf16),
            pltpu.VMEM((256, 256), bf16),
            pltpu.VMEM((256, 256), bf16),
            pltpu.SemaphoreType.DMA((4,)),
            pltpu.SemaphoreType.DMA((6,)),
            pltpu.SemaphoreType.DMA((kx_count,)),
            pltpu.SemaphoreType.DMA((4, group_size)),
            pltpu.SemaphoreType.DMA((4, group_size)),
            pltpu.SemaphoreType.DMA((2, 2, sample_count)),
            pltpu.SemaphoreType.DMA((2, 2, sample_count)),
            pltpu.SemaphoreType.DMA((2,)),
        ],
        compiler_params=pltpu.CompilerParams(
            collective_id=0, has_side_effects=True, vmem_limit_bytes=56 * 1024 * 1024
        ),
        name="fourier_layer",
    )(
        field_in, cotangent,
        mode_weights.reshape(kx_count, mode_block * channels, pair_width),
        point_weights, *tables,
    )
    groups = mode_block // 16
    weight_grad, field_out, field_grad = pl.pallas_call(
        weight_kernel,
        out_shape=[
            jax.ShapeDtypeStruct((x_length * groups, 16 * channels, pair_width), f32),
            jax.ShapeDtypeStruct((1, 1) + plane, bf16),
            jax.ShapeDtypeStruct((1, 1) + plane, bf16),
        ],
        in_specs=[anywhere] * 4,
        out_specs=[anywhere] * 3,
        scratch_shapes=[
            pltpu.VMEM((sample_count,) + coef_shape, bf16),
            pltpu.VMEM((sample_count,) + coef_shape, bf16),
            pltpu.VMEM((1, 1) + plane, bf16),
            pltpu.VMEM((1, 1) + plane, bf16),
            pltpu.VMEM((x_length * groups, 16 * channels, pair_width), f32),
            pltpu.SemaphoreType.DMA((4,)),
            pltpu.SemaphoreType.DMA((2,)),
            pltpu.SemaphoreType.DMA((x_length * groups,)),
        ],
        compiler_params=pltpu.CompilerParams(vmem_limit_bytes=56 * 1024 * 1024),
        name="weight_gradient",
    )(shared_in, shared_grad, field_out, field_grad)
    return (
        field_out, field_grad,
        weight_grad.reshape(x_length, mode_block, channels, pair_width),
    )


def folds(field_in, mode_weights, point_weights):
    group_size, sample_count = lax.axis_size("gx"), lax.axis_size("sa")
    kx_count, mode_block, channels = mode_weights.shape[:3]
    planes, y_count, last_width = field_in.shape[1:]
    return (
        planes == 1
        and field_in.shape[0] == 1
        and channels == 64
        and last_width == 16 * channels
        and y_count % 16 == 0
        and group_size % 4 == 0
        and mode_block == 64
        and kx_count % group_size == 0
        and kx_count == sample_count * group_size
    )


def on_device(field_in, cotangent, mode_weights, point_weights):
    if folds(field_in, mode_weights, point_weights):
        return fused_device(field_in, cotangent, mode_weights, point_weights)
    local_field = field_in[0]
    planes, y_count, last_width = local_field.shape
    channels = point_weights.shape[0]
    z_count = last_width // channels
    kx_count = mode_weights.shape[0]
    x_length = planes * lax.axis_size("gx")
    norm_scale = 1.0 / math.sqrt(x_length * y_count * z_count)
    coeffs_in = forward_x(toward_modes(forward_yz(local_field, channels)), kx_count, norm_scale)
    mixed_modes = mix_forward(coeffs_in, mode_weights)
    spec_out = inverse_yz(
        toward_planes(inverse_x(mixed_modes, x_length)), y_count, z_count, norm_scale
    )
    pre_act = spec_out + pointwise(local_field, point_weights)
    activated, gelu_slope = gelu_parts(pre_act)
    out_grad = (cotangent[0].astype(jnp.float32) * gelu_slope).astype(jnp.bfloat16)
    coeffs_grad = forward_x(toward_modes(forward_yz(out_grad, channels)), kx_count, norm_scale)
    back_modes = mix_backward(coeffs_grad, mode_weights)
    spec_grad = inverse_yz(
        toward_planes(inverse_x(back_modes, x_length)), y_count, z_count, norm_scale
    )
    field_grad = (spec_grad + pointwise(out_grad, point_weights.T)).astype(jnp.bfloat16)
    shared_in, shared_grad = (
        lax.all_to_all(coeffs_in[None], "sa", split_axis=1, concat_axis=0, tiled=True),
        lax.all_to_all(coeffs_grad[None], "sa", split_axis=1, concat_axis=0, tiled=True),
    )
    weight_grad = sample_sum(shared_in, shared_grad)
    return (activated.astype(jnp.bfloat16)[None], field_grad[None], weight_grad)


def solution(mesh):
    in_specs = (
        P("sa", "gx", None, None),
        P("sa", "gx", None, None),
        P(None, "gx", None, None),
        P(),
    )
    out_specs = (P("sa", "gx", None, None), P("sa", "gx", None, None), P("sa", "gx", None, None))
    return jax.shard_map(
        on_device, mesh=mesh, in_specs=in_specs, out_specs=out_specs, check_vma=False
    )
```

```python
import functools
import math

import jax
import jax.numpy as jnp
import numpy as np
from jax import lax
from jax.experimental import pallas as pl
from jax.experimental.pallas import tpu as pltpu
from jax.sharding import PartitionSpec as P

KY = 32
KZ = 16


HIGHEST_PREC = lax.Precision.HIGHEST
GELU_COEF = 0.044715


def partner(block, axis, distance):
    count = lax.axis_size(axis)
    route = []
    for low in range(count):
        high = low | 1 << distance
        if high != low and high < count:
            route += [(low, high), (high, low)]
    return lax.ppermute(block, axis, route)


def angles(freq_count, grid_count):
    frequency = jnp.arange(freq_count, dtype=jnp.int32) - freq_count // 2
    places = jnp.arange(grid_count, dtype=jnp.int32)
    turn_index = jnp.mod(frequency[:, None] * places[None, :], grid_count)
    return turn_index.astype(jnp.float32) * (2.0 * math.pi / grid_count)


def gelu_parts(pre_act):
    root_const = math.sqrt(2.0 / math.pi)
    inner_arg = root_const * (pre_act + GELU_COEF * pre_act * pre_act * pre_act)
    tangent = jnp.tanh(inner_arg)
    activated = 0.5 * pre_act * (1.0 + tangent)
    gelu_slope = 0.5 * (1.0 + tangent) + 0.5 * pre_act * (1.0 - tangent * tangent) * root_const * (
        1.0 + 3.0 * GELU_COEF * pre_act * pre_act
    )
    return (activated, gelu_slope)


def along_z_forward(data_in, table_z):
    return jnp.einsum("pyzc,kz->pykc", data_in, table_z, precision=HIGHEST_PREC)


def along_z_inverse(data_in, table_z):
    return jnp.einsum("pykc,kz->pyzc", data_in, table_z, precision=HIGHEST_PREC)


def forward_yz(local_field, channels):
    planes, y_count, last_width = local_field.shape
    z_count = last_width // channels
    theta_y = angles(KY, y_count)
    table_y = jnp.concatenate([jnp.cos(theta_y), -jnp.sin(theta_y)], 0).astype(jnp.bfloat16)
    first_pass = jnp.einsum("fy,pyq->pfq", table_y, local_field, preferred_element_type=jnp.float32)
    first_pass = first_pass.reshape(planes, 2, KY, z_count, channels)
    theta_z = angles(KZ, z_count)
    cos_z = jnp.cos(theta_z)
    sin_z = jnp.sin(theta_z)
    real_in = first_pass[:, 0]
    imag_in = first_pass[:, 1]
    real_out = along_z_forward(real_in, cos_z) + along_z_forward(imag_in, sin_z)
    imag_out = along_z_forward(imag_in, cos_z) - along_z_forward(real_in, sin_z)
    mode_data = jnp.concatenate([real_out, imag_out], -1)
    return mode_data.reshape(planes, KY * KZ, 2 * channels).astype(jnp.bfloat16)


def forward_x(mode_data, kx_count, norm_scale):
    x_length, mode_block, pair_width = mode_data.shape
    channels = pair_width // 2
    theta_x = angles(kx_count, x_length)
    flat_data = mode_data.reshape(x_length, mode_block * pair_width)
    cos_part = jnp.dot(
        jnp.cos(theta_x).astype(jnp.bfloat16), flat_data, preferred_element_type=jnp.float32
    ).reshape(kx_count, mode_block, pair_width)
    sin_part = jnp.dot(
        jnp.sin(theta_x).astype(jnp.bfloat16), flat_data, preferred_element_type=jnp.float32
    ).reshape(kx_count, mode_block, pair_width)
    real_out = cos_part[..., :channels] + sin_part[..., channels:]
    imag_out = cos_part[..., channels:] - sin_part[..., :channels]
    return (jnp.concatenate([real_out, imag_out], -1) * norm_scale).astype(jnp.bfloat16)


def inverse_x(mixed_modes, x_length):
    kx_count, mode_block, pair_width = mixed_modes.shape
    channels = pair_width // 2
    theta_x = angles(kx_count, x_length).T
    flat_data = mixed_modes.reshape(kx_count, mode_block * pair_width)
    cos_part = jnp.dot(
        jnp.cos(theta_x).astype(jnp.bfloat16), flat_data, preferred_element_type=jnp.float32
    ).reshape(x_length, mode_block, pair_width)
    sin_part = jnp.dot(
        jnp.sin(theta_x).astype(jnp.bfloat16), flat_data, preferred_element_type=jnp.float32
    ).reshape(x_length, mode_block, pair_width)
    real_out = cos_part[..., :channels] - sin_part[..., channels:]
    imag_out = cos_part[..., channels:] + sin_part[..., :channels]
    return jnp.concatenate([real_out, imag_out], -1).astype(jnp.bfloat16)


def inverse_yz(planes_data, y_count, z_count, norm_scale):
    planes, mode_total, pair_width = planes_data.shape
    channels = pair_width // 2
    wide_data = planes_data.astype(jnp.float32).reshape(planes, KY, KZ, pair_width)
    real_in = wide_data[..., :channels]
    imag_in = wide_data[..., channels:]
    theta_z = angles(KZ, z_count)
    cos_z = jnp.cos(theta_z)
    sin_z = jnp.sin(theta_z)
    real_mid = along_z_inverse(real_in, cos_z) - along_z_inverse(imag_in, sin_z)
    imag_mid = along_z_inverse(imag_in, cos_z) + along_z_inverse(real_in, sin_z)
    stacked = jnp.concatenate([real_mid, imag_mid], 1).reshape(planes, 2 * KY, z_count * channels)
    theta_y = angles(KY, y_count)
    table_y = jnp.concatenate([jnp.cos(theta_y), -jnp.sin(theta_y)], 0)
    return jnp.einsum("pfq,fy->pyq", stacked, table_y, precision=HIGHEST_PREC) * norm_scale


def mix_forward(coeffs, weights_local):
    channels = weights_local.shape[2]
    real_part = jnp.einsum(
        "kmc,kmcp->kmp", coeffs[..., :channels], weights_local, preferred_element_type=jnp.float32
    )
    imag_part = jnp.einsum(
        "kmc,kmcp->kmp", coeffs[..., channels:], weights_local, preferred_element_type=jnp.float32
    )
    out_real = real_part[..., :channels] - imag_part[..., channels:]
    out_imag = real_part[..., channels:] + imag_part[..., :channels]
    return jnp.concatenate([out_real, out_imag], -1).astype(jnp.bfloat16)


def mix_backward(coeffs, weights_local):
    channels = weights_local.shape[2]
    swapped = jnp.concatenate([coeffs[..., channels:], -coeffs[..., :channels]], -1)
    first_half = jnp.einsum(
        "kmp,kmcp->kmc", coeffs, weights_local, preferred_element_type=jnp.float32
    )
    second_half = jnp.einsum(
        "kmp,kmcp->kmc", swapped, weights_local, preferred_element_type=jnp.float32
    )
    return jnp.concatenate([first_half, second_half], -1).astype(jnp.bfloat16)


def pointwise(local_field, weights_small):
    planes, y_count, last_width = local_field.shape
    channels = weights_small.shape[0]
    paired = jnp.kron(jnp.eye(2, dtype=weights_small.dtype), weights_small)
    cell_pairs = local_field.reshape(planes * y_count * last_width // (2 * channels), 2 * channels)
    return jnp.dot(cell_pairs, paired, preferred_element_type=jnp.float32).reshape(
        planes, y_count, last_width
    )


def sample_sum(left_side, right_side):
    channels = left_side.shape[-1] // 2
    left_real = left_side[..., :channels]
    left_imag = left_side[..., channels:]
    right_real = right_side[..., :channels]
    right_imag = right_side[..., channels:]

    def outer_sum(left_op, right_op):
        return jnp.einsum("skmc,skmo->kmco", left_op, right_op, preferred_element_type=jnp.float32)

    real_sum = outer_sum(left_real, right_real) + outer_sum(left_imag, right_imag)
    imag_sum = outer_sum(left_real, right_imag) - outer_sum(left_imag, right_real)
    return jnp.concatenate([real_sum, imag_sum], -1)


def partner_rounds(slot_buffer):
    slot_count = slot_buffer.shape[0]
    my_index = lax.axis_index("gx")
    for bit_pos in range(slot_count.bit_length() - 1):
        shaped = slot_buffer.reshape(
            (slot_count >> bit_pos + 1, 2, 1 << bit_pos) + slot_buffer.shape[1:]
        )
        lower_half = shaped[:, 0]
        upper_half = shaped[:, 1]
        own_bit = jnp.bitwise_and(jnp.right_shift(my_index, bit_pos), 1) == 1
        outgoing = jnp.where(own_bit, lower_half, upper_half)
        incoming = partner(outgoing, "gx", bit_pos)
        new_lower = jnp.where(own_bit, incoming, lower_half)
        new_upper = jnp.where(own_bit, upper_half, incoming)
        slot_buffer = jnp.stack([new_lower, new_upper], 1).reshape(slot_buffer.shape)
    return slot_buffer


def toward_modes(mode_data):
    planes, mode_total, pair_width = mode_data.shape
    group_size = lax.axis_size("gx")
    slot_buffer = mode_data.reshape(
        planes, group_size, mode_total // group_size, pair_width
    ).transpose(1, 0, 2, 3)
    return partner_rounds(slot_buffer).reshape(
        planes * group_size, mode_total // group_size, pair_width
    )


def toward_planes(back_planes):
    x_length, mode_block, pair_width = back_planes.shape
    group_size = lax.axis_size("gx")
    slot_buffer = back_planes.reshape(group_size, x_length // group_size, mode_block, pair_width)
    arrived = partner_rounds(slot_buffer)
    return arrived.transpose(1, 0, 2, 3).reshape(
        x_length // group_size, group_size * mode_block, pair_width
    )


MESH = pl.DeviceIdType.MESH
NT = (((1,), (1,)), ((), ()))
ROOT_CONST = math.sqrt(2.0 / math.pi)


def angles_host(freq_count, grid_count):
    frequency = np.arange(freq_count) - freq_count // 2
    turn_index = np.mod(frequency[:, None] * np.arange(grid_count)[None, :], grid_count)
    return turn_index.astype(np.float32) * np.float32(2.0 * math.pi / grid_count)


def host_tables(y_count, z_count, channels):
    theta_y = angles_host(KY, y_count)
    table_y = np.concatenate([np.cos(theta_y), -np.sin(theta_y)], 0)
    theta_z = angles_host(KZ, z_count)
    eye = np.eye(16, dtype=np.float32)
    fwd_z = np.concatenate([np.kron(eye, np.cos(theta_z)), np.kron(eye, np.sin(theta_z))], 0)
    inv_z = np.concatenate([np.kron(eye, np.cos(theta_z).T), np.kron(eye, np.sin(theta_z).T)], 0)
    spread = np.tile(np.eye(channels, dtype=np.float32), (256 // channels, 1))
    return [jnp.asarray(t, jnp.bfloat16) for t in (table_y, table_y.T, fwd_z, inv_z, spread)]


def x_tables(kx_count, x_length):
    theta_x = angles_host(kx_count, x_length)[:x_length]
    rounded = [np.asarray(f(theta_x), jnp.bfloat16).astype(np.float32) for f in (np.cos, np.sin)]
    return [np.where(np.abs(t) < 1e-5, 0.0, t) for t in rounded]


def dot32(left, right):
    return jnp.dot(left, right, preferred_element_type=jnp.float32)


def lanes_low(shape):
    return lax.broadcasted_iota(jnp.int32, shape, 1) < 64


def swap(block):
    return pltpu.roll(block, 64, 1)


def turned(block):
    swapped = swap(block)
    return jnp.where(lanes_low(block.shape), swapped, -swapped)


def x_pass(read, write, cos_t, sin_t, mode_block):
    length = cos_t.shape[0]
    half = length // 2

    def step(index, carry):
        rows = pl.ds(pl.multiple_of(index * 16, 16), 16)
        data = [read(j, rows) for j in range(length)]
        folded = [
            [data[j] + data[j + half] for j in range(half)],
            [data[j] - data[j + half] for j in range(half)],
        ]
        spun = [[turned(block) for block in group] for group in folded]
        for k in range(length):
            total = None
            for j in range(half):
                for coef, block in ((cos_t[k, j], folded[k % 2][j]), (sin_t[k, j], spun[k % 2][j])):
                    coef = float(coef)
                    if coef == 0.0:
                        continue
                    term = block if coef == 1.0 else -block if coef == -1.0 else block * coef
                    total = term if total is None else total + term
            write(k, rows, total)
        return carry

    lax.fori_loop(0, mode_block // 16, step, 0, unroll=2)


def spread_cells(first_pass, mid, first_cell):
    low = lanes_low((KY, 128))
    for pair in range(first_pass.shape[1] // 128):
        real_in = first_pass[:KY, pair * 128 : pair * 128 + 128]
        imag_in = first_pass[KY:, pair * 128 : pair * 128 + 128]
        mid[:, first_cell + 2 * pair, :] = jnp.where(low, real_in, swap(imag_in))
        mid[:, first_cell + 2 * pair + 1, :] = jnp.where(low, swap(real_in), imag_in)


def forward_z(fwd_z, mid, send):
    group_size, mode_block, pair_width = send.shape
    per_half = 256 // mode_block
    for half in range(2):
        block = mid[16 * half : 16 * half + 16].reshape(256, pair_width).astype(jnp.bfloat16)
        both = dot32(fwd_z[...], block)
        data = both[:256] + turned(both[256:])
        send[half * per_half : (half + 1) * per_half] = data.reshape(
            per_half, mode_block, pair_width
        ).astype(jnp.bfloat16)


def inverse_planes(arrived, inv_z, mid, stacked, norm_scale):
    group_size, mode_block, pair_width = arrived.shape
    per_half = 256 // mode_block
    for half in range(2):
        block = arrived[half * per_half : (half + 1) * per_half].reshape(256, pair_width)
        both = dot32(inv_z[...], block)
        mid[16 * half : 16 * half + 16] = (
            (both[:256] - turned(both[256:])) * norm_scale
        ).reshape(16, 16, pair_width)
    low = lanes_low((KY, 128))
    for pair in range(stacked.shape[1] // 128):
        even = mid[:, 2 * pair, :]
        odd = mid[:, 2 * pair + 1, :]
        columns = slice(pair * 128, pair * 128 + 128)
        stacked[:KY, columns] = jnp.where(low, even, swap(odd)).astype(jnp.bfloat16)
        stacked[KY:, columns] = jnp.where(low, swap(even), odd).astype(jnp.bfloat16)


def fused_kernel(
    cos_x, sin_x, norm_scale, group_size, sample_count, alias_count,
    field_hbm, cot_hbm, weights_hbm, point_hbm, y_hbm, y_t_hbm, fwd_hbm, inv_hbm, spread_hbm,
    field_out, field_grad, shared_in, shared_grad,
    point_ref, table_y, table_y_t, fwd_z, inv_z, spread,
    field, cot, weights, folded, send, arrive, gathered_coefs, mixed, mid, mid_next, stacked, accum,
    out_block, grad_block, tail_block, point_wide, point_wide_t,
    load_sem, table_sem, weight_sem, send_sem, recv_sem, sa_send, sa_recv, own_sem,
):
    me = lax.axis_index("gx")
    mine = lax.axis_index("sa")
    x_length = group_size
    mode_block = send.shape[2]
    groups = mode_block // 16

    load_field = pltpu.make_async_copy(field_hbm.at[0, 0], field, load_sem.at[0])
    load_cot = pltpu.make_async_copy(cot_hbm.at[0, 0], cot, load_sem.at[1])
    load_tables = [
        pltpu.make_async_copy(source, target, table_sem.at[index])
        for index, (source, target) in enumerate((
            (y_hbm, table_y), (fwd_hbm, fwd_z), (point_hbm, point_ref),
            (spread_hbm, spread), (inv_hbm, inv_z), (y_t_hbm, table_y_t),
        ))
    ]
    load_field.start()
    for load in load_tables:
        load.start()
    load_cot.start()

    def weight_copy(kx):
        return pltpu.make_async_copy(weights_hbm.at[kx], weights.at[kx], weight_sem.at[kx])

    for residue in range(x_length):
        for alias in range(alias_count):
            weight_copy(residue + x_length * alias).start()

    barrier = pltpu.get_barrier_semaphore()
    for hop in range(1, group_size):
        pl.semaphore_signal(
            barrier, inc=1, device_id={"gx": lax.rem(me + hop, group_size)}, device_id_type=MESH
        )
    for hop in range(1, sample_count):
        pl.semaphore_signal(
            barrier, inc=1, device_id={"sa": lax.rem(mine + hop, sample_count)}, device_id_type=MESH
        )

    def plane_copy(turn, hop):
        target = lax.rem(me + hop, group_size)
        return pltpu.make_async_remote_copy(
            src_ref=send.at[turn, target],
            dst_ref=arrive.at[turn, me],
            send_sem=send_sem.at[turn, hop],
            recv_sem=recv_sem.at[turn, hop],
            device_id={"gx": target},
            device_id_type=MESH,
        )

    def exchange_start(turn):
        for hop in range(1, group_size):
            plane_copy(turn, hop).start()
        arrive[turn, me] = send[turn, me]

    def exchange_wait(turn):
        for hop in range(1, group_size):
            plane_copy(turn, hop).wait_recv()

    coef_in = gathered_coefs.at[0, mine]
    coef_grad = gathered_coefs.at[1, mine]
    last = sample_count - 1

    def line_copy(which, way, step, slot):
        target = lax.rem(mine + (1, last)[way], sample_count)
        return pltpu.make_async_remote_copy(
            src_ref=gathered_coefs.at[which, slot],
            dst_ref=gathered_coefs.at[which, slot],
            send_sem=sa_send.at[which, way, step],
            recv_sem=sa_recv.at[which, way, step],
            device_id={"sa": target},
            device_id_type=MESH,
        )

    def line_step(which, step):
        @pl.when(mine >= step)
        def from_below():
            slot = lax.rem(mine + sample_count - step, sample_count)
            if step > 0:
                line_copy(which, 0, step - 1, slot).wait_recv()
            if step < last:
                @pl.when(mine < last)
                def onward():
                    line_copy(which, 0, step, slot).start()

        @pl.when(mine + step <= last)
        def from_above():
            slot = lax.rem(mine + step, sample_count)
            if step > 0:
                line_copy(which, 1, step - 1, slot).wait_recv()
            if step < last:
                @pl.when(mine > 0)
                def onward():
                    line_copy(which, 1, step, slot).start()

    def line_finish(which):
        for step in range(last):
            @pl.when((mine >= step) & (mine < last))
            def sent_up():
                line_copy(which, 0, step, lax.rem(mine + sample_count - step, sample_count)).wait_send()

            @pl.when((mine + step <= last) & (mine > 0))
            def sent_down():
                line_copy(which, 1, step, lax.rem(mine + step, sample_count)).wait_send()

    def share(which):
        return pltpu.make_async_copy(
            gathered_coefs.at[which], (shared_in, shared_grad)[which], own_sem.at[which]
        )

    def forward_modes(turn, coef):
        def read(j, rows):
            return arrive[turn, j, rows, :].astype(jnp.float32)

        def write(k, rows, value):
            coef[k, rows, :] = (value * norm_scale).astype(jnp.bfloat16)

        x_pass(read, write, cos_x, sin_x, mode_block)

    def inverse_modes(turn):
        def read(j, rows):
            return mixed[j, rows, :]

        def write(k, rows, value):
            send[turn, k, rows, :] = value.astype(jnp.bfloat16)

        x_pass(read, write, cos_x.T, -sin_x.T, mode_block)

    def wait_weights(residue):
        for alias in range(alias_count):
            weight_copy(residue + x_length * alias).wait()

    def fold_rows(pair, start):
        for part in range(1024 // 128):
            rows = pl.ds(pl.multiple_of(start + part * 128, 128), 128)
            for side in range(2):
                residue = 2 * pair + side
                terms = [
                    weights[residue + x_length * alias, rows, :] for alias in range(alias_count)
                ]
                while len(terms) > 1:
                    terms = [sum(terms[k + 1 : k + 2], terms[k]) for k in range(0, len(terms), 2)]
                folded[pair, rows, side * 128 : side * 128 + 128] = terms[0]

    row_index = lax.broadcasted_iota(jnp.int32, (8, 128), 0)
    low16 = lanes_low((16, 128))
    own_half = (row_index + lax.broadcasted_iota(jnp.int32, (8, 128), 1) // 64) % 2 == 0
    own_pair = [row_index // 2 == pair for pair in range(4)]

    def diagonal(block):
        empty = jnp.zeros((8, 128), jnp.float32)
        columns = []
        for part in range(8):
            half = block[:8] if part < 4 else block[8:]
            kept = jnp.where(own_pair[part % 4], jnp.where(own_half, half, 0.0), 0.0)
            stacked_rows = [kept, empty] if part < 4 else [empty, kept]
            columns.append(jnp.concatenate(stacked_rows, 0).astype(jnp.bfloat16))
        return jnp.concatenate(columns, 1)

    def gathered(block):
        halves = []
        for half in range(2):
            rows = slice(half * 8, half * 8 + 8)
            kept = block[rows, half * 512 : half * 512 + 128]
            for part in range(1, 4):
                start = half * 512 + part * 128
                kept = jnp.where(own_pair[part], block[rows, start : start + 128], kept)
            halves.append(jnp.where(own_half, kept, 0.0))
        total = jnp.concatenate(halves, 0)
        return total + swap(total)

    def mix_in_group(pair, group):
        rows = slice(group * 16, group * 16 + 16)
        parts = []
        for side in range(2):
            coef = coef_in[2 * pair + side, rows, :].astype(jnp.float32)
            other = swap(coef)
            parts += [diagonal(jnp.where(low16, coef, other)), diagonal(jnp.where(low16, other, coef))]
        product = dot32(
            jnp.concatenate(parts, 0), folded[pair, group * 1024 : group * 1024 + 1024, :]
        )
        for side in range(2):
            own = product[side * 32 : side * 32 + 32, side * 128 : side * 128 + 128]
            mixed[2 * pair + side, rows, :] = own[:16] - turned(own[16:])

    def wait_pair(pair):
        wait_weights(2 * pair)
        wait_weights(2 * pair + 1)

    def fold_first(pair):
        wait_pair(pair)

        def step(index, inner):
            fold_rows(pair, index * 1024)
            return inner

        lax.fori_loop(0, groups, step, 0)

    def mix_and_fold(pair, carry):
        wait_pair(pair)
        for group in range(groups):
            mix_in_group(pair - 1, group)
            fold_rows(pair, group * 1024)
        return carry

    def mix_back(pair, carry):
        empty = jnp.zeros((32, 128), jnp.bfloat16)
        for group in range(groups):
            rows = slice(group * 16, group * 16 + 16)
            parts = []
            for side in range(2):
                coef = coef_grad[2 * pair + side, rows, :].astype(jnp.float32)
                both = jnp.concatenate([coef, turned(coef)], 0).astype(jnp.bfloat16)
                parts.append(jnp.concatenate([both, empty] if side == 0 else [empty, both], 1))
            product = lax.dot_general(
                jnp.concatenate(parts, 0), folded[pair, group * 1024 : group * 1024 + 1024, :],
                NT, preferred_element_type=jnp.float32,
            )
            for side in range(2):
                start = side * 32
                mixed[2 * pair + side, rows, :] = jnp.where(
                    low16, gathered(product[start : start + 16]),
                    gathered(product[start + 16 : start + 32]),
                )
        return carry

    def pointwise_into(source, wide):
        for part in range(accum.shape[1] // 256):
            columns = slice(part * 256, part * 256 + 256)
            accum[:, columns] = dot32(source[:, columns], wide[...])

    load_field.wait()
    load_tables[0].wait()
    spread_cells(dot32(table_y[...], field[...]), mid, 0)
    load_tables[1].wait()
    forward_z(fwd_z, mid, send.at[0])
    pl.semaphore_wait(barrier, group_size + sample_count - 2)
    exchange_start(0)

    same_block = (
        lax.broadcasted_iota(jnp.int32, (256, 256), 0) // 64
        == lax.broadcasted_iota(jnp.int32, (256, 256), 1) // 64
    )

    def widened(block):
        wide = lax.dot_general(block.astype(jnp.bfloat16), spread[...], NT, preferred_element_type=jnp.float32)
        return jnp.where(same_block, wide, 0.0).astype(jnp.bfloat16)

    for load in load_tables[2:]:
        load.wait()
    point_wide[...] = widened(dot32(spread[...], point_ref[...]))
    point_wide_t[...] = widened(
        lax.dot_general(spread[...], point_ref[...], NT, preferred_element_type=jnp.float32)
    )
    pointwise_into(field, point_wide)

    fold_first(0)
    exchange_wait(0)
    forward_modes(0, coef_in)
    line_step(0, 0)
    lax.fori_loop(1, x_length // 2, mix_and_fold, 0)
    for group in range(groups):
        mix_in_group(x_length // 2 - 1, group)
    line_step(0, 1)
    inverse_modes(1)
    exchange_start(1)
    load_cot.wait()
    exchange_wait(1)
    inverse_planes(arrive.at[1], inv_z, mid, stacked, norm_scale)
    for part in range(accum.shape[1] // 256):
        columns = slice(part * 256, part * 256 + 256)
        spectrum = dot32(table_y_t[...], stacked[:, columns])
        for start in range(0, accum.shape[0], 32):
            rows = slice(start, start + 32)
            pre_act = accum[rows, columns] + spectrum[rows]
            square = pre_act * pre_act
            half_gate = 0.5 + 0.5 * jnp.tanh(pre_act * (ROOT_CONST + ROOT_CONST * GELU_COEF * square))
            activated = pre_act * half_gate
            inner_slope = 2.0 * ROOT_CONST + 6.0 * ROOT_CONST * GELU_COEF * square
            gelu_slope = half_gate + activated * (1.0 - half_gate) * inner_slope
            out_block[rows, columns] = activated.astype(jnp.bfloat16)
            grad_block[rows, columns] = (cot[rows, columns].astype(jnp.float32) * gelu_slope).astype(
                jnp.bfloat16
            )
        spread_cells(dot32(table_y[...], grad_block[:, columns]), mid_next, 4 * part)
    forward_z(fwd_z, mid_next, send.at[2])
    exchange_start(2)
    line_step(0, 2)
    store_out = pltpu.make_async_copy(out_block, field_out.at[0, 0], load_sem.at[2])
    store_out.start()

    pointwise_into(grad_block, point_wide_t)
    exchange_wait(2)
    forward_modes(2, coef_grad)
    line_step(1, 0)
    lax.fori_loop(0, x_length // 2, mix_back, 0)
    inverse_modes(3)
    exchange_start(3)
    line_step(1, 1)
    exchange_wait(3)
    line_step(1, 2)
    for step in range(3, sample_count):
        line_step(0, step)
    share(0).start()
    inverse_planes(arrive.at[3], inv_z, mid, stacked, norm_scale)
    for part in range(accum.shape[1] // 256):
        columns = slice(part * 256, part * 256 + 256)
        tail_block[:, columns] = (
            accum[:, columns] + dot32(table_y_t[...], stacked[:, columns])
        ).astype(jnp.bfloat16)
    store_grad = pltpu.make_async_copy(tail_block, field_grad.at[0, 0], load_sem.at[3])
    store_grad.start()

    for turn in range(4):
        for hop in range(1, group_size):
            plane_copy(turn, hop).wait_send()
    for step in range(3, sample_count):
        line_step(1, step)
    share(1).start()
    for which in range(2):
        line_finish(which)
        share(which).wait()
    store_out.wait()
    store_grad.wait()


def weight_kernel(
    left_hbm, right_hbm, first_hbm, second_hbm, weight_out, first_out, second_out,
    left_ref, right_ref, first_ref, second_ref, blocks, load_sem, pass_sem, block_sem,
):
    loads = [
        pltpu.make_async_copy(left_hbm, left_ref, load_sem.at[0]),
        pltpu.make_async_copy(right_hbm, right_ref, load_sem.at[1]),
    ]
    fetches = [
        pltpu.make_async_copy(first_hbm, first_ref, load_sem.at[2]),
        pltpu.make_async_copy(second_hbm, second_ref, load_sem.at[3]),
    ]
    passes = [
        pltpu.make_async_copy(first_ref, first_out, pass_sem.at[0]),
        pltpu.make_async_copy(second_ref, second_out, pass_sem.at[1]),
    ]
    for copy in loads + fetches:
        copy.start()
    for copy in loads:
        copy.wait()
    sample_count, x_length, mode_block = left_ref.shape[:3]
    depth = 2 * sample_count * 16
    groups = mode_block // 16
    own_lane = lax.broadcasted_iota(jnp.int32, (64, depth), 1) % 16

    def block_copy(index):
        return pltpu.make_async_copy(blocks.at[index], weight_out.at[index], block_sem.at[index])

    def operands(residue, rows):
        left = jnp.concatenate([left_ref[s, residue, rows, :] for s in range(sample_count)], 0)
        right = jnp.concatenate([right_ref[s, residue, rows, :] for s in range(sample_count)], 0)
        flipped = left.astype(jnp.float32).T
        flipped = jnp.concatenate([flipped[:64], flipped[64:]], axis=1)
        wide = right.astype(jnp.float32)
        stack = jnp.concatenate([wide, turned(wide)], 0).astype(jnp.bfloat16)
        kept = jnp.concatenate(
            [jnp.where(own_lane == mode, flipped, 0.0).astype(jnp.bfloat16) for mode in range(16)], 0
        )
        return kept, stack

    def step(pair, carry):
        for group in range(groups):
            rows = slice(group * 16, group * 16 + 16)
            kept_a, stack_a = operands(2 * pair, rows)
            kept_b, stack_b = operands(2 * pair + 1, rows)
            empty = jnp.zeros_like(stack_a)
            stack = jnp.concatenate(
                [jnp.concatenate([stack_a, empty], 1), jnp.concatenate([empty, stack_b], 1)], 0
            )
            product = dot32(jnp.concatenate([kept_a, kept_b], 1), stack)
            for side in range(2):
                index = (2 * pair + side) * groups + group
                blocks[index] = product[:, side * 128 : side * 128 + 128]
                block_copy(index).start()
        return carry

    step(0, 0)
    for fetch, copy in zip(fetches, passes):
        fetch.wait()
        copy.start()
    lax.fori_loop(1, x_length // 2, step, 0)

    def finish(index, carry):
        block_copy(index).wait()
        return carry

    lax.fori_loop(0, x_length * groups, finish, 0)
    for copy in passes:
        copy.wait()


def fused_device(field_in, cotangent, mode_weights, point_weights):
    y_count, last_width = field_in.shape[2:]
    channels = point_weights.shape[0]
    z_count = last_width // channels
    kx_count, mode_block = mode_weights.shape[:2]
    group_size = lax.axis_size("gx")
    sample_count = lax.axis_size("sa")
    x_length = group_size
    pair_width = 2 * channels
    norm_scale = 1.0 / math.sqrt(x_length * y_count * z_count)
    cos_x, sin_x = x_tables(kx_count, x_length)
    tables = host_tables(y_count, z_count, channels)
    bf16, f32 = jnp.bfloat16, jnp.float32
    plane = (y_count, last_width)
    coef_shape = (x_length, mode_block, pair_width)
    anywhere = pl.BlockSpec(memory_space=pl.ANY)
    field_out, field_grad, shared_in, shared_grad = pl.pallas_call(
        functools.partial(
            fused_kernel, cos_x, sin_x, norm_scale, group_size, sample_count, kx_count // x_length
        ),
        out_shape=[
            jax.ShapeDtypeStruct((1, 1) + plane, bf16),
            jax.ShapeDtypeStruct((1, 1) + plane, bf16),
            jax.ShapeDtypeStruct((sample_count,) + coef_shape, bf16),
            jax.ShapeDtypeStruct((sample_count,) + coef_shape, bf16),
        ],
        in_specs=[anywhere] * 9,
        out_specs=[anywhere] * 4,
        scratch_shapes=[
            pltpu.VMEM((channels, channels), bf16),
            *[pltpu.VMEM(table.shape, bf16) for table in tables],
            pltpu.VMEM(plane, bf16),
            pltpu.VMEM(plane, bf16),
            pltpu.VMEM((kx_count, mode_block * channels, pair_width), bf16),
            pltpu.VMEM((x_length // 2, mode_block * channels, 2 * pair_width), bf16),
            pltpu.VMEM((4,) + coef_shape, bf16),
            pltpu.VMEM((4,) + coef_shape, bf16),
            pltpu.VMEM((2, sample_count) + coef_shape, bf16),
            pltpu.VMEM(coef_shape, f32),
            pltpu.VMEM((KY, z_count, pair_width), f32),
            pltpu.VMEM((KY, z_count, pair_width), f32),
            pltpu.VMEM((2 * KY, last_width), bf16),
            pltpu.VMEM(plane, f32),
            pltpu.VMEM(plane, bf16),
            pltpu.VMEM(plane, bf16),
            pltpu.VMEM(plane, bf16),
            pltpu.VMEM((256, 256), bf16),
            pltpu.VMEM((256, 256), bf16),
            pltpu.SemaphoreType.DMA((4,)),
            pltpu.SemaphoreType.DMA((6,)),
            pltpu.SemaphoreType.DMA((kx_count,)),
            pltpu.SemaphoreType.DMA((4, group_size)),
            pltpu.SemaphoreType.DMA((4, group_size)),
            pltpu.SemaphoreType.DMA((2, 2, sample_count)),
            pltpu.SemaphoreType.DMA((2, 2, sample_count)),
            pltpu.SemaphoreType.DMA((2,)),
        ],
        compiler_params=pltpu.CompilerParams(
            collective_id=0, has_side_effects=True, vmem_limit_bytes=56 * 1024 * 1024
        ),
        name="fourier_layer",
    )(
        field_in, cotangent,
        mode_weights.reshape(kx_count, mode_block * channels, pair_width),
        point_weights, *tables,
    )
    groups = mode_block // 16
    weight_grad, field_out, field_grad = pl.pallas_call(
        weight_kernel,
        out_shape=[
            jax.ShapeDtypeStruct((x_length * groups, 16 * channels, pair_width), f32),
            jax.ShapeDtypeStruct((1, 1) + plane, bf16),
            jax.ShapeDtypeStruct((1, 1) + plane, bf16),
        ],
        in_specs=[anywhere] * 4,
        out_specs=[anywhere] * 3,
        scratch_shapes=[
            pltpu.VMEM((sample_count,) + coef_shape, bf16),
            pltpu.VMEM((sample_count,) + coef_shape, bf16),
            pltpu.VMEM((1, 1) + plane, bf16),
            pltpu.VMEM((1, 1) + plane, bf16),
            pltpu.VMEM((x_length * groups, 16 * channels, pair_width), f32),
            pltpu.SemaphoreType.DMA((4,)),
            pltpu.SemaphoreType.DMA((2,)),
            pltpu.SemaphoreType.DMA((x_length * groups,)),
        ],
        compiler_params=pltpu.CompilerParams(vmem_limit_bytes=56 * 1024 * 1024),
        name="weight_gradient",
    )(shared_in, shared_grad, field_out, field_grad)
    return (
        field_out, field_grad,
        weight_grad.reshape(x_length, mode_block, channels, pair_width),
    )


def folds(field_in, mode_weights, point_weights):
    group_size, sample_count = lax.axis_size("gx"), lax.axis_size("sa")
    kx_count, mode_block, channels = mode_weights.shape[:3]
    planes, y_count, last_width = field_in.shape[1:]
    return (
        planes == 1
        and field_in.shape[0] == 1
        and channels == 64
        and last_width == 16 * channels
        and y_count % 16 == 0
        and group_size % 4 == 0
        and mode_block == 64
        and kx_count % group_size == 0
        and kx_count == sample_count * group_size
    )


def on_device(field_in, cotangent, mode_weights, point_weights):
    if folds(field_in, mode_weights, point_weights):
        return fused_device(field_in, cotangent, mode_weights, point_weights)
    local_field = field_in[0]
    planes, y_count, last_width = local_field.shape
    channels = point_weights.shape[0]
    z_count = last_width // channels
    kx_count = mode_weights.shape[0]
    x_length = planes * lax.axis_size("gx")
    norm_scale = 1.0 / math.sqrt(x_length * y_count * z_count)
    coeffs_in = forward_x(toward_modes(forward_yz(local_field, channels)), kx_count, norm_scale)
    mixed_modes = mix_forward(coeffs_in, mode_weights)
    spec_out = inverse_yz(
        toward_planes(inverse_x(mixed_modes, x_length)), y_count, z_count, norm_scale
    )
    pre_act = spec_out + pointwise(local_field, point_weights)
    activated, gelu_slope = gelu_parts(pre_act)
    out_grad = (cotangent[0].astype(jnp.float32) * gelu_slope).astype(jnp.bfloat16)
    coeffs_grad = forward_x(toward_modes(forward_yz(out_grad, channels)), kx_count, norm_scale)
    back_modes = mix_backward(coeffs_grad, mode_weights)
    spec_grad = inverse_yz(
        toward_planes(inverse_x(back_modes, x_length)), y_count, z_count, norm_scale
    )
    field_grad = (spec_grad + pointwise(out_grad, point_weights.T)).astype(jnp.bfloat16)
    shared_in, shared_grad = (
        lax.all_to_all(coeffs_in[None], "sa", split_axis=1, concat_axis=0, tiled=True),
        lax.all_to_all(coeffs_grad[None], "sa", split_axis=1, concat_axis=0, tiled=True),
    )
    weight_grad = sample_sum(shared_in, shared_grad)
    return (activated.astype(jnp.bfloat16)[None], field_grad[None], weight_grad)


def solution(mesh):
    in_specs = (
        P("sa", "gx", None, None),
        P("sa", "gx", None, None),
        P(None, "gx", None, None),
        P(),
    )
    out_specs = (P("sa", "gx", None, None), P("sa", "gx", None, None), P("sa", "gx", None, None))
    return jax.shard_map(
        on_device, mesh=mesh, in_specs=in_specs, out_specs=out_specs, check_vma=False
    )
```

```python
import functools
import math

import jax
import jax.numpy as jnp
import numpy as np
from jax import lax
from jax.experimental import pallas as pl
from jax.experimental.pallas import tpu as pltpu
from jax.sharding import PartitionSpec as P

KY = 32
KZ = 16


HIGHEST_PREC = lax.Precision.HIGHEST
GELU_COEF = 0.044715


def partner(block, axis, distance):
    count = lax.axis_size(axis)
    route = []
    for low in range(count):
        high = low | 1 << distance
        if high != low and high < count:
            route += [(low, high), (high, low)]
    return lax.ppermute(block, axis, route)


def angles(freq_count, grid_count):
    frequency = jnp.arange(freq_count, dtype=jnp.int32) - freq_count // 2
    places = jnp.arange(grid_count, dtype=jnp.int32)
    turn_index = jnp.mod(frequency[:, None] * places[None, :], grid_count)
    return turn_index.astype(jnp.float32) * (2.0 * math.pi / grid_count)


def gelu_parts(pre_act):
    root_const = math.sqrt(2.0 / math.pi)
    inner_arg = root_const * (pre_act + GELU_COEF * pre_act * pre_act * pre_act)
    tangent = jnp.tanh(inner_arg)
    activated = 0.5 * pre_act * (1.0 + tangent)
    gelu_slope = 0.5 * (1.0 + tangent) + 0.5 * pre_act * (1.0 - tangent * tangent) * root_const * (
        1.0 + 3.0 * GELU_COEF * pre_act * pre_act
    )
    return (activated, gelu_slope)


def along_z_forward(data_in, table_z):
    return jnp.einsum("pyzc,kz->pykc", data_in, table_z, precision=HIGHEST_PREC)


def along_z_inverse(data_in, table_z):
    return jnp.einsum("pykc,kz->pyzc", data_in, table_z, precision=HIGHEST_PREC)


def forward_yz(local_field, channels):
    planes, y_count, last_width = local_field.shape
    z_count = last_width // channels
    theta_y = angles(KY, y_count)
    table_y = jnp.concatenate([jnp.cos(theta_y), -jnp.sin(theta_y)], 0).astype(jnp.bfloat16)
    first_pass = jnp.einsum("fy,pyq->pfq", table_y, local_field, preferred_element_type=jnp.float32)
    first_pass = first_pass.reshape(planes, 2, KY, z_count, channels)
    theta_z = angles(KZ, z_count)
    cos_z = jnp.cos(theta_z)
    sin_z = jnp.sin(theta_z)
    real_in = first_pass[:, 0]
    imag_in = first_pass[:, 1]
    real_out = along_z_forward(real_in, cos_z) + along_z_forward(imag_in, sin_z)
    imag_out = along_z_forward(imag_in, cos_z) - along_z_forward(real_in, sin_z)
    mode_data = jnp.concatenate([real_out, imag_out], -1)
    return mode_data.reshape(planes, KY * KZ, 2 * channels).astype(jnp.bfloat16)


def forward_x(mode_data, kx_count, norm_scale):
    x_length, mode_block, pair_width = mode_data.shape
    channels = pair_width // 2
    theta_x = angles(kx_count, x_length)
    flat_data = mode_data.reshape(x_length, mode_block * pair_width)
    cos_part = jnp.dot(
        jnp.cos(theta_x).astype(jnp.bfloat16), flat_data, preferred_element_type=jnp.float32
    ).reshape(kx_count, mode_block, pair_width)
    sin_part = jnp.dot(
        jnp.sin(theta_x).astype(jnp.bfloat16), flat_data, preferred_element_type=jnp.float32
    ).reshape(kx_count, mode_block, pair_width)
    real_out = cos_part[..., :channels] + sin_part[..., channels:]
    imag_out = cos_part[..., channels:] - sin_part[..., :channels]
    return (jnp.concatenate([real_out, imag_out], -1) * norm_scale).astype(jnp.bfloat16)


def inverse_x(mixed_modes, x_length):
    kx_count, mode_block, pair_width = mixed_modes.shape
    channels = pair_width // 2
    theta_x = angles(kx_count, x_length).T
    flat_data = mixed_modes.reshape(kx_count, mode_block * pair_width)
    cos_part = jnp.dot(
        jnp.cos(theta_x).astype(jnp.bfloat16), flat_data, preferred_element_type=jnp.float32
    ).reshape(x_length, mode_block, pair_width)
    sin_part = jnp.dot(
        jnp.sin(theta_x).astype(jnp.bfloat16), flat_data, preferred_element_type=jnp.float32
    ).reshape(x_length, mode_block, pair_width)
    real_out = cos_part[..., :channels] - sin_part[..., channels:]
    imag_out = cos_part[..., channels:] + sin_part[..., :channels]
    return jnp.concatenate([real_out, imag_out], -1).astype(jnp.bfloat16)


def inverse_yz(planes_data, y_count, z_count, norm_scale):
    planes, mode_total, pair_width = planes_data.shape
    channels = pair_width // 2
    wide_data = planes_data.astype(jnp.float32).reshape(planes, KY, KZ, pair_width)
    real_in = wide_data[..., :channels]
    imag_in = wide_data[..., channels:]
    theta_z = angles(KZ, z_count)
    cos_z = jnp.cos(theta_z)
    sin_z = jnp.sin(theta_z)
    real_mid = along_z_inverse(real_in, cos_z) - along_z_inverse(imag_in, sin_z)
    imag_mid = along_z_inverse(imag_in, cos_z) + along_z_inverse(real_in, sin_z)
    stacked = jnp.concatenate([real_mid, imag_mid], 1).reshape(planes, 2 * KY, z_count * channels)
    theta_y = angles(KY, y_count)
    table_y = jnp.concatenate([jnp.cos(theta_y), -jnp.sin(theta_y)], 0)
    return jnp.einsum("pfq,fy->pyq", stacked, table_y, precision=HIGHEST_PREC) * norm_scale


def mix_forward(coeffs, weights_local):
    channels = weights_local.shape[2]
    real_part = jnp.einsum(
        "kmc,kmcp->kmp", coeffs[..., :channels], weights_local, preferred_element_type=jnp.float32
    )
    imag_part = jnp.einsum(
        "kmc,kmcp->kmp", coeffs[..., channels:], weights_local, preferred_element_type=jnp.float32
    )
    out_real = real_part[..., :channels] - imag_part[..., channels:]
    out_imag = real_part[..., channels:] + imag_part[..., :channels]
    return jnp.concatenate([out_real, out_imag], -1).astype(jnp.bfloat16)


def mix_backward(coeffs, weights_local):
    channels = weights_local.shape[2]
    swapped = jnp.concatenate([coeffs[..., channels:], -coeffs[..., :channels]], -1)
    first_half = jnp.einsum(
        "kmp,kmcp->kmc", coeffs, weights_local, preferred_element_type=jnp.float32
    )
    second_half = jnp.einsum(
        "kmp,kmcp->kmc", swapped, weights_local, preferred_element_type=jnp.float32
    )
    return jnp.concatenate([first_half, second_half], -1).astype(jnp.bfloat16)


def pointwise(local_field, weights_small):
    planes, y_count, last_width = local_field.shape
    channels = weights_small.shape[0]
    paired = jnp.kron(jnp.eye(2, dtype=weights_small.dtype), weights_small)
    cell_pairs = local_field.reshape(planes * y_count * last_width // (2 * channels), 2 * channels)
    return jnp.dot(cell_pairs, paired, preferred_element_type=jnp.float32).reshape(
        planes, y_count, last_width
    )


def sample_sum(left_side, right_side):
    channels = left_side.shape[-1] // 2
    left_real = left_side[..., :channels]
    left_imag = left_side[..., channels:]
    right_real = right_side[..., :channels]
    right_imag = right_side[..., channels:]

    def outer_sum(left_op, right_op):
        return jnp.einsum("skmc,skmo->kmco", left_op, right_op, preferred_element_type=jnp.float32)

    real_sum = outer_sum(left_real, right_real) + outer_sum(left_imag, right_imag)
    imag_sum = outer_sum(left_real, right_imag) - outer_sum(left_imag, right_real)
    return jnp.concatenate([real_sum, imag_sum], -1)


def partner_rounds(slot_buffer):
    slot_count = slot_buffer.shape[0]
    my_index = lax.axis_index("gx")
    for bit_pos in range(slot_count.bit_length() - 1):
        shaped = slot_buffer.reshape(
            (slot_count >> bit_pos + 1, 2, 1 << bit_pos) + slot_buffer.shape[1:]
        )
        lower_half = shaped[:, 0]
        upper_half = shaped[:, 1]
        own_bit = jnp.bitwise_and(jnp.right_shift(my_index, bit_pos), 1) == 1
        outgoing = jnp.where(own_bit, lower_half, upper_half)
        incoming = partner(outgoing, "gx", bit_pos)
        new_lower = jnp.where(own_bit, incoming, lower_half)
        new_upper = jnp.where(own_bit, upper_half, incoming)
        slot_buffer = jnp.stack([new_lower, new_upper], 1).reshape(slot_buffer.shape)
    return slot_buffer


def toward_modes(mode_data):
    planes, mode_total, pair_width = mode_data.shape
    group_size = lax.axis_size("gx")
    slot_buffer = mode_data.reshape(
        planes, group_size, mode_total // group_size, pair_width
    ).transpose(1, 0, 2, 3)
    return partner_rounds(slot_buffer).reshape(
        planes * group_size, mode_total // group_size, pair_width
    )


def toward_planes(back_planes):
    x_length, mode_block, pair_width = back_planes.shape
    group_size = lax.axis_size("gx")
    slot_buffer = back_planes.reshape(group_size, x_length // group_size, mode_block, pair_width)
    arrived = partner_rounds(slot_buffer)
    return arrived.transpose(1, 0, 2, 3).reshape(
        x_length // group_size, group_size * mode_block, pair_width
    )


MESH = pl.DeviceIdType.MESH
NT = (((1,), (1,)), ((), ()))
ROOT_CONST = math.sqrt(2.0 / math.pi)


def angles_host(freq_count, grid_count):
    frequency = np.arange(freq_count) - freq_count // 2
    turn_index = np.mod(frequency[:, None] * np.arange(grid_count)[None, :], grid_count)
    return turn_index.astype(np.float32) * np.float32(2.0 * math.pi / grid_count)


def host_tables(y_count, z_count, channels):
    theta_y = angles_host(KY, y_count)
    table_y = np.concatenate([np.cos(theta_y), -np.sin(theta_y)], 0)
    theta_z = angles_host(KZ, z_count)
    eye = np.eye(16, dtype=np.float32)
    fwd_z = np.concatenate([np.kron(eye, np.cos(theta_z)), np.kron(eye, np.sin(theta_z))], 0)
    inv_z = np.concatenate([np.kron(eye, np.cos(theta_z).T), np.kron(eye, np.sin(theta_z).T)], 0)
    spread = np.tile(np.eye(channels, dtype=np.float32), (256 // channels, 1))
    return [jnp.asarray(t, jnp.bfloat16) for t in (table_y, table_y.T, fwd_z, inv_z, spread)]


def x_tables(kx_count, x_length):
    theta_x = angles_host(kx_count, x_length)[:x_length]
    rounded = [np.asarray(f(theta_x), jnp.bfloat16).astype(np.float32) for f in (np.cos, np.sin)]
    return [np.where(np.abs(t) < 1e-5, 0.0, t) for t in rounded]


def dot32(left, right):
    return jnp.dot(left, right, preferred_element_type=jnp.float32)


def lanes_low(shape):
    return lax.broadcasted_iota(jnp.int32, shape, 1) < 64


def swap(block):
    return pltpu.roll(block, 64, 1)


def turned(block):
    swapped = swap(block)
    return jnp.where(lanes_low(block.shape), swapped, -swapped)


def x_pass(read, write, cos_t, sin_t, mode_block):
    length = cos_t.shape[0]
    half = length // 2

    def step(index, carry):
        rows = pl.ds(pl.multiple_of(index * 16, 16), 16)
        data = [read(j, rows) for j in range(length)]
        folded = [
            [data[j] + data[j + half] for j in range(half)],
            [data[j] - data[j + half] for j in range(half)],
        ]
        spun = [[turned(block) for block in group] for group in folded]
        for k in range(length):
            total = None
            for j in range(half):
                for coef, block in ((cos_t[k, j], folded[k % 2][j]), (sin_t[k, j], spun[k % 2][j])):
                    coef = float(coef)
                    if coef == 0.0:
                        continue
                    term = block if coef == 1.0 else -block if coef == -1.0 else block * coef
                    total = term if total is None else total + term
            write(k, rows, total)
        return carry

    lax.fori_loop(0, mode_block // 16, step, 0, unroll=2)


def spread_cells(first_pass, mid, first_cell):
    low = lanes_low((KY, 128))
    for pair in range(first_pass.shape[1] // 128):
        real_in = first_pass[:KY, pair * 128 : pair * 128 + 128]
        imag_in = first_pass[KY:, pair * 128 : pair * 128 + 128]
        mid[:, first_cell + 2 * pair, :] = jnp.where(low, real_in, swap(imag_in))
        mid[:, first_cell + 2 * pair + 1, :] = jnp.where(low, swap(real_in), imag_in)


def forward_z(fwd_z, mid, send):
    group_size, mode_block, pair_width = send.shape
    per_half = 256 // mode_block
    for half in range(2):
        block = mid[16 * half : 16 * half + 16].reshape(256, pair_width).astype(jnp.bfloat16)
        both = dot32(fwd_z[...], block)
        data = both[:256] + turned(both[256:])
        send[half * per_half : (half + 1) * per_half] = data.reshape(
            per_half, mode_block, pair_width
        ).astype(jnp.bfloat16)


def inverse_planes(arrived, inv_z, mid, stacked, norm_scale):
    group_size, mode_block, pair_width = arrived.shape
    per_half = 256 // mode_block
    for half in range(2):
        block = arrived[half * per_half : (half + 1) * per_half].reshape(256, pair_width)
        both = dot32(inv_z[...], block)
        mid[16 * half : 16 * half + 16] = (
            (both[:256] - turned(both[256:])) * norm_scale
        ).reshape(16, 16, pair_width)
    low = lanes_low((KY, 128))
    for pair in range(stacked.shape[1] // 128):
        even = mid[:, 2 * pair, :]
        odd = mid[:, 2 * pair + 1, :]
        columns = slice(pair * 128, pair * 128 + 128)
        stacked[:KY, columns] = jnp.where(low, even, swap(odd)).astype(jnp.bfloat16)
        stacked[KY:, columns] = jnp.where(low, swap(even), odd).astype(jnp.bfloat16)


def fused_kernel(
    cos_x, sin_x, norm_scale, group_size, sample_count, alias_count,
    field_hbm, cot_hbm, weights_hbm, point_hbm, y_hbm, y_t_hbm, fwd_hbm, inv_hbm, spread_hbm,
    field_out, field_grad, shared_in, shared_grad,
    point_ref, table_y, table_y_t, fwd_z, inv_z, spread,
    field, cot, weights, folded, folded_t, send, arrive, coef_in, coef_grad, mixed, mid, mid_next, stacked, accum,
    out_block, grad_block, tail_block, point_wide, point_wide_t,
    load_sem, table_sem, weight_sem, send_sem, recv_sem, sa_send, sa_recv, own_sem,
):
    me = lax.axis_index("gx")
    mine = lax.axis_index("sa")
    x_length = group_size
    mode_block = send.shape[2]
    groups = mode_block // 16

    load_field = pltpu.make_async_copy(field_hbm.at[0, 0], field, load_sem.at[0])
    load_cot = pltpu.make_async_copy(cot_hbm.at[0, 0], cot, load_sem.at[1])
    load_tables = [
        pltpu.make_async_copy(source, target, table_sem.at[index])
        for index, (source, target) in enumerate((
            (y_hbm, table_y), (fwd_hbm, fwd_z), (point_hbm, point_ref),
            (spread_hbm, spread), (inv_hbm, inv_z), (y_t_hbm, table_y_t),
        ))
    ]
    load_field.start()
    for load in load_tables:
        load.start()
    load_cot.start()

    def weight_copy(kx):
        return pltpu.make_async_copy(weights_hbm.at[kx], weights.at[kx], weight_sem.at[kx])

    for residue in range(x_length):
        for alias in range(alias_count):
            weight_copy(residue + x_length * alias).start()

    barrier = pltpu.get_barrier_semaphore()
    for hop in range(1, group_size):
        pl.semaphore_signal(
            barrier, inc=1, device_id={"gx": lax.rem(me + hop, group_size)}, device_id_type=MESH
        )
    for hop in range(1, sample_count):
        pl.semaphore_signal(
            barrier, inc=1, device_id={"sa": lax.rem(mine + hop, sample_count)}, device_id_type=MESH
        )

    def plane_copy(turn, hop):
        target = lax.rem(me + hop, group_size)
        return pltpu.make_async_remote_copy(
            src_ref=send.at[turn, target],
            dst_ref=arrive.at[turn, me],
            send_sem=send_sem.at[turn, hop],
            recv_sem=recv_sem.at[turn, hop],
            device_id={"gx": target},
            device_id_type=MESH,
        )

    def exchange_start(turn):
        for hop in range(1, group_size):
            plane_copy(turn, hop).start()
        arrive[turn, me] = send[turn, me]

    def exchange_wait(turn):
        for hop in range(1, group_size):
            plane_copy(turn, hop).wait_recv()

    def sample_copy(which, half, hop):
        source, target = ((coef_in, shared_in), (coef_grad, shared_grad))[which]
        span = pl.ds(half * (x_length // 2), x_length // 2)
        return pltpu.make_async_remote_copy(
            src_ref=source.at[span],
            dst_ref=target.at[mine, span],
            send_sem=sa_send.at[which, half, hop],
            recv_sem=sa_recv.at[which, half, hop],
            device_id={"sa": lax.rem(mine + hop, sample_count)},
            device_id_type=MESH,
        )

    def own_copy(which):
        source, target = ((coef_in, shared_in), (coef_grad, shared_grad))[which]
        return pltpu.make_async_copy(source, target.at[mine], own_sem.at[which])

    def samples_start(which, half):
        for hop in range(1, sample_count):
            sample_copy(which, half, hop).start()
        if half == 0:
            own_copy(which).start()

    def forward_modes(turn, coef):
        def read(j, rows):
            return arrive[turn, j, rows, :].astype(jnp.float32)

        def write(k, rows, value):
            coef[k, rows, :] = (value * norm_scale).astype(jnp.bfloat16)

        x_pass(read, write, cos_x, sin_x, mode_block)

    def inverse_modes(turn):
        def read(j, rows):
            return mixed[j, rows, :]

        def write(k, rows, value):
            send[turn, k, rows, :] = value.astype(jnp.bfloat16)

        x_pass(read, write, cos_x.T, -sin_x.T, mode_block)

    def wait_weights(residue):
        for alias in range(alias_count):
            weight_copy(residue + x_length * alias).wait()

    def fold_rows(pair, start):
        for part in range(1024 // 128):
            rows = slice(start + part * 128, start + part * 128 + 128)
            for side in range(2):
                residue = 2 * pair + side
                terms = [
                    weights[residue + x_length * alias, rows, :] for alias in range(alias_count)
                ]
                while len(terms) > 1:
                    terms = [sum(terms[k + 1 : k + 2], terms[k]) for k in range(0, len(terms), 2)]
                columns = slice(side * 128, side * 128 + 128)
                folded[pair, rows, columns] = terms[0]
                folded_t[pair, columns, rows] = terms[0].T

    row_index = lax.broadcasted_iota(jnp.int32, (8, 128), 0)
    low16 = lanes_low((16, 128))
    own_half = (row_index + lax.broadcasted_iota(jnp.int32, (8, 128), 1) // 64) % 2 == 0
    own_pair = [row_index // 2 == pair for pair in range(4)]

    def diagonal(block):
        empty = jnp.zeros((8, 128), jnp.float32)
        columns = []
        for part in range(8):
            half = block[:8] if part < 4 else block[8:]
            kept = jnp.where(own_pair[part % 4], jnp.where(own_half, half, 0.0), 0.0)
            stacked_rows = [kept, empty] if part < 4 else [empty, kept]
            columns.append(jnp.concatenate(stacked_rows, 0).astype(jnp.bfloat16))
        return jnp.concatenate(columns, 1)

    def gathered(block):
        halves = []
        for half in range(2):
            rows = slice(half * 8, half * 8 + 8)
            kept = block[rows, half * 512 : half * 512 + 128]
            for part in range(1, 4):
                start = half * 512 + part * 128
                kept = jnp.where(own_pair[part], block[rows, start : start + 128], kept)
            halves.append(jnp.where(own_half, kept, 0.0))
        total = jnp.concatenate(halves, 0)
        return total + swap(total)

    def mix_in_group(pair, group):
        rows = slice(group * 16, group * 16 + 16)
        parts = []
        for side in range(2):
            coef = coef_in[2 * pair + side, rows, :].astype(jnp.float32)
            other = swap(coef)
            parts += [diagonal(jnp.where(low16, coef, other)), diagonal(jnp.where(low16, other, coef))]
        product = dot32(
            jnp.concatenate(parts, 0), folded[pair, group * 1024 : group * 1024 + 1024, :]
        )
        for side in range(2):
            own = product[side * 32 : side * 32 + 32, side * 128 : side * 128 + 128]
            mixed[2 * pair + side, rows, :] = own[:16] - turned(own[16:])

    def wait_pair(pair):
        wait_weights(2 * pair)
        wait_weights(2 * pair + 1)

    def fold_first(pair):
        wait_pair(pair)

        for group in range(groups):
            fold_rows(pair, group * 1024)

    def mix_and_fold(pair, carry):
        wait_pair(pair)
        for group in range(groups):
            mix_in_group(pair - 1, group)
            fold_rows(pair, group * 1024)
        return carry

    def mix_back(pair, carry):
        empty = jnp.zeros((32, 128), jnp.bfloat16)
        for group in range(groups):
            rows = slice(group * 16, group * 16 + 16)
            parts = []
            for side in range(2):
                coef = coef_grad[2 * pair + side, rows, :].astype(jnp.float32)
                both = jnp.concatenate([coef, turned(coef)], 0).astype(jnp.bfloat16)
                parts.append(jnp.concatenate([both, empty] if side == 0 else [empty, both], 1))
            product = dot32(
                jnp.concatenate(parts, 0), folded_t[pair, :, group * 1024 : group * 1024 + 1024]
            )
            for side in range(2):
                start = side * 32
                mixed[2 * pair + side, rows, :] = jnp.where(
                    low16, gathered(product[start : start + 16]),
                    gathered(product[start + 16 : start + 32]),
                )
        return carry

    def pointwise_into(source, wide):
        for part in range(accum.shape[1] // 256):
            columns = slice(part * 256, part * 256 + 256)
            accum[:, columns] = dot32(source[:, columns], wide[...])

    load_field.wait()
    load_tables[0].wait()
    spread_cells(dot32(table_y[...], field[...]), mid, 0)
    load_tables[1].wait()
    forward_z(fwd_z, mid, send.at[0])
    pl.semaphore_wait(barrier, group_size + sample_count - 2)
    exchange_start(0)

    same_block = (
        lax.broadcasted_iota(jnp.int32, (256, 256), 0) // 64
        == lax.broadcasted_iota(jnp.int32, (256, 256), 1) // 64
    )

    def widened(block):
        wide = lax.dot_general(block.astype(jnp.bfloat16), spread[...], NT, preferred_element_type=jnp.float32)
        return jnp.where(same_block, wide, 0.0).astype(jnp.bfloat16)

    for load in load_tables[2:]:
        load.wait()
    point_wide[...] = widened(dot32(spread[...], point_ref[...]))
    point_wide_t[...] = widened(
        lax.dot_general(spread[...], point_ref[...], NT, preferred_element_type=jnp.float32)
    )
    pointwise_into(field, point_wide)

    fold_first(0)
    exchange_wait(0)
    forward_modes(0, coef_in)
    samples_start(0, 0)
    lax.fori_loop(1, x_length // 2, mix_and_fold, 0)
    for group in range(groups):
        mix_in_group(x_length // 2 - 1, group)
    inverse_modes(1)
    exchange_start(1)
    load_cot.wait()
    exchange_wait(1)
    samples_start(0, 1)
    inverse_planes(arrive.at[1], inv_z, mid, stacked, norm_scale)
    for part in range(accum.shape[1] // 256):
        columns = slice(part * 256, part * 256 + 256)
        spectrum = dot32(table_y_t[...], stacked[:, columns])
        for start in range(0, accum.shape[0], 32):
            rows = slice(start, start + 32)
            pre_act = accum[rows, columns] + spectrum[rows]
            square = pre_act * pre_act
            half_gate = 0.5 + 0.5 * jnp.tanh(pre_act * (ROOT_CONST + ROOT_CONST * GELU_COEF * square))
            activated = pre_act * half_gate
            inner_slope = 2.0 * ROOT_CONST + 6.0 * ROOT_CONST * GELU_COEF * square
            gelu_slope = half_gate + activated * (1.0 - half_gate) * inner_slope
            out_block[rows, columns] = activated.astype(jnp.bfloat16)
            grad_block[rows, columns] = (cot[rows, columns].astype(jnp.float32) * gelu_slope).astype(
                jnp.bfloat16
            )
        spread_cells(dot32(table_y[...], grad_block[:, columns]), mid_next, 4 * part)
    forward_z(fwd_z, mid_next, send.at[2])
    exchange_start(2)
    store_out = pltpu.make_async_copy(out_block, field_out.at[0, 0], load_sem.at[2])
    store_out.start()

    pointwise_into(grad_block, point_wide_t)
    exchange_wait(2)
    forward_modes(2, coef_grad)
    samples_start(1, 0)
    lax.fori_loop(0, x_length // 2, mix_back, 0)
    inverse_modes(3)
    exchange_start(3)
    samples_start(1, 1)
    exchange_wait(3)
    inverse_planes(arrive.at[3], inv_z, mid, stacked, norm_scale)
    for part in range(accum.shape[1] // 256):
        columns = slice(part * 256, part * 256 + 256)
        tail_block[:, columns] = (
            accum[:, columns] + dot32(table_y_t[...], stacked[:, columns])
        ).astype(jnp.bfloat16)
    store_grad = pltpu.make_async_copy(tail_block, field_grad.at[0, 0], load_sem.at[3])
    store_grad.start()

    for turn in range(4):
        for hop in range(1, group_size):
            plane_copy(turn, hop).wait_send()
    for which in range(2):
        own_copy(which).wait()
        for half in range(2):
            for hop in range(1, sample_count):
                sample_copy(which, half, hop).wait()
    store_out.wait()
    store_grad.wait()


def weight_kernel(
    left_hbm, right_hbm, first_hbm, second_hbm, weight_out, first_out, second_out,
    left_ref, right_ref, first_ref, second_ref, masks, blocks, load_sem, pass_sem, block_sem,
):
    loads = [
        pltpu.make_async_copy(left_hbm, left_ref, load_sem.at[0]),
        pltpu.make_async_copy(right_hbm, right_ref, load_sem.at[1]),
    ]
    fetches = [
        pltpu.make_async_copy(first_hbm, first_ref, load_sem.at[2]),
        pltpu.make_async_copy(second_hbm, second_ref, load_sem.at[3]),
    ]
    passes = [
        pltpu.make_async_copy(first_ref, first_out, pass_sem.at[0]),
        pltpu.make_async_copy(second_ref, second_out, pass_sem.at[1]),
    ]
    for copy in loads + fetches:
        copy.start()
    for copy in loads:
        copy.wait()
    sample_count, x_length, mode_block = left_ref.shape[:3]
    depth = 2 * sample_count * 16
    groups = mode_block // 16
    own_lane = lax.broadcasted_iota(jnp.int32, (64, depth), 1) % 16
    for mode in range(16):
        masks[mode] = jnp.where(own_lane == mode, 1.0, 0.0).astype(jnp.bfloat16)

    def block_copy(index):
        return pltpu.make_async_copy(blocks.at[index], weight_out.at[index], block_sem.at[index])

    def operands(residue, rows):
        left = jnp.concatenate([left_ref[s, residue, rows, :] for s in range(sample_count)], 0)
        right = jnp.concatenate([right_ref[s, residue, rows, :] for s in range(sample_count)], 0)
        flipped = left.astype(jnp.float32).T
        flipped = jnp.concatenate([flipped[:64], flipped[64:]], axis=1).astype(jnp.bfloat16)
        wide = right.astype(jnp.float32)
        stack = jnp.concatenate([wide, turned(wide)], 0).astype(jnp.bfloat16)
        kept = jnp.concatenate(
            [flipped * masks[mode] for mode in range(16)], 0
        )
        return kept, stack

    def step(pair, carry):
        for group in range(groups):
            rows = slice(group * 16, group * 16 + 16)
            kept_a, stack_a = operands(2 * pair, rows)
            kept_b, stack_b = operands(2 * pair + 1, rows)
            empty = jnp.zeros_like(stack_a)
            stack = jnp.concatenate(
                [jnp.concatenate([stack_a, empty], 1), jnp.concatenate([empty, stack_b], 1)], 0
            )
            product = dot32(jnp.concatenate([kept_a, kept_b], 1), stack)
            for side in range(2):
                index = (2 * pair + side) * groups + group
                blocks[index] = product[:, side * 128 : side * 128 + 128]
                block_copy(index).start()
        return carry

    step(0, 0)
    for fetch, copy in zip(fetches, passes):
        fetch.wait()
        copy.start()
    lax.fori_loop(1, x_length // 2, step, 0)

    def finish(index, carry):
        block_copy(index).wait()
        return carry

    lax.fori_loop(0, x_length * groups, finish, 0)
    for copy in passes:
        copy.wait()


def fused_device(field_in, cotangent, mode_weights, point_weights):
    y_count, last_width = field_in.shape[2:]
    channels = point_weights.shape[0]
    z_count = last_width // channels
    kx_count, mode_block = mode_weights.shape[:2]
    group_size = lax.axis_size("gx")
    sample_count = lax.axis_size("sa")
    x_length = group_size
    pair_width = 2 * channels
    norm_scale = 1.0 / math.sqrt(x_length * y_count * z_count)
    cos_x, sin_x = x_tables(kx_count, x_length)
    tables = host_tables(y_count, z_count, channels)
    bf16, f32 = jnp.bfloat16, jnp.float32
    plane = (y_count, last_width)
    coef_shape = (x_length, mode_block, pair_width)
    anywhere = pl.BlockSpec(memory_space=pl.ANY)
    field_out, field_grad, shared_in, shared_grad = pl.pallas_call(
        functools.partial(
            fused_kernel, cos_x, sin_x, norm_scale, group_size, sample_count, kx_count // x_length
        ),
        out_shape=[
            jax.ShapeDtypeStruct((1, 1) + plane, bf16),
            jax.ShapeDtypeStruct((1, 1) + plane, bf16),
            jax.ShapeDtypeStruct((sample_count,) + coef_shape, bf16),
            jax.ShapeDtypeStruct((sample_count,) + coef_shape, bf16),
        ],
        in_specs=[anywhere] * 9,
        out_specs=[anywhere] * 4,
        scratch_shapes=[
            pltpu.VMEM((channels, channels), bf16),
            *[pltpu.VMEM(table.shape, bf16) for table in tables],
            pltpu.VMEM(plane, bf16),
            pltpu.VMEM(plane, bf16),
            pltpu.VMEM((kx_count, mode_block * channels, pair_width), bf16),
            pltpu.VMEM((x_length // 2, mode_block * channels, 2 * pair_width), bf16),
            pltpu.VMEM((x_length // 2, 2 * pair_width, mode_block * channels), bf16),
            pltpu.VMEM((4,) + coef_shape, bf16),
            pltpu.VMEM((4,) + coef_shape, bf16),
            pltpu.VMEM(coef_shape, bf16),
            pltpu.VMEM(coef_shape, bf16),
            pltpu.VMEM(coef_shape, f32),
            pltpu.VMEM((KY, z_count, pair_width), f32),
            pltpu.VMEM((KY, z_count, pair_width), f32),
            pltpu.VMEM((2 * KY, last_width), bf16),
            pltpu.VMEM(plane, f32),
            pltpu.VMEM(plane, bf16),
            pltpu.VMEM(plane, bf16),
            pltpu.VMEM(plane, bf16),
            pltpu.VMEM((256, 256), bf16),
            pltpu.VMEM((256, 256), bf16),
            pltpu.SemaphoreType.DMA((4,)),
            pltpu.SemaphoreType.DMA((6,)),
            pltpu.SemaphoreType.DMA((kx_count,)),
            pltpu.SemaphoreType.DMA((4, group_size)),
            pltpu.SemaphoreType.DMA((4, group_size)),
            pltpu.SemaphoreType.DMA((2, 2, sample_count)),
            pltpu.SemaphoreType.DMA((2, 2, sample_count)),
            pltpu.SemaphoreType.DMA((2,)),
        ],
        compiler_params=pltpu.CompilerParams(
            collective_id=0, has_side_effects=True, vmem_limit_bytes=60 * 1024 * 1024
        ),
        name="fourier_layer",
    )(
        field_in, cotangent,
        mode_weights.reshape(kx_count, mode_block * channels, pair_width),
        point_weights, *tables,
    )
    groups = mode_block // 16
    weight_grad, field_out, field_grad = pl.pallas_call(
        weight_kernel,
        out_shape=[
            jax.ShapeDtypeStruct((x_length * groups, 16 * channels, pair_width), f32),
            jax.ShapeDtypeStruct((1, 1) + plane, bf16),
            jax.ShapeDtypeStruct((1, 1) + plane, bf16),
        ],
        in_specs=[anywhere] * 4,
        out_specs=[anywhere] * 3,
        scratch_shapes=[
            pltpu.VMEM((sample_count,) + coef_shape, bf16),
            pltpu.VMEM((sample_count,) + coef_shape, bf16),
            pltpu.VMEM((1, 1) + plane, bf16),
            pltpu.VMEM((1, 1) + plane, bf16),
            pltpu.VMEM((16, channels, 2 * sample_count * 16), bf16),
            pltpu.VMEM((x_length * groups, 16 * channels, pair_width), f32),
            pltpu.SemaphoreType.DMA((4,)),
            pltpu.SemaphoreType.DMA((2,)),
            pltpu.SemaphoreType.DMA((x_length * groups,)),
        ],
        compiler_params=pltpu.CompilerParams(vmem_limit_bytes=56 * 1024 * 1024),
        name="weight_gradient",
    )(shared_in, shared_grad, field_out, field_grad)
    return (
        field_out, field_grad,
        weight_grad.reshape(x_length, mode_block, channels, pair_width),
    )


def folds(field_in, mode_weights, point_weights):
    group_size, sample_count = lax.axis_size("gx"), lax.axis_size("sa")
    kx_count, mode_block, channels = mode_weights.shape[:3]
    planes, y_count, last_width = field_in.shape[1:]
    return (
        planes == 1
        and field_in.shape[0] == 1
        and channels == 64
        and last_width == 16 * channels
        and y_count % 16 == 0
        and group_size % 4 == 0
        and mode_block == 64
        and kx_count % group_size == 0
        and kx_count == sample_count * group_size
    )


def on_device(field_in, cotangent, mode_weights, point_weights):
    if folds(field_in, mode_weights, point_weights):
        return fused_device(field_in, cotangent, mode_weights, point_weights)
    local_field = field_in[0]
    planes, y_count, last_width = local_field.shape
    channels = point_weights.shape[0]
    z_count = last_width // channels
    kx_count = mode_weights.shape[0]
    x_length = planes * lax.axis_size("gx")
    norm_scale = 1.0 / math.sqrt(x_length * y_count * z_count)
    coeffs_in = forward_x(toward_modes(forward_yz(local_field, channels)), kx_count, norm_scale)
    mixed_modes = mix_forward(coeffs_in, mode_weights)
    spec_out = inverse_yz(
        toward_planes(inverse_x(mixed_modes, x_length)), y_count, z_count, norm_scale
    )
    pre_act = spec_out + pointwise(local_field, point_weights)
    activated, gelu_slope = gelu_parts(pre_act)
    out_grad = (cotangent[0].astype(jnp.float32) * gelu_slope).astype(jnp.bfloat16)
    coeffs_grad = forward_x(toward_modes(forward_yz(out_grad, channels)), kx_count, norm_scale)
    back_modes = mix_backward(coeffs_grad, mode_weights)
    spec_grad = inverse_yz(
        toward_planes(inverse_x(back_modes, x_length)), y_count, z_count, norm_scale
    )
    field_grad = (spec_grad + pointwise(out_grad, point_weights.T)).astype(jnp.bfloat16)
    shared_in, shared_grad = (
        lax.all_to_all(coeffs_in[None], "sa", split_axis=1, concat_axis=0, tiled=True),
        lax.all_to_all(coeffs_grad[None], "sa", split_axis=1, concat_axis=0, tiled=True),
    )
    weight_grad = sample_sum(shared_in, shared_grad)
    return (activated.astype(jnp.bfloat16)[None], field_grad[None], weight_grad)


def solution(mesh):
    in_specs = (
        P("sa", "gx", None, None),
        P("sa", "gx", None, None),
        P(None, "gx", None, None),
        P(),
    )
    out_specs = (P("sa", "gx", None, None), P("sa", "gx", None, None), P("sa", "gx", None, None))
    return jax.shard_map(
        on_device, mesh=mesh, in_specs=in_specs, out_specs=out_specs, check_vma=False
    )
```
